32 devices in a mesh: grp: 2 (over x), blk: 16 (over z, y, core).
Axes of the slice: x: 2, y: 2, z: 4, core: 2. Of those that a mesh axis runs over, the one named last changes fastest.
Arguments:
- integrals: bfloat16 [32, 16, 3, 4096], P(('grp', 'blk')), parts along dimension 0, may hold values from -6 to 6
- occupied: bfloat16 [32, 3, 4096], P(('grp', 'blk')), parts along dimension 0, may hold values from -0.5 to 0.5
- virtual: bfloat16 [32, 3, 4096], P(('grp', 'blk')), parts along dimension 0, may hold values from -0.5 to 0.5
- integral_block_mask: int32 [16, 3], replicated, may hold values 0 or 1
- occupied_block_mask: int32 [16, 3], replicated, may hold values 0 or 1
- virtual_block_mask: int32 [16, 3], replicated, may hold values 0 or 1
- block_orbital_count: int32 [16], replicated, may hold values from 32 to 64
Outputs:
- polarizability: float32 [32, 16], P(('grp', 'blk')), parts along dimension 0
The draws below stay inside these ranges and needn't reach their ends.
There are 2 independent parts, one for each index of `grp`. The reference program is written for one: setup_inputs(seed, part) draws one part's arguments, and reference() takes and returns one part's arrays. A program takes and returns all parts, laid end to end along the dimension named above; an argument that names none is the same for every part. Nothing has to cross between parts.
All inputs are finite; a program needn't handle non-finite values.
Results may differ from the reference program's by a relative error of at most 0.0037.
Values may be sent and summed in bfloat16 or wider, within the bound.
No kernel may reach another device: no remote copies, remote signals or barrier semaphores. Data moves between devices by JAX's collectives and lax.ppermute only.
A program may use at most 64 MiB of HBM per device.

```python
import math
import jax
import jax.numpy as jnp
from jax import lax

PADDED_ORBITALS = 64
NBLK = 16
SLAB = 16


def with_ends(entries, rng, least, high):
    shape = entries.shape
    place = [jax.random.randint(jax.random.fold_in(rng, axis), (), 0, shape[axis]) for axis in range(len(shape))]
    entries = entries.at[tuple(place)].set(least)
    longest = shape.index(max(shape))
    place[longest] = (place[longest] + 1) % shape[longest]
    return entries.at[tuple(place)].set(high)


def level_of(own_key, shape, shards, low, high):
    def one(axis_at, parts):
        steps = jax.random.uniform(jax.random.fold_in(jax.random.fold_in(own_key, 6), axis_at), (parts,), jnp.float32, low / len(shards), high / len(shards))
        return jnp.repeat(jnp.exp(steps), shape[axis_at] // parts).reshape((-1,) + (1,) * (len(shape) - axis_at - 1))

    level = one(*shards[0])
    for cut in shards[1:]:
        level = level * one(*cut)
    return level


def centred(own_key, extent, deviation, bound, shards=(), kind=jnp.bfloat16):
    values = jax.random.normal(own_key, extent, jnp.float32) * deviation
    if len(shards) > 0:
        values = level_of(own_key, extent, shards, -0.22, 0.18) * values
    return jnp.clip(values, min=-bound, max=bound).astype(kind)


def setup_inputs(seed: int = 0, part: int = 0) -> dict:
    seeds = jax.random.split(jax.random.key(seed), 8)
    part_keys = jax.random.split(jax.random.fold_in(seeds[7], part), 8)
    integrals = centred(part_keys[0], (SLAB, NBLK, 3, PADDED_ORBITALS * PADDED_ORBITALS), 1.0, 6.0, ((0, 16),))
    occupied = centred(part_keys[1], (NBLK, 3, PADDED_ORBITALS * PADDED_ORBITALS), (2 * PADDED_ORBITALS) ** -0.5, 0.5, ((0, 16),))
    virtual = centred(part_keys[2], (NBLK, 3, PADDED_ORBITALS * PADDED_ORBITALS), (2 * PADDED_ORBITALS) ** -0.5, 0.5, ((0, 16),))
    integral_block_mask = with_ends((jax.random.randint(seeds[3], (NBLK, 3), 0, 4) < 3).astype(jnp.int32), jax.random.fold_in(seeds[3], 1), 0, 1)
    occupied_block_mask = with_ends((jax.random.randint(seeds[4], (NBLK, 3), 0, 4) < 3).astype(jnp.int32), jax.random.fold_in(seeds[4], 1), 0, 1)
    virtual_block_mask = with_ends((jax.random.randint(seeds[5], (NBLK, 3), 0, 4) < 3).astype(jnp.int32), jax.random.fold_in(seeds[5], 1), 0, 1)
    block_orbital_count = with_ends(jax.random.randint(seeds[6], (NBLK,), PADDED_ORBITALS // 2, PADDED_ORBITALS + 1), jax.random.fold_in(seeds[6], 1), PADDED_ORBITALS // 2, PADDED_ORBITALS).astype(jnp.int32)
    return {"integrals": integrals, "occupied": occupied, "virtual": virtual, "integral_block_mask": integral_block_mask, "occupied_block_mask": occupied_block_mask, "virtual_block_mask": virtual_block_mask, "block_orbital_count": block_orbital_count}


def cyclic_boundary(array, margin, axis_pos):
    length = array.shape[axis_pos]
    front = lax.slice_in_dim(array, length - margin, length, axis=axis_pos)
    back = lax.slice_in_dim(array, 0, margin, axis=axis_pos)
    return jnp.concatenate([front, array, back], axis_pos)

def pairwise_terms(screening_input, occupied_input, virtual_input, integral_mask_input, occupied_mask_input, virtual_mask_input, block_count_input, target_blocks, window_border):
    aux_rows = screening_input.shape[0]
    window_extent = target_blocks + 2
    lane_index = jnp.arange(window_border, dtype=jnp.int32)
    usable = (lane_index[None, :] < block_count_input[:, None]).astype(jnp.float32)
    row_part = usable[1:window_extent + 1]
    col_part = jnp.stack([usable[shift_val:shift_val + window_extent] for shift_val in range(3)], 1)
    factor = integral_mask_input.astype(jnp.float32)[:, :, None, None] * row_part[:, None, :, None] * col_part[:, :, None, :]
    screened = screening_input.astype(jnp.float32).reshape(aux_rows, window_extent, 3, window_border, window_border) * factor[None]
    occ_blocks = occupied_input.astype(jnp.float32).reshape(window_extent, 3, window_border, window_border) * occupied_mask_input.astype(jnp.float32)[:, :, None, None]
    virtual_block_list = virtual_input.astype(jnp.float32).reshape(window_extent, 3, window_border, window_border) * virtual_mask_input.astype(jnp.float32)[:, :, None, None]
    forward_list = []
    backward_list = []
    for offset in range(5):
        forward_window = jnp.zeros((aux_rows, target_blocks, window_border, window_border), jnp.float32)
        backward_window = jnp.zeros((aux_rows, target_blocks, window_border, window_border), jnp.float32)
        for source in range(3):
            first_idx = 2 - source
            second_idx = first_idx + offset - 2
            if 0 <= second_idx <= 2:
                forward_window = forward_window + jnp.einsum('stml,tmn->stln', screened[:, source:source + target_blocks, first_idx], occ_blocks[source:source + target_blocks, second_idx])
                backward_window = backward_window + jnp.einsum('tml,stmn->stln', virtual_block_list[source:source + target_blocks, first_idx], screened[:, source:source + target_blocks, second_idx])
        forward_list.append(forward_window.reshape(aux_rows, target_blocks, window_border * window_border))
        backward_list.append(backward_window.reshape(aux_rows, target_blocks, window_border * window_border))
    return (jnp.stack(forward_list, 2).astype(jnp.bfloat16), jnp.stack(backward_list, 2).astype(jnp.bfloat16))

def reference(integrals, occupied, virtual, integral_block_mask, occupied_block_mask, virtual_block_mask, block_orbital_count):
    integrals_padded = cyclic_boundary(integrals, 1, 1)
    occupied_padded = cyclic_boundary(occupied, 1, 0)
    virtual_padded = cyclic_boundary(virtual, 1, 0)
    integral_mask_padded = cyclic_boundary(integral_block_mask, 1, 0)
    occupied_mask_padded = cyclic_boundary(occupied_block_mask, 1, 0)
    virtual_mask_padded = cyclic_boundary(virtual_block_mask, 1, 0)
    block_count_padded = cyclic_boundary(block_orbital_count, 2, 0)

    def step(carry, block_position):
        forward_window, backward_window = pairwise_terms(lax.dynamic_slice_in_dim(integrals_padded, block_position, 3, 1), lax.dynamic_slice_in_dim(occupied_padded, block_position, 3, 0), lax.dynamic_slice_in_dim(virtual_padded, block_position, 3, 0), lax.dynamic_slice_in_dim(integral_mask_padded, block_position, 3, 0), lax.dynamic_slice_in_dim(occupied_mask_padded, block_position, 3, 0), lax.dynamic_slice_in_dim(virtual_mask_padded, block_position, 3, 0), lax.dynamic_slice_in_dim(block_count_padded, block_position, 5, 0), 1, PADDED_ORBITALS)
        forward_window, backward_window = lax.optimization_barrier((forward_window, backward_window))
        flat_fwd = forward_window.astype(jnp.float32).reshape(SLAB, -1)
        flat_bwd = backward_window.astype(jnp.float32).reshape(SLAB, -1)
        return (carry + jnp.einsum('sk,qk->sq', flat_fwd, flat_bwd), None)
    chi_sum, _ = lax.scan(step, jnp.zeros((SLAB, SLAB), jnp.float32), jnp.arange(NBLK, dtype=jnp.int32))
    return chi_sum * jnp.float32(1.0 / math.sqrt(5 * PADDED_ORBITALS * PADDED_ORBITALS * NBLK))
```

```python
import functools
import math

import jax
import jax.numpy as jnp
from jax import lax
from jax.experimental import pallas as pl
from jax.experimental.pallas import tpu as pltpu
from jax.sharding import PartitionSpec as P

EDGE = 64
HALF = 32
LANES = 128
VMEM = pl.BlockSpec(memory_space=pltpu.VMEM)
SMEM = pl.BlockSpec(memory_space=pltpu.SMEM)


def block_order(count):
    if count == 16:
        chips = [0, 2, 4, 6, 7, 5, 3, 1]
        return [2 * chip + core for chip in chips for core in (0, 1)]
    return list(range(count))


def block_of(device, count):
    order = block_order(count)
    if order == list(range(count)):
        return device
    block = jnp.int32(0)
    for j, d in enumerate(order):
        block = jnp.where(device == d, j, block)
    return block


def pack_kernel(works_on, x_ref, out_ref, rows_ref):
    blocks = x_ref.shape[1]
    for a in range(3):
        for c in range(HALF):
            rows_ref[a, pl.ds(c, blocks, stride=HALF), :] = x_ref[
                a, :, c * LANES : (c + 1) * LANES
            ].astype(jnp.float32)
        for d, b in enumerate(works_on):
            out_ref[d, pl.ds(a * HALF, HALF), :] = rows_ref[a, pl.ds(b * HALF, HALF), :].astype(
                jnp.bfloat16
            )


def prep_kernel(
    total, members, imask, omask, vmask, count, gprev, gown, gnext, vir_ref, occ_ref
):
    own = block_of(lax.axis_index("blk"), members)
    greens = (gprev, gown, gnext)
    lane = lax.broadcasted_iota(jnp.int32, (HALF, LANES), 1)
    row = lax.broadcasted_iota(jnp.int32, (HALF, LANES), 0)
    left = lane < EDGE
    col = jnp.where(left, lane, lane - EDGE)
    block = [lax.rem(own + (total + k - 2), total) for k in range(5)]
    held = [count[b] for b in block]
    cols = [(col < held[k]).astype(jnp.float32) for k in range(5)]
    rows = [[(2 * row + par < held[s + 1]).astype(jnp.float32) for par in range(2)] for s in range(3)]
    vir = []
    for s in range(3):
        v = greens[s][pl.ds((5 - s) * HALF, HALF), :].astype(jnp.float32) * cols[2]
        vir.append((v * rows[s][0], pltpu.roll(v, EDGE, 1) * rows[s][1]))
    for t in range(5):
        parts = []
        for par in range(2):
            for s in range(3):
                if 0 <= t - s <= 2:
                    m = block[s + 1]
                    factor = (vmask[2 - s, m] * imask[t - s, m]).astype(jnp.float32)
                    parts.append(vir[s][par] * factor)
        while len(parts) < 8:
            parts.append(jnp.zeros((HALF, LANES), jnp.float32))
        vir_ref[t] = jnp.concatenate(parts, 0).T[:EDGE].astype(jnp.bfloat16)
    for s in range(3):
        m = block[s + 1]
        for t in range(5):
            to = pl.ds(t * LANES, LANES)
            if 0 <= t - s <= 2:
                factor = (omask[t - s, m] * imask[2 - s, m]).astype(jnp.float32)
                o = greens[s][pl.ds((t - s) * HALF, HALF), :].astype(jnp.float32) * (cols[t] * factor)
                turned = pltpu.roll(o, EDGE, 1)
            for half in range(2):
                for par in range(2):
                    at = pl.ds((half * 6 + s * 2 + par) * HALF, HALF)
                    if 0 <= t - s <= 2:
                        value = (o if half == par else turned) * rows[s][par]
                        kept = jnp.where(left == (half == 0), value, 0.0).astype(jnp.bfloat16)
                    else:
                        kept = jnp.zeros((HALF, LANES), jnp.bfloat16)
                    occ_ref[at, to] = kept


def main_kernel(scale, vir_ref, occ_ref, sprev, sown, snext, out_ref, half_ref, full_ref):
    rows = sown.shape[0]
    slabs = (sprev, sown, snext)
    left = lax.broadcasted_iota(jnp.int32, (HALF, LANES), 1) < EDGE
    for j in range(rows // 2):
        sides = []
        for s in range(3):
            one, two = slabs[s][2 * j], slabs[s][2 * j + 1]
            sides.append(
                (
                    jnp.concatenate([one[:, :EDGE], two[:, :EDGE]], 1),
                    jnp.concatenate([one[:, EDGE:], two[:, EDGE:]], 1),
                )
            )
        for t in range(5):
            parts = [
                sides[s][par][(t - s) * HALF : (t - s + 1) * HALF]
                for par in range(2)
                for s in range(3)
                if 0 <= t - s <= 2
            ]
            both = jnp.dot(
                vir_ref[t][:, : HALF * len(parts)],
                jnp.concatenate(parts, 0),
                preferred_element_type=jnp.float32,
            )
            half_ref[pl.ds(j * EDGE, EDGE), pl.ds(t * LANES, LANES)] = both.astype(jnp.bfloat16)
    for j in range(0, rows // 2, 4):
        full = lax.dot_general(
            occ_ref[...],
            half_ref[pl.ds(j * EDGE, 4 * EDGE), :],
            (((1,), (1,)), ((), ())),
            preferred_element_type=jnp.float32,
        )
        for half in range(2):
            for s in range(3):
                at = (half * 6 + s * 2) * HALF
                for pair in range(2):
                    to = slice(pair * LANES, (pair + 1) * LANES)
                    even = full[at : at + HALF, to]
                    odd = full[at + HALF : at + 2 * HALF, to]
                    first = 2 * (j + 2 * pair) + half
                    place = pl.ds(s * HALF, HALF)
                    full_ref[first, place, :] = jnp.where(
                        left, even, pltpu.roll(odd, EDGE, 1)
                    ).astype(jnp.bfloat16)
                    full_ref[first + 2, place, :] = jnp.where(
                        left, pltpu.roll(even, EDGE, 1), odd
                    ).astype(jnp.bfloat16)
    group = 16
    span = group * 16
    ri = lax.broadcasted_iota(jnp.int32, (span, span), 0)
    ci = lax.broadcasted_iota(jnp.int32, (span, span), 1)
    same = lax.rem(ri, 16) == lax.rem(ci, 16)
    pick = (
        lax.broadcasted_iota(jnp.int32, (span, group), 0) // 16
        == lax.broadcasted_iota(jnp.int32, (span, group), 1)
    ).astype(jnp.float32)
    for p in range(0, rows, group):
        for q in range(0, rows, group):
            acc = None
            for s in range(3):
                for c in range(2):
                    lhs = slabs[s][pl.ds(p, group), pl.ds((2 - s) * HALF + c * 16, 16), :]
                    rhs = full_ref[pl.ds(q, group), pl.ds(s * HALF + c * 16, 16), :]
                    one = lax.dot_general(
                        lhs.reshape(span, LANES),
                        rhs.reshape(span, LANES),
                        (((1,), (1,)), ((), ())),
                        preferred_element_type=jnp.float32,
                    )
                    acc = one if acc is None else acc + one
            kept = jnp.where(same, acc, 0.0).reshape(group, 16, span)
            summed = jnp.sum(kept, axis=1)
            out_ref[pl.ds(p, group), pl.ds(q, group)] = scale * jnp.dot(
                summed, pick, preferred_element_type=jnp.float32, precision=lax.Precision.HIGHEST
            )


def body(integrals, occupied, virtual, imask, omask, vmask, count):
    total = integrals.shape[1]
    members = lax.axis_size("blk")
    order = block_order(members)
    works_on = [order.index(d) for d in range(members)]

    greens = jnp.concatenate([occupied[0], virtual[0]], 0).reshape(6 * HALF, LANES)

    def from_block(shift):
        return [(b, order[(b - shift) % members]) for b in range(members)]

    greens = tuple(lax.ppermute(greens, "blk", from_block(k)) for k in (-1, 0, 1))
    rows = pl.pallas_call(
        functools.partial(pack_kernel, works_on),
        out_shape=jax.ShapeDtypeStruct((members, 3 * HALF, LANES), jnp.bfloat16),
        in_specs=[VMEM],
        out_specs=VMEM,
        scratch_shapes=[pltpu.VMEM((3, total * HALF, LANES), jnp.float32)],
        compiler_params=pltpu.CompilerParams(vmem_limit_bytes=32 * 1024 * 1024),
        name="pack",
    )(jnp.transpose(integrals[0], (1, 0, 2)))
    rows, *greens = lax.optimization_barrier((rows, *greens))
    own = lax.all_to_all(rows, "blk", split_axis=0, concat_axis=0, tiled=True)
    own, *greens = lax.optimization_barrier((own, *greens))
    vir, occ = pl.pallas_call(
        functools.partial(prep_kernel, total, members),
        out_shape=(
            jax.ShapeDtypeStruct((5, EDGE, 2 * LANES), jnp.bfloat16),
            jax.ShapeDtypeStruct((12 * HALF, 5 * LANES), jnp.bfloat16),
        ),
        in_specs=[SMEM] * 4 + [VMEM] * 3,
        out_specs=(VMEM, VMEM),
        name="prep",
    )(imask.T, omask.T, vmask.T, count, *greens)

    forth = [(order[j], order[(j + 1) % members]) for j in range(members)]
    back = [(order[(j + 1) % members], order[j]) for j in range(members)]
    sprev = lax.ppermute(own, "blk", forth)
    snext = lax.ppermute(own, "blk", back)
    part = pl.pallas_call(
        functools.partial(main_kernel, 1.0 / math.sqrt(5 * EDGE * EDGE * total)),
        out_shape=jax.ShapeDtypeStruct((members, members), jnp.float32),
        in_specs=[VMEM] * 5,
        out_specs=VMEM,
        scratch_shapes=[
            pltpu.VMEM((members // 2 * EDGE, 5 * LANES), jnp.bfloat16),
            pltpu.VMEM((members, 3 * HALF, LANES), jnp.bfloat16),
        ],
        compiler_params=pltpu.CompilerParams(vmem_limit_bytes=48 * 1024 * 1024),
        name="products",
    )(vir, occ, sprev, own, snext)
    mine = lax.all_to_all(part, "blk", split_axis=0, concat_axis=0, tiled=True)
    return jnp.sum(mine, axis=0, keepdims=True)


def solution(mesh):
    return jax.shard_map(
        body,
        mesh=mesh,
        in_specs=(
            P(("grp", "blk"), None, None, None),
            P(("grp", "blk"), None, None),
            P(("grp", "blk"), None, None),
            P(),
            P(),
            P(),
            P(),
        ),
        out_specs=P(("grp", "blk"), None),
        check_vma=False,
    )
```

```python
import functools
import math

import jax
import jax.numpy as jnp
from jax import lax
from jax.experimental import pallas as pl
from jax.experimental.pallas import tpu as pltpu
from jax.sharding import PartitionSpec as P

EDGE = 64
HALF = 32
LANES = 128
VMEM = pl.BlockSpec(memory_space=pltpu.VMEM)
SMEM = pl.BlockSpec(memory_space=pltpu.SMEM)


def block_order(count):
    if count == 16:
        chips = [0, 2, 4, 6, 7, 5, 3, 1]
        return [2 * chip + core for chip in chips for core in (0, 1)]
    return list(range(count))


def block_of(device, count):
    order = block_order(count)
    if order == list(range(count)):
        return device
    block = jnp.int32(0)
    for j, d in enumerate(order):
        block = jnp.where(device == d, j, block)
    return block


def pack_kernel(works_on, x_ref, occ_ref, vir_ref, out_ref, greens_ref, rows_ref):
    blocks = x_ref.shape[1]
    for k, ref in enumerate((occ_ref, vir_ref)):
        for c in range(HALF):
            rows_ref[3, pl.ds(3 * HALF * k + c, 3, stride=HALF), :] = ref[
                :, c * LANES : (c + 1) * LANES
            ].astype(jnp.float32)
    greens_ref[...] = rows_ref[3, pl.ds(0, 6 * HALF), :].astype(jnp.bfloat16)
    for a in range(3):
        for c in range(HALF):
            rows_ref[a, pl.ds(c, blocks, stride=HALF), :] = x_ref[
                a, :, c * LANES : (c + 1) * LANES
            ].astype(jnp.float32)
        for d, b in enumerate(works_on):
            out_ref[d, pl.ds(a * HALF, HALF), :] = rows_ref[a, pl.ds(b * HALF, HALF), :].astype(
                jnp.bfloat16
            )


def main_kernel(scale, total, rows, table, sprev, sown, snext, out_ref, vir_ref, occ_ref, half_ref, full_ref):
    slabs = (sprev, sown, snext)
    block_rows = 3 * HALF
    greens = rows * block_rows
    left = lax.broadcasted_iota(jnp.int32, (HALF, LANES), 1) < EDGE

    own = block_of(lax.axis_index("blk"), rows)
    lane = lax.broadcasted_iota(jnp.int32, (HALF, LANES), 1)
    row = lax.broadcasted_iota(jnp.int32, (HALF, LANES), 0)
    col = jnp.where(left, lane, lane - EDGE)
    block = [lax.rem(own + (total + k - 2), total) for k in range(5)]
    held = [table[9, b] for b in block]
    cols = [(col < held[k]).astype(jnp.float32) for k in range(5)]
    keep = [[(2 * row + par < held[s + 1]).astype(jnp.float32) for par in range(2)] for s in range(3)]
    vir = [[], []]
    for s in range(3):
        v = slabs[s][pl.ds(greens + (5 - s) * HALF, HALF), :].astype(jnp.float32)
        v = v * (cols[2] * table[8 - s, block[s + 1]].astype(jnp.float32))
        vir[0].append(v * keep[s][0])
        vir[1].append(pltpu.roll(v, EDGE, 1) * keep[s][1])
    for par in range(2):
        vir[par].append(jnp.zeros((HALF, LANES), jnp.float32))
    turned = jnp.concatenate([jnp.concatenate(vir[par], 0).T[:EDGE] for par in range(2)], 1)
    which = lax.rem(lax.broadcasted_iota(jnp.int32, (EDGE, 2 * LANES), 1), LANES) // HALF
    for t in range(5):
        factor = jnp.zeros((EDGE, 2 * LANES), jnp.float32)
        for s in range(3):
            if 0 <= t - s <= 2:
                factor = jnp.where(which == s, table[t - s, block[s + 1]].astype(jnp.float32), factor)
        vir_ref[t] = (turned * factor).astype(jnp.bfloat16)
    for s in range(3):
        m = block[s + 1]
        for t in range(5):
            to = pl.ds(t * LANES, LANES)
            if 0 <= t - s <= 2:
                factor = (table[3 + t - s, m] * table[2 - s, m]).astype(jnp.float32)
                o = slabs[s][pl.ds(greens + (t - s) * HALF, HALF), :].astype(jnp.float32)
                o = o * (cols[t] * factor)
                swapped = pltpu.roll(o, EDGE, 1)
            for half in range(2):
                for par in range(2):
                    at = pl.ds((half * 6 + s * 2 + par) * HALF, HALF)
                    if 0 <= t - s <= 2:
                        value = (o if half == par else swapped) * keep[s][par]
                        occ_ref[at, to] = jnp.where(left == (half == 0), value, 0.0).astype(
                            jnp.bfloat16
                        )
                    else:
                        occ_ref[at, to] = jnp.zeros((HALF, LANES), jnp.bfloat16)

    blank = jnp.zeros((HALF, LANES), jnp.bfloat16)
    for j in range(rows // 2):
        sides = []
        for s in range(3):
            one = slabs[s][pl.ds(2 * j * block_rows, block_rows), :]
            two = slabs[s][pl.ds((2 * j + 1) * block_rows, block_rows), :]
            sides.append(
                (
                    jnp.concatenate([one[:, :EDGE], two[:, :EDGE]], 1),
                    jnp.concatenate([one[:, EDGE:], two[:, EDGE:]], 1),
                )
            )
        for t in range(5):
            parts = []
            for par in range(2):
                for s in range(3):
                    if 0 <= t - s <= 2:
                        parts.append(sides[s][par][(t - s) * HALF : (t - s + 1) * HALF])
                    else:
                        parts.append(blank)
                parts.append(blank)
            both = jnp.dot(
                vir_ref[t], jnp.concatenate(parts, 0), preferred_element_type=jnp.float32
            )
            half_ref[pl.ds(j * EDGE, EDGE), pl.ds(t * LANES, LANES)] = both.astype(jnp.bfloat16)
    for j in range(0, rows // 2, 4):
        full = lax.dot_general(
            occ_ref[...],
            half_ref[pl.ds(j * EDGE, 4 * EDGE), :],
            (((1,), (1,)), ((), ())),
            preferred_element_type=jnp.float32,
        )
        for half in range(2):
            for s in range(3):
                at = (half * 6 + s * 2) * HALF
                for pair in range(2):
                    to = slice(pair * LANES, (pair + 1) * LANES)
                    even = full[at : at + HALF, to]
                    odd = full[at + HALF : at + 2 * HALF, to]
                    first = 2 * (j + 2 * pair) + half
                    place = pl.ds(s * HALF, HALF)
                    full_ref[first, place, :] = jnp.where(
                        left, even, pltpu.roll(odd, EDGE, 1)
                    ).astype(jnp.bfloat16)
                    full_ref[first + 2, place, :] = jnp.where(
                        left, pltpu.roll(even, EDGE, 1), odd
                    ).astype(jnp.bfloat16)
    group = 16
    span = group * 16
    ri = lax.broadcasted_iota(jnp.int32, (span, span), 0)
    ci = lax.broadcasted_iota(jnp.int32, (span, span), 1)
    same = lax.rem(ri, 16) == lax.rem(ci, 16)
    pick = (
        lax.broadcasted_iota(jnp.int32, (span, group), 0) // 16
        == lax.broadcasted_iota(jnp.int32, (span, group), 1)
    ).astype(jnp.float32)
    for p in range(0, rows, group):
        for q in range(0, rows, group):
            acc = None
            for s in range(3):
                for c in range(2):
                    lhs = jnp.concatenate(
                        [
                            slabs[s][pl.ds(k * block_rows + (2 - s) * HALF + c * 16, 16), :]
                            for k in range(p, p + group)
                        ],
                        0,
                    )
                    rhs = full_ref[pl.ds(q, group), pl.ds(s * HALF + c * 16, 16), :]
                    one = lax.dot_general(
                        lhs,
                        rhs.reshape(span, LANES),
                        (((1,), (1,)), ((), ())),
                        preferred_element_type=jnp.float32,
                    )
                    acc = one if acc is None else acc + one
            kept = jnp.where(same, acc, 0.0).reshape(group, 16, span)
            summed = jnp.sum(kept, axis=1)
            out_ref[pl.ds(p, group), pl.ds(q, group)] = scale * jnp.dot(
                summed, pick, preferred_element_type=jnp.float32, precision=lax.Precision.HIGHEST
            )


def body(integrals, occupied, virtual, imask, omask, vmask, count):
    total = integrals.shape[1]
    members = lax.axis_size("blk")
    order = block_order(members)
    works_on = [order.index(d) for d in range(members)]

    rows, greens = pl.pallas_call(
        functools.partial(pack_kernel, works_on),
        out_shape=(
            jax.ShapeDtypeStruct((members, 3 * HALF, LANES), jnp.bfloat16),
            jax.ShapeDtypeStruct((6 * HALF, LANES), jnp.bfloat16),
        ),
        in_specs=[VMEM] * 3,
        out_specs=(VMEM, VMEM),
        scratch_shapes=[pltpu.VMEM((4, total * HALF, LANES), jnp.float32)],
        compiler_params=pltpu.CompilerParams(vmem_limit_bytes=32 * 1024 * 1024),
        name="pack",
    )(jnp.transpose(integrals[0], (1, 0, 2)), occupied[0], virtual[0])
    greens = lax.ppermute(greens, "blk", list(enumerate(order)))
    own = lax.all_to_all(rows, "blk", split_axis=0, concat_axis=0, tiled=True)
    slab = jnp.concatenate([own.reshape(members * 3 * HALF, LANES), greens], 0)
    forth = [(order[j], order[(j + 1) % members]) for j in range(members)]
    back = [(order[(j + 1) % members], order[j]) for j in range(members)]
    sprev = lax.ppermute(slab, "blk", forth)
    snext = lax.ppermute(slab, "blk", back)
    table = jnp.concatenate([imask.T, omask.T, vmask.T, count[None]], 0)
    part = pl.pallas_call(
        functools.partial(main_kernel, 1.0 / math.sqrt(5 * EDGE * EDGE * total), total, members),
        out_shape=jax.ShapeDtypeStruct((members, members), jnp.float32),
        in_specs=[SMEM] + [VMEM] * 3,
        out_specs=VMEM,
        scratch_shapes=[
            pltpu.VMEM((5, EDGE, 2 * LANES), jnp.bfloat16),
            pltpu.VMEM((12 * HALF, 5 * LANES), jnp.bfloat16),
            pltpu.VMEM((members // 2 * EDGE, 5 * LANES), jnp.bfloat16),
            pltpu.VMEM((members, 3 * HALF, LANES), jnp.bfloat16),
        ],
        compiler_params=pltpu.CompilerParams(vmem_limit_bytes=48 * 1024 * 1024),
        name="products",
    )(table, sprev, slab, snext)
    mine = lax.all_to_all(part, "blk", split_axis=0, concat_axis=0, tiled=True)
    return jnp.sum(mine, axis=0, keepdims=True)


def solution(mesh):
    return jax.shard_map(
        body,
        mesh=mesh,
        in_specs=(
            P(("grp", "blk"), None, None, None),
            P(("grp", "blk"), None, None),
            P(("grp", "blk"), None, None),
            P(),
            P(),
            P(),
            P(),
        ),
        out_specs=P(("grp", "blk"), None),
        check_vma=False,
    )
```

```python
import functools
import math

import jax
import jax.numpy as jnp
from jax import lax
from jax.experimental import pallas as pl
from jax.experimental.pallas import tpu as pltpu
from jax.sharding import PartitionSpec as P

EDGE = 64
HALF = 32
LANES = 128
VMEM = pl.BlockSpec(memory_space=pltpu.VMEM)
SMEM = pl.BlockSpec(memory_space=pltpu.SMEM)


def block_order(count):
    if count == 16:
        chips = [0, 2, 4, 6, 7, 5, 3, 1]
        return [2 * chip + core for chip in chips for core in (0, 1)]
    return list(range(count))


def pack_kernel(works_on, x_hbm, imask_hbm, out_hbm, x_ref, imask_ref, rows_ref, out_ref, sems):
    blocks = x_ref.shape[1]
    copies = [pltpu.make_async_copy(x_hbm.at[a], x_ref.at[a], sems.at[a]) for a in range(3)]
    masks = pltpu.make_async_copy(imask_hbm, imask_ref, sems.at[3])
    masks.start()
    for copy in copies:
        copy.start()
    diagonal = lax.broadcasted_iota(jnp.int32, (blocks, blocks), 0) == lax.broadcasted_iota(
        jnp.int32, (blocks, blocks), 1
    )
    masks.wait()
    sent = []
    for a in range(3):
        mask = jnp.where(diagonal, imask_ref[pl.ds(a, 1), :].astype(jnp.float32), 0.0)
        mask = jnp.broadcast_to(jnp.sum(mask, axis=1, keepdims=True), (blocks, LANES))
        copies[a].wait()
        for c in range(HALF):
            rows_ref[a, pl.ds(c, blocks, stride=HALF), :] = (
                x_ref[a, :, c * LANES : (c + 1) * LANES].astype(jnp.float32) * mask
            )
        part = pl.ds(a * HALF, HALF)
        for d, b in enumerate(works_on):
            out_ref[d, part, :] = rows_ref[a, pl.ds(b * HALF, HALF), :].astype(jnp.bfloat16)
        sent.append(
            pltpu.make_async_copy(out_ref.at[:, part, :], out_hbm.at[:, part, :], sems.at[4 + a])
        )
        sent[a].start()
    for copy in sent:
        copy.wait()


def prep_kernel(total, omask, vmask, count, occ_ref, vir_ref, out_ref, rows_ref):
    own = lax.axis_index("blk")
    for k, ref in enumerate((occ_ref, vir_ref)):
        for c in range(HALF):
            rows_ref[k, pl.ds(c, 3, stride=HALF), :] = ref[
                :, c * LANES : (c + 1) * LANES
            ].astype(jnp.float32)
    lane = lax.broadcasted_iota(jnp.int32, (HALF, LANES), 1)
    row = lax.broadcasted_iota(jnp.int32, (HALF, LANES), 0)
    left = lane < EDGE
    col = jnp.where(left, lane, lane - EDGE)
    keep = [(2 * row + par < count[own]).astype(jnp.float32) for par in range(2)]
    vir, occ = [], []
    for a in range(3):
        used = (col < count[lax.rem(own + (total + a - 1), total)]).astype(jnp.float32)
        v = rows_ref[1, pl.ds(a * HALF, HALF), :] * (used * vmask[a, own].astype(jnp.float32))
        vir += [v * keep[0], pltpu.roll(v, EDGE, 1) * keep[1]]
        o = rows_ref[0, pl.ds(a * HALF, HALF), :] * (used * omask[a, own].astype(jnp.float32))
        occ.append((pltpu.roll(o, EDGE, 1) * keep[0], o * keep[1]))
    vir += [jnp.zeros((HALF, LANES), jnp.float32)] * 2
    first = jnp.concatenate(vir[:4], 0).T[:EDGE]
    second = jnp.concatenate(vir[4:], 0).T[:EDGE]
    for a, turned in enumerate((first, pltpu.roll(first, EDGE, 1), second)):
        for par in range(2):
            out_ref[pl.ds((2 * a + par) * HALF, HALF), :] = jnp.where(
                left, turned[par * HALF : (par + 1) * HALF], occ[a][par]
            ).astype(jnp.bfloat16)


def main_kernel(scale, rows, sprev, sown, snext, out_ref, occ_ref, half_ref, full_ref):
    slabs = (sprev, sown, snext)
    block_rows = 3 * HALF
    greens = rows * block_rows
    left = lax.broadcasted_iota(jnp.int32, (HALF, LANES), 1) < EDGE

    def green(s, a):
        return slabs[s][pl.ds(greens + a * EDGE, EDGE), :]

    vir = jnp.concatenate([green(s, 2 - s)[:, :EDGE] for s in range(3)], 1)
    none = jnp.zeros((EDGE, EDGE), jnp.bfloat16)
    for s in range(3):
        for t in range(5):
            for half in range(2):
                at = pl.ds((half * 3 + s) * EDGE, EDGE)
                to = pl.ds(t * LANES, LANES)
                if 0 <= t - s <= 2:
                    o = green(s, t - s)[:, EDGE:]
                    occ_ref[at, to] = jnp.concatenate([none, o] if half else [o, none], 1)
                else:
                    occ_ref[at, to] = jnp.zeros((EDGE, LANES), jnp.bfloat16)

    blank = jnp.zeros((EDGE, LANES), jnp.bfloat16)
    for j in range(rows // 2):
        sides = []
        for s in range(3):
            one = slabs[s][pl.ds(2 * j * block_rows, block_rows), :]
            two = slabs[s][pl.ds((2 * j + 1) * block_rows, block_rows), :]
            sides.append(
                (
                    jnp.concatenate([one[:, :EDGE], two[:, :EDGE]], 1),
                    jnp.concatenate([one[:, EDGE:], two[:, EDGE:]], 1),
                )
            )
        for t in range(5):
            parts = []
            for s in range(3):
                if 0 <= t - s <= 2:
                    parts += [sides[s][par][(t - s) * HALF : (t - s + 1) * HALF] for par in range(2)]
                else:
                    parts.append(blank)
            both = jnp.dot(vir, jnp.concatenate(parts, 0), preferred_element_type=jnp.float32)
            half_ref[pl.ds(j * EDGE, EDGE), pl.ds(t * LANES, LANES)] = both.astype(jnp.bfloat16)
    for j in range(0, rows // 2, 4):
        full = lax.dot_general(
            occ_ref[...],
            half_ref[pl.ds(j * EDGE, 4 * EDGE), :],
            (((1,), (1,)), ((), ())),
            preferred_element_type=jnp.float32,
        )
        for half in range(2):
            for s in range(3):
                at = (half * 6 + s * 2) * HALF
                for pair in range(2):
                    to = slice(pair * LANES, (pair + 1) * LANES)
                    even = full[at : at + HALF, to]
                    odd = full[at + HALF : at + 2 * HALF, to]
                    first = 2 * (j + 2 * pair) + half
                    place = pl.ds(s * HALF, HALF)
                    full_ref[first, place, :] = jnp.where(
                        left, even, pltpu.roll(odd, EDGE, 1)
                    ).astype(jnp.bfloat16)
                    full_ref[first + 2, place, :] = jnp.where(
                        left, pltpu.roll(even, EDGE, 1), odd
                    ).astype(jnp.bfloat16)
    group = 16
    span = group * 16
    ri = lax.broadcasted_iota(jnp.int32, (span, span), 0)
    ci = lax.broadcasted_iota(jnp.int32, (span, span), 1)
    same = lax.rem(ri, 16) == lax.rem(ci, 16)
    pick = (
        lax.broadcasted_iota(jnp.int32, (span, group), 0) // 16
        == lax.broadcasted_iota(jnp.int32, (span, group), 1)
    ).astype(jnp.float32)
    for p in range(0, rows, group):
        for q in range(0, rows, group):
            acc = None
            for s in range(3):
                for c in range(2):
                    lhs = jnp.concatenate(
                        [
                            slabs[s][pl.ds(k * block_rows + (2 - s) * HALF + c * 16, 16), :]
                            for k in range(p, p + group)
                        ],
                        0,
                    )
                    rhs = full_ref[pl.ds(q, group), pl.ds(s * HALF + c * 16, 16), :]
                    one = lax.dot_general(
                        lhs,
                        rhs.reshape(span, LANES),
                        (((1,), (1,)), ((), ())),
                        preferred_element_type=jnp.float32,
                    )
                    acc = one if acc is None else acc + one
            kept = jnp.where(same, acc, 0.0).reshape(group, 16, span)
            summed = jnp.sum(kept, axis=1)
            out_ref[pl.ds(p, group), pl.ds(q, group)] = scale * jnp.dot(
                summed, pick, preferred_element_type=jnp.float32, precision=lax.Precision.HIGHEST
            )


def body(integrals, occupied, virtual, imask, omask, vmask, count):
    total = integrals.shape[1]
    members = lax.axis_size("blk")
    order = block_order(members)
    works_on = [order.index(d) for d in range(members)]

    rows = pl.pallas_call(
        functools.partial(pack_kernel, works_on),
        out_shape=jax.ShapeDtypeStruct((members, 3 * HALF, LANES), jnp.bfloat16),
        in_specs=[pl.BlockSpec(memory_space=pl.ANY)] * 2,
        out_specs=pl.BlockSpec(memory_space=pl.ANY),
        scratch_shapes=[
            pltpu.VMEM((3, total, EDGE * EDGE), jnp.bfloat16),
            pltpu.VMEM((3, total), jnp.int32),
            pltpu.VMEM((3, total * HALF, LANES), jnp.float32),
            pltpu.VMEM((members, 3 * HALF, LANES), jnp.bfloat16),
            pltpu.SemaphoreType.DMA((7,)),
        ],
        compiler_params=pltpu.CompilerParams(vmem_limit_bytes=63 * 1024 * 1024),
        name="pack",
    )(jnp.transpose(integrals[0], (1, 0, 2)), imask.T)
    greens = pl.pallas_call(
        functools.partial(prep_kernel, total),
        out_shape=jax.ShapeDtypeStruct((6 * HALF, LANES), jnp.bfloat16),
        in_specs=[SMEM] * 3 + [VMEM] * 2,
        out_specs=VMEM,
        scratch_shapes=[pltpu.VMEM((2, 3 * HALF, LANES), jnp.float32)],
        name="prep",
    )(omask.T, vmask.T, count, occupied[0], virtual[0])
    greens = lax.ppermute(greens, "blk", list(enumerate(order)))
    own = lax.all_to_all(rows, "blk", split_axis=0, concat_axis=0, tiled=True)
    slab = jnp.concatenate([own.reshape(members * 3 * HALF, LANES), greens], 0)
    forth = [(order[j], order[(j + 1) % members]) for j in range(members)]
    back = [(order[(j + 1) % members], order[j]) for j in range(members)]
    sprev = lax.ppermute(slab, "blk", forth)
    snext = lax.ppermute(slab, "blk", back)
    part = pl.pallas_call(
        functools.partial(main_kernel, 1.0 / math.sqrt(5 * EDGE * EDGE * total), members),
        out_shape=jax.ShapeDtypeStruct((members, members), jnp.float32),
        in_specs=[VMEM] * 3,
        out_specs=VMEM,
        scratch_shapes=[
            pltpu.VMEM((12 * HALF, 5 * LANES), jnp.bfloat16),
            pltpu.VMEM((members // 2 * EDGE, 5 * LANES), jnp.bfloat16),
            pltpu.VMEM((members, 3 * HALF, LANES), jnp.bfloat16),
        ],
        compiler_params=pltpu.CompilerParams(vmem_limit_bytes=48 * 1024 * 1024),
        name="products",
    )(sprev, slab, snext)
    mine = lax.all_to_all(part, "blk", split_axis=0, concat_axis=0, tiled=True)
    return jnp.sum(mine, axis=0, keepdims=True)


def solution(mesh):
    return jax.shard_map(
        body,
        mesh=mesh,
        in_specs=(
            P(("grp", "blk"), None, None, None),
            P(("grp", "blk"), None, None),
            P(("grp", "blk"), None, None),
            P(),
            P(),
            P(),
            P(),
        ),
        out_specs=P(("grp", "blk"), None),
        check_vma=False,
    )
```

```python
import functools
import math

import jax
import jax.numpy as jnp
from jax import lax
from jax.experimental import pallas as pl
from jax.experimental.pallas import tpu as pltpu
from jax.sharding import PartitionSpec as P

EDGE = 64
HALF = 32
LANES = 128
VMEM = pl.BlockSpec(memory_space=pltpu.VMEM)
SMEM = pl.BlockSpec(memory_space=pltpu.SMEM)


def block_order(count):
    if count == 16:
        chips = [0, 2, 4, 6, 7, 5, 3, 1]
        return [2 * chip + core for chip in chips for core in (0, 1)]
    return list(range(count))


def pack_kernel(works_on, x_hbm, imask_hbm, out_hbm, x_ref, imask_ref, rows_ref, out_ref, sems):
    blocks = x_ref.shape[1]
    copies = [pltpu.make_async_copy(x_hbm.at[a], x_ref.at[a], sems.at[a]) for a in range(3)]
    masks = pltpu.make_async_copy(imask_hbm, imask_ref, sems.at[3])
    masks.start()
    for copy in copies:
        copy.start()
    diagonal = lax.broadcasted_iota(jnp.int32, (blocks, blocks), 0) == lax.broadcasted_iota(
        jnp.int32, (blocks, blocks), 1
    )
    masks.wait()
    sent = []
    for a in range(3):
        mask = jnp.where(diagonal, imask_ref[pl.ds(a, 1), :].astype(jnp.float32), 0.0)
        mask = jnp.broadcast_to(jnp.sum(mask, axis=1, keepdims=True), (blocks, LANES))
        copies[a].wait()
        for c in range(HALF):
            rows_ref[a, pl.ds(c, blocks, stride=HALF), :] = (
                x_ref[a, :, c * LANES : (c + 1) * LANES].astype(jnp.float32) * mask
            )
        part = pl.ds(a * HALF, HALF)
        for d, b in enumerate(works_on):
            out_ref[d, part, :] = rows_ref[a, pl.ds(b * HALF, HALF), :].astype(jnp.bfloat16)
        sent.append(
            pltpu.make_async_copy(out_ref.at[:, part, :], out_hbm.at[:, part, :], sems.at[4 + a])
        )
        sent[a].start()
    for copy in sent:
        copy.wait()


def prep_kernel(total, omask, vmask, count, occ_ref, vir_ref, out_ref, rows_ref):
    own = lax.axis_index("blk")
    for k, ref in enumerate((occ_ref, vir_ref)):
        for c in range(HALF):
            rows_ref[k, pl.ds(c, 3, stride=HALF), :] = ref[
                :, c * LANES : (c + 1) * LANES
            ].astype(jnp.float32)
    lane = lax.broadcasted_iota(jnp.int32, (HALF, LANES), 1)
    row = lax.broadcasted_iota(jnp.int32, (HALF, LANES), 0)
    left = lane < EDGE
    col = jnp.where(left, lane, lane - EDGE)
    keep = [(2 * row + par < count[own]).astype(jnp.float32) for par in range(2)]
    vir, occ = [], []
    for a in range(3):
        used = (col < count[lax.rem(own + (total + a - 1), total)]).astype(jnp.float32)
        v = rows_ref[1, pl.ds(a * HALF, HALF), :] * (used * vmask[a, own].astype(jnp.float32))
        vir += [v * keep[0], pltpu.roll(v, EDGE, 1) * keep[1]]
        o = rows_ref[0, pl.ds(a * HALF, HALF), :] * (used * omask[a, own].astype(jnp.float32))
        occ.append((pltpu.roll(o, EDGE, 1) * keep[0], o * keep[1]))
    vir += [jnp.zeros((HALF, LANES), jnp.float32)] * 2
    first = jnp.concatenate(vir[:4], 0).T[:EDGE]
    second = jnp.concatenate(vir[4:], 0).T[:EDGE]
    for a, turned in enumerate((first, pltpu.roll(first, EDGE, 1), second)):
        for par in range(2):
            out_ref[pl.ds((2 * a + par) * HALF, HALF), :] = jnp.where(
                left, turned[par * HALF : (par + 1) * HALF], occ[a][par]
            ).astype(jnp.bfloat16)


def main_kernel(
    scale, rows, sprev, sown, gown, snext, out_ref, occ_ref, far_ref, half_ref, full_ref
):
    pair = 2 * HALF

    def slab(s, q, a):
        if s == 0:
            return sprev[pl.ds(q * pair + (a - 1) * HALF, HALF), :]
        if s == 2:
            return snext[pl.ds(q * pair + a * HALF, HALF), :]
        return sown[q, pl.ds(a * HALF, HALF), :]

    def green(s, a):
        if s == 0:
            return sprev[pl.ds(rows * pair + (a - 1) * EDGE, EDGE), :]
        if s == 2:
            return snext[pl.ds(rows * pair + a * EDGE, EDGE), :]
        return gown[pl.ds(a * EDGE, EDGE), :]

    none = jnp.zeros((EDGE, EDGE), jnp.bfloat16)
    near = [green(0, 2)[:, :EDGE], green(1, 1)[:, :EDGE], green(2, 0)[:, :EDGE]]
    vir = [
        jnp.concatenate(
            [
                jnp.concatenate(near[:2], 1),
                jnp.concatenate([none, green(1, 2)[:, :EDGE]], 1),
            ],
            0,
        ),
        jnp.concatenate(near, 1),
        jnp.concatenate(
            [
                jnp.concatenate(near[1:], 1),
                jnp.concatenate([green(1, 0)[:, :EDGE], none], 1),
            ],
            0,
        ),
    ]
    used = ({0: 1, 1: 2}, {0: 0, 1: 1, 2: 2}, {1: 0, 2: 1})
    for s in range(3):
        for t in range(3):
            for half in range(2):
                at = pl.ds((half * 3 + s) * EDGE, EDGE)
                to = pl.ds(t * LANES, LANES)
                if t in used[s]:
                    o = green(s, used[s][t])[:, EDGE:]
                    occ_ref[at, to] = jnp.concatenate([none, o] if half else [o, none], 1)
                else:
                    occ_ref[at, to] = jnp.zeros((EDGE, LANES), jnp.bfloat16)
    for k in range(2):
        o = green(1, 2 * k)[:, EDGE:]
        far_ref[k] = jnp.concatenate(
            [jnp.concatenate([o, none], 1), jnp.concatenate([none, o], 1)], 0
        )

    members = (((0, 1), (1, 0)), ((0, 2), (1, 1), (2, 0)), ((1, 2), (2, 1)))
    for j in range(0, rows // 2, 2):

        def side(s, a):
            even, odd = [], []
            for k in range(j, j + 2):
                one, two = slab(s, 2 * k, a), slab(s, 2 * k + 1, a)
                even.append(jnp.concatenate([one[:, :EDGE], two[:, :EDGE]], 1))
                odd.append(jnp.concatenate([one[:, EDGE:], two[:, EDGE:]], 1))
            return [jnp.concatenate(even, 1), jnp.concatenate(odd, 1)]

        for t in range(3):
            parts = []
            for s, a in members[t]:
                parts += side(s, a)
            both = jnp.dot(vir[t], jnp.concatenate(parts, 0), preferred_element_type=jnp.float32)
            both = both.astype(jnp.bfloat16)
            for k in range(2):
                at = pl.ds((j + k) * EDGE, EDGE)
                piece = both[:, k * LANES : (k + 1) * LANES]
                half_ref[at, pl.ds(t * LANES, LANES)] = piece[:EDGE]
                if t != 1:
                    half_ref[at, pl.ds((3 + t // 2) * LANES, LANES)] = piece[EDGE:]

    left = lax.broadcasted_iota(jnp.int32, (HALF, LANES), 1) < EDGE
    for j in range(0, rows // 2, 4):
        at = pl.ds(j * EDGE, 4 * EDGE)
        nt = (((1,), (1,)), ((), ()))
        full = lax.dot_general(
            occ_ref[...], half_ref[at, pl.ds(0, 3 * LANES)], nt, preferred_element_type=jnp.float32
        )
        far = [
            lax.dot_general(
                far_ref[k],
                half_ref[at, pl.ds((3 + k) * LANES, LANES)],
                nt,
                preferred_element_type=jnp.float32,
            )
            for k in range(2)
        ]
        for half in range(2):
            for g in range(5):
                if g < 3:
                    block = full[(half * 3 + g) * EDGE : (half * 3 + g + 1) * EDGE]
                else:
                    block = far[g - 3][half * EDGE : (half + 1) * EDGE]
                for k in range(2):
                    even = block[:HALF, k * LANES : (k + 1) * LANES]
                    odd = block[HALF:, k * LANES : (k + 1) * LANES]
                    first = 2 * (j + 2 * k) + half
                    place = pl.ds(g * HALF, HALF)
                    full_ref[first, place, :] = jnp.where(
                        left, even, pltpu.roll(odd, EDGE, 1)
                    ).astype(jnp.bfloat16)
                    full_ref[first + 2, place, :] = jnp.where(
                        left, pltpu.roll(even, EDGE, 1), odd
                    ).astype(jnp.bfloat16)

    group = 16
    span = group * 16
    ri = lax.broadcasted_iota(jnp.int32, (span, span), 0)
    ci = lax.broadcasted_iota(jnp.int32, (span, span), 1)
    same = lax.rem(ri, 16) == lax.rem(ci, 16)
    pick = (
        lax.broadcasted_iota(jnp.int32, (span, group), 0) // 16
        == lax.broadcasted_iota(jnp.int32, (span, group), 1)
    ).astype(jnp.float32)
    for p in range(0, rows, group):
        for q in range(0, rows, group):
            acc = None
            for g, (s, a) in enumerate(((0, 2), (1, 1), (2, 0), (1, 2), (1, 0))):
                lhs = [slab(s, k, a) for k in range(p, p + group)]
                lhs = [jnp.concatenate([x[:16], x[16:]], 1) for x in lhs]
                rhs = [
                    full_ref[pl.ds(q, group), pl.ds(g * HALF + c * 16, 16), :].reshape(span, LANES)
                    for c in range(2)
                ]
                one = lax.dot_general(
                    jnp.concatenate(lhs, 0),
                    jnp.concatenate(rhs, 1),
                    (((1,), (1,)), ((), ())),
                    preferred_element_type=jnp.float32,
                )
                acc = one if acc is None else acc + one
            kept = jnp.where(same, acc, 0.0).reshape(group, 16, span)
            summed = jnp.sum(kept, axis=1)
            out_ref[pl.ds(p, group), pl.ds(q, group)] = scale * jnp.dot(
                summed, pick, preferred_element_type=jnp.float32, precision=lax.Precision.HIGHEST
            )


def body(integrals, occupied, virtual, imask, omask, vmask, count):
    total = integrals.shape[1]
    members = lax.axis_size("blk")
    order = block_order(members)
    works_on = [order.index(d) for d in range(members)]

    rows = pl.pallas_call(
        functools.partial(pack_kernel, works_on),
        out_shape=jax.ShapeDtypeStruct((members, 3 * HALF, LANES), jnp.bfloat16),
        in_specs=[pl.BlockSpec(memory_space=pl.ANY)] * 2,
        out_specs=pl.BlockSpec(memory_space=pl.ANY),
        scratch_shapes=[
            pltpu.VMEM((3, total, EDGE * EDGE), jnp.bfloat16),
            pltpu.VMEM((3, total), jnp.int32),
            pltpu.VMEM((3, total * HALF, LANES), jnp.float32),
            pltpu.VMEM((members, 3 * HALF, LANES), jnp.bfloat16),
            pltpu.SemaphoreType.DMA((7,)),
        ],
        compiler_params=pltpu.CompilerParams(vmem_limit_bytes=63 * 1024 * 1024),
        name="pack",
    )(jnp.transpose(integrals[0], (1, 0, 2)), imask.T)
    greens = pl.pallas_call(
        functools.partial(prep_kernel, total),
        out_shape=jax.ShapeDtypeStruct((6 * HALF, LANES), jnp.bfloat16),
        in_specs=[SMEM] * 3 + [VMEM] * 2,
        out_specs=VMEM,
        scratch_shapes=[pltpu.VMEM((2, 3 * HALF, LANES), jnp.float32)],
        name="prep",
    )(omask.T, vmask.T, count, occupied[0], virtual[0])
    greens = lax.ppermute(greens, "blk", list(enumerate(order)))
    own = lax.all_to_all(rows, "blk", split_axis=0, concat_axis=0, tiled=True)
    forth = [(order[j], order[(j + 1) % members]) for j in range(members)]
    back = [(order[(j + 1) % members], order[j]) for j in range(members)]
    later = jnp.concatenate([own[:, HALF:].reshape(-1, LANES), greens[EDGE:]], 0)
    early = jnp.concatenate([own[:, : 2 * HALF].reshape(-1, LANES), greens[: 2 * EDGE]], 0)
    sprev = lax.ppermute(later, "blk", forth)
    snext = lax.ppermute(early, "blk", back)
    part = pl.pallas_call(
        functools.partial(main_kernel, 1.0 / math.sqrt(5 * EDGE * EDGE * total), members),
        out_shape=jax.ShapeDtypeStruct((members, members), jnp.float32),
        in_specs=[VMEM] * 4,
        out_specs=VMEM,
        scratch_shapes=[
            pltpu.VMEM((6 * EDGE, 3 * LANES), jnp.bfloat16),
            pltpu.VMEM((2, 2 * EDGE, LANES), jnp.bfloat16),
            pltpu.VMEM((members // 2 * EDGE, 5 * LANES), jnp.bfloat16),
            pltpu.VMEM((members, 5 * HALF, LANES), jnp.bfloat16),
        ],
        compiler_params=pltpu.CompilerParams(vmem_limit_bytes=48 * 1024 * 1024),
        name="products",
    )(sprev, own, greens, snext)
    mine = lax.all_to_all(part, "blk", split_axis=0, concat_axis=0, tiled=True)
    return jnp.sum(mine, axis=0, keepdims=True)


def solution(mesh):
    return jax.shard_map(
        body,
        mesh=mesh,
        in_specs=(
            P(("grp", "blk"), None, None, None),
            P(("grp", "blk"), None, None),
            P(("grp", "blk"), None, None),
            P(),
            P(),
            P(),
            P(),
        ),
        out_specs=P(("grp", "blk"), None),
        check_vma=False,
    )
```

```python
import functools
import math

import jax
import jax.numpy as jnp
from jax import lax
from jax.experimental import pallas as pl
from jax.experimental.pallas import tpu as pltpu
from jax.sharding import PartitionSpec as P

EDGE = 64
HALF = 32
LANES = 128
VMEM = pl.BlockSpec(memory_space=pltpu.VMEM)
SMEM = pl.BlockSpec(memory_space=pltpu.SMEM)


def block_order(count):
    if count == 16:
        chips = [0, 2, 4, 6, 7, 5, 3, 1]
        return [2 * chip + core for chip in chips for core in (0, 1)]
    return list(range(count))


def block_of(device, count):
    order = block_order(count)
    if order == list(range(count)):
        return device
    block = jnp.int32(0)
    for j, d in enumerate(order):
        block = jnp.where(device == d, j, block)
    return block


def pack_kernel(works_on, x_ref, out_ref, rows_ref):
    blocks = x_ref.shape[1]
    for a in range(3):
        for c in range(HALF):
            rows_ref[a, pl.ds(c, blocks, stride=HALF), :] = x_ref[
                a, :, c * LANES : (c + 1) * LANES
            ].astype(jnp.float32)
        for d, b in enumerate(works_on):
            out_ref[d, pl.ds(a * HALF, HALF), :] = rows_ref[a, pl.ds(b * HALF, HALF), :].astype(
                jnp.bfloat16
            )


def prep_kernel(total, omask, vmask, count, occ_ref, vir_ref, out_ref, rows_ref):
    own = lax.axis_index("blk")
    for k, ref in enumerate((occ_ref, vir_ref)):
        for c in range(HALF):
            rows_ref[k, pl.ds(c, 3, stride=HALF), :] = ref[
                :, c * LANES : (c + 1) * LANES
            ].astype(jnp.float32)
    lane = lax.broadcasted_iota(jnp.int32, (HALF, LANES), 1)
    row = lax.broadcasted_iota(jnp.int32, (HALF, LANES), 0)
    left = lane < EDGE
    col = jnp.where(left, lane, lane - EDGE)
    keep = [(2 * row + par < count[own]).astype(jnp.float32) for par in range(2)]
    vir, occ = [], []
    for a in range(3):
        used = (col < count[lax.rem(own + (total + a - 1), total)]).astype(jnp.float32)
        v = rows_ref[1, pl.ds(a * HALF, HALF), :] * (used * vmask[a, own].astype(jnp.float32))
        vir += [v * keep[0], pltpu.roll(v, EDGE, 1) * keep[1]]
        o = rows_ref[0, pl.ds(a * HALF, HALF), :] * (used * omask[a, own].astype(jnp.float32))
        occ.append((pltpu.roll(o, EDGE, 1) * keep[0], o * keep[1]))
    vir += [jnp.zeros((HALF, LANES), jnp.float32)] * 2
    first = jnp.concatenate(vir[:4], 0).T[:EDGE]
    second = jnp.concatenate(vir[4:], 0).T[:EDGE]
    for a, turned in enumerate((first, pltpu.roll(first, EDGE, 1), second)):
        for par in range(2):
            out_ref[pl.ds((2 * a + par) * HALF, HALF), :] = jnp.where(
                left, turned[par * HALF : (par + 1) * HALF], occ[a][par]
            ).astype(jnp.bfloat16)


def main_kernel(
    scale, rows, imask, sprev, sown, gown, snext, out_ref, occ_ref, far_ref, half_ref, full_ref
):
    pair = 2 * HALF

    def slab(s, q, a):
        if s == 0:
            return sprev[pl.ds(q * pair + (a - 1) * HALF, HALF), :]
        if s == 2:
            return snext[pl.ds(q * pair + a * HALF, HALF), :]
        return sown[q, pl.ds(a * HALF, HALF), :]

    def green(s, a):
        if s == 0:
            return sprev[pl.ds(rows * pair + (a - 1) * EDGE, EDGE), :]
        if s == 2:
            return snext[pl.ds(rows * pair + a * EDGE, EDGE), :]
        return gown[pl.ds(a * EDGE, EDGE), :]

    own = block_of(lax.axis_index("blk"), rows)
    block = [lax.rem(own + (rows + s - 1), rows) for s in range(3)]

    def screened(x, *at):
        x = x.astype(jnp.float32)
        for s, a in at:
            x = x * imask[a, block[s]].astype(jnp.float32)
        return x.astype(jnp.bfloat16)

    none = jnp.zeros((EDGE, EDGE), jnp.bfloat16)

    def vir_part(s, to, a):
        return screened(green(s, to)[:, :EDGE], (s, a))

    members = (((0, 1), (1, 0)), ((0, 2), (1, 1), (2, 0)), ((1, 2), (2, 1)))
    vir = [jnp.concatenate([vir_part(s, 2 - s, a) for s, a in members[t]], 1) for t in range(3)]
    vir[0] = jnp.concatenate([vir[0], jnp.concatenate([none, vir_part(1, 2, 0)], 1)], 0)
    vir[2] = jnp.concatenate([vir[2], jnp.concatenate([vir_part(1, 0, 2), none], 1)], 0)
    used = ({0: 1, 1: 2}, {0: 0, 1: 1, 2: 2}, {1: 0, 2: 1})
    for s in range(3):
        for t in range(3):
            for half in range(2):
                at = pl.ds((half * 3 + s) * EDGE, EDGE)
                to = pl.ds(t * LANES, LANES)
                if t in used[s]:
                    o = screened(green(s, used[s][t])[:, EDGE:], (s, 2 - s))
                    occ_ref[at, to] = jnp.concatenate([none, o] if half else [o, none], 1)
                else:
                    occ_ref[at, to] = jnp.zeros((EDGE, LANES), jnp.bfloat16)
    for k in range(2):
        o = screened(green(1, 2 * k)[:, EDGE:], (1, 2 - 2 * k))
        far_ref[k] = jnp.concatenate(
            [jnp.concatenate([o, none], 1), jnp.concatenate([none, o], 1)], 0
        )

    for j in range(0, rows // 2, 2):

        def side(s, a):
            even, odd = [], []
            for k in range(j, j + 2):
                one, two = slab(s, 2 * k, a), slab(s, 2 * k + 1, a)
                even.append(jnp.concatenate([one[:, :EDGE], two[:, :EDGE]], 1))
                odd.append(jnp.concatenate([one[:, EDGE:], two[:, EDGE:]], 1))
            return [jnp.concatenate(even, 1), jnp.concatenate(odd, 1)]

        for t in range(3):
            parts = []
            for s, a in members[t]:
                parts += side(s, a)
            both = jnp.dot(vir[t], jnp.concatenate(parts, 0), preferred_element_type=jnp.float32)
            both = both.astype(jnp.bfloat16)
            for k in range(2):
                at = pl.ds((j + k) * EDGE, EDGE)
                piece = both[:, k * LANES : (k + 1) * LANES]
                half_ref[at, pl.ds(t * LANES, LANES)] = piece[:EDGE]
                if t != 1:
                    half_ref[at, pl.ds((3 + t // 2) * LANES, LANES)] = piece[EDGE:]

    left = lax.broadcasted_iota(jnp.int32, (HALF, LANES), 1) < EDGE
    for j in range(0, rows // 2, 4):
        at = pl.ds(j * EDGE, 4 * EDGE)
        nt = (((1,), (1,)), ((), ()))
        full = lax.dot_general(
            occ_ref[...], half_ref[at, pl.ds(0, 3 * LANES)], nt, preferred_element_type=jnp.float32
        )
        far = [
            lax.dot_general(
                far_ref[k],
                half_ref[at, pl.ds((3 + k) * LANES, LANES)],
                nt,
                preferred_element_type=jnp.float32,
            )
            for k in range(2)
        ]
        for half in range(2):
            for g in range(5):
                if g < 3:
                    block = full[(half * 3 + g) * EDGE : (half * 3 + g + 1) * EDGE]
                else:
                    block = far[g - 3][half * EDGE : (half + 1) * EDGE]
                for k in range(2):
                    even = block[:HALF, k * LANES : (k + 1) * LANES]
                    odd = block[HALF:, k * LANES : (k + 1) * LANES]
                    first = 2 * (j + 2 * k) + half
                    place = pl.ds(g * HALF, HALF)
                    full_ref[first, place, :] = jnp.where(
                        left, even, pltpu.roll(odd, EDGE, 1)
                    ).astype(jnp.bfloat16)
                    full_ref[first + 2, place, :] = jnp.where(
                        left, pltpu.roll(even, EDGE, 1), odd
                    ).astype(jnp.bfloat16)

    group = 16
    span = group * 16
    ri = lax.broadcasted_iota(jnp.int32, (span, span), 0)
    ci = lax.broadcasted_iota(jnp.int32, (span, span), 1)
    same = lax.rem(ri, 16) == lax.rem(ci, 16)
    pick = (
        lax.broadcasted_iota(jnp.int32, (span, group), 0) // 16
        == lax.broadcasted_iota(jnp.int32, (span, group), 1)
    ).astype(jnp.float32)
    for p in range(0, rows, group):
        for q in range(0, rows, group):
            acc = None
            for g, (s, a) in enumerate(((0, 2), (1, 1), (2, 0), (1, 2), (1, 0))):
                lhs = [slab(s, k, a) for k in range(p, p + group)]
                lhs = [jnp.concatenate([x[:16], x[16:]], 1) for x in lhs]
                rhs = [
                    full_ref[pl.ds(q, group), pl.ds(g * HALF + c * 16, 16), :].reshape(span, LANES)
                    for c in range(2)
                ]
                one = lax.dot_general(
                    jnp.concatenate(lhs, 0),
                    jnp.concatenate(rhs, 1),
                    (((1,), (1,)), ((), ())),
                    preferred_element_type=jnp.float32,
                )
                acc = one if acc is None else acc + one
            kept = jnp.where(same, acc, 0.0).reshape(group, 16, span)
            summed = jnp.sum(kept, axis=1)
            out_ref[pl.ds(p, group), pl.ds(q, group)] = scale * jnp.dot(
                summed, pick, preferred_element_type=jnp.float32, precision=lax.Precision.HIGHEST
            )


def body(integrals, occupied, virtual, imask, omask, vmask, count):
    total = integrals.shape[1]
    members = lax.axis_size("blk")
    order = block_order(members)
    works_on = [order.index(d) for d in range(members)]

    rows = pl.pallas_call(
        functools.partial(pack_kernel, works_on),
        out_shape=jax.ShapeDtypeStruct((members, 3 * HALF, LANES), jnp.bfloat16),
        in_specs=[VMEM],
        out_specs=VMEM,
        scratch_shapes=[pltpu.VMEM((3, total * HALF, LANES), jnp.float32)],
        compiler_params=pltpu.CompilerParams(vmem_limit_bytes=max(8, total // 4) * 1024 * 1024),
        name="pack",
    )(jnp.transpose(integrals[0], (1, 0, 2)))
    greens = pl.pallas_call(
        functools.partial(prep_kernel, total),
        out_shape=jax.ShapeDtypeStruct((6 * HALF, LANES), jnp.bfloat16),
        in_specs=[SMEM] * 3 + [VMEM] * 2,
        out_specs=VMEM,
        scratch_shapes=[pltpu.VMEM((2, 3 * HALF, LANES), jnp.float32)],
        name="prep",
    )(omask.T, vmask.T, count, occupied[0], virtual[0])
    greens = lax.ppermute(greens, "blk", list(enumerate(order)))
    own = lax.all_to_all(rows, "blk", split_axis=0, concat_axis=0, tiled=True)
    forth = [(order[j], order[(j + 1) % members]) for j in range(members)]
    back = [(order[(j + 1) % members], order[j]) for j in range(members)]
    later = jnp.concatenate([own[:, HALF:].reshape(-1, LANES), greens[EDGE:]], 0)
    early = jnp.concatenate([own[:, : 2 * HALF].reshape(-1, LANES), greens[: 2 * EDGE]], 0)
    sprev = lax.ppermute(later, "blk", forth)
    snext = lax.ppermute(early, "blk", back)
    part = pl.pallas_call(
        functools.partial(main_kernel, 1.0 / math.sqrt(5 * EDGE * EDGE * total), members),
        out_shape=jax.ShapeDtypeStruct((members, members), jnp.float32),
        in_specs=[SMEM] + [VMEM] * 4,
        out_specs=VMEM,
        scratch_shapes=[
            pltpu.VMEM((6 * EDGE, 3 * LANES), jnp.bfloat16),
            pltpu.VMEM((2, 2 * EDGE, LANES), jnp.bfloat16),
            pltpu.VMEM((members // 2 * EDGE, 5 * LANES), jnp.bfloat16),
            pltpu.VMEM((members, 5 * HALF, LANES), jnp.bfloat16),
        ],
        compiler_params=pltpu.CompilerParams(vmem_limit_bytes=48 * 1024 * 1024),
        name="products",
    )(imask.T, sprev, own, greens, snext)
    mine = lax.all_to_all(part, "blk", split_axis=0, concat_axis=0, tiled=True)
    return jnp.sum(mine, axis=0, keepdims=True)


def solution(mesh):
    return jax.shard_map(
        body,
        mesh=mesh,
        in_specs=(
            P(("grp", "blk"), None, None, None),
            P(("grp", "blk"), None, None),
            P(("grp", "blk"), None, None),
            P(),
            P(),
            P(),
            P(),
        ),
        out_specs=P(("grp", "blk"), None),
        check_vma=False,
    )
```

```python
import functools
import math

import jax
import jax.numpy as jnp
from jax import lax
from jax.experimental import pallas as pl
from jax.experimental.pallas import tpu as pltpu
from jax.sharding import PartitionSpec as P

EDGE = 64
HALF = 32
LANES = 128
VMEM = pl.BlockSpec(memory_space=pltpu.VMEM)
SMEM = pl.BlockSpec(memory_space=pltpu.SMEM)


def block_order(count):
    if count == 16:
        chips = [3, 1, 0, 2, 4, 6, 7, 5]
        return [2 * chip + core for chip in chips for core in (0, 1)]
    return list(range(count))


def pack_kernel(works_on, x_hbm, imask_hbm, out_hbm, x_ref, imask_ref, rows_ref, out_ref, sems):
    blocks = x_ref.shape[1]
    copies = [pltpu.make_async_copy(x_hbm.at[a], x_ref.at[a], sems.at[a]) for a in range(3)]
    masks = pltpu.make_async_copy(imask_hbm, imask_ref, sems.at[3])
    masks.start()
    for copy in copies:
        copy.start()
    diagonal = lax.broadcasted_iota(jnp.int32, (blocks, blocks), 0) == lax.broadcasted_iota(
        jnp.int32, (blocks, blocks), 1
    )
    masks.wait()
    sent = []
    for a in range(3):
        mask = jnp.where(diagonal, imask_ref[pl.ds(a, 1), :].astype(jnp.float32), 0.0)
        mask = jnp.broadcast_to(jnp.sum(mask, axis=1, keepdims=True), (blocks, LANES))
        copies[a].wait()
        for c in range(HALF):
            rows_ref[a, pl.ds(c, blocks, stride=HALF), :] = (
                x_ref[a, :, c * LANES : (c + 1) * LANES].astype(jnp.float32) * mask
            )
        part = pl.ds(a * HALF, HALF)
        for d, b in enumerate(works_on):
            out_ref[d, part, :] = rows_ref[a, pl.ds(b * HALF, HALF), :].astype(jnp.bfloat16)
        sent.append(
            pltpu.make_async_copy(out_ref.at[:, part, :], out_hbm.at[:, part, :], sems.at[4 + a])
        )
        sent[a].start()
    for copy in sent:
        copy.wait()


def prep_kernel(total, omask, vmask, count, occ_ref, vir_ref, out_ref, rows_ref):
    own = lax.axis_index("blk")
    for k, ref in enumerate((occ_ref, vir_ref)):
        for c in range(HALF):
            rows_ref[k, pl.ds(c, 3, stride=HALF), :] = ref[
                :, c * LANES : (c + 1) * LANES
            ].astype(jnp.float32)
    lane = lax.broadcasted_iota(jnp.int32, (HALF, LANES), 1)
    row = lax.broadcasted_iota(jnp.int32, (HALF, LANES), 0)
    left = lane < EDGE
    col = jnp.where(left, lane, lane - EDGE)
    keep = [(2 * row + par < count[own]).astype(jnp.float32) for par in range(2)]
    vir, occ = [], []
    for a in range(3):
        used = (col < count[lax.rem(own + (total + a - 1), total)]).astype(jnp.float32)
        v = rows_ref[1, pl.ds(a * HALF, HALF), :] * (used * vmask[a, own].astype(jnp.float32))
        vir += [v * keep[0], pltpu.roll(v, EDGE, 1) * keep[1]]
        o = rows_ref[0, pl.ds(a * HALF, HALF), :] * (used * omask[a, own].astype(jnp.float32))
        occ.append((pltpu.roll(o, EDGE, 1) * keep[0], o * keep[1]))
    vir += [jnp.zeros((HALF, LANES), jnp.float32)] * 2
    first = jnp.concatenate(vir[:4], 0).T[:EDGE]
    second = jnp.concatenate(vir[4:], 0).T[:EDGE]
    for a, turned in enumerate((first, pltpu.roll(first, EDGE, 1), second)):
        for par in range(2):
            out_ref[pl.ds((2 * a + par) * HALF, HALF), :] = jnp.where(
                left, turned[par * HALF : (par + 1) * HALF], occ[a][par]
            ).astype(jnp.bfloat16)


def main_kernel(
    scale, rows, sprev, sown, gown, snext, out_ref, occ_ref, far_ref, half_ref, full_ref
):
    pair = 2 * HALF

    def slab(s, q, a):
        if s == 0:
            return sprev[pl.ds(q * pair + (a - 1) * HALF, HALF), :]
        if s == 2:
            return snext[pl.ds(q * pair + a * HALF, HALF), :]
        return sown[q, pl.ds(a * HALF, HALF), :]

    def green(s, a):
        if s == 0:
            return sprev[pl.ds(rows * pair + (a - 1) * EDGE, EDGE), :]
        if s == 2:
            return snext[pl.ds(rows * pair + a * EDGE, EDGE), :]
        return gown[pl.ds(a * EDGE, EDGE), :]

    none = jnp.zeros((EDGE, EDGE), jnp.bfloat16)
    near = [green(0, 2)[:, :EDGE], green(1, 1)[:, :EDGE], green(2, 0)[:, :EDGE]]
    vir = [
        jnp.concatenate(
            [
                jnp.concatenate(near[:2], 1),
                jnp.concatenate([none, green(1, 2)[:, :EDGE]], 1),
            ],
            0,
        ),
        jnp.concatenate(near, 1),
        jnp.concatenate(
            [
                jnp.concatenate(near[1:], 1),
                jnp.concatenate([green(1, 0)[:, :EDGE], none], 1),
            ],
            0,
        ),
    ]
    used = ({0: 1, 1: 2}, {0: 0, 1: 1, 2: 2}, {1: 0, 2: 1})
    for s in range(3):
        for t in range(3):
            for half in range(2):
                at = pl.ds((half * 3 + s) * EDGE, EDGE)
                to = pl.ds(t * LANES, LANES)
                if t in used[s]:
                    o = green(s, used[s][t])[:, EDGE:]
                    occ_ref[at, to] = jnp.concatenate([none, o] if half else [o, none], 1)
                else:
                    occ_ref[at, to] = jnp.zeros((EDGE, LANES), jnp.bfloat16)
    for k in range(2):
        o = green(1, 2 * k)[:, EDGE:]
        far_ref[k] = jnp.concatenate(
            [jnp.concatenate([o, none], 1), jnp.concatenate([none, o], 1)], 0
        )

    members = (((0, 1), (1, 0)), ((0, 2), (1, 1), (2, 0)), ((1, 2), (2, 1)))
    for j in range(0, rows // 2, 2):

        def side(s, a):
            even, odd = [], []
            for k in range(j, j + 2):
                one, two = slab(s, 2 * k, a), slab(s, 2 * k + 1, a)
                even.append(jnp.concatenate([one[:, :EDGE], two[:, :EDGE]], 1))
                odd.append(jnp.concatenate([one[:, EDGE:], two[:, EDGE:]], 1))
            return [jnp.concatenate(even, 1), jnp.concatenate(odd, 1)]

        for t in range(3):
            parts = []
            for s, a in members[t]:
                parts += side(s, a)
            both = jnp.dot(vir[t], jnp.concatenate(parts, 0), preferred_element_type=jnp.float32)
            both = both.astype(jnp.bfloat16)
            for k in range(2):
                at = pl.ds((j + k) * EDGE, EDGE)
                piece = both[:, k * LANES : (k + 1) * LANES]
                half_ref[at, pl.ds(t * LANES, LANES)] = piece[:EDGE]
                if t != 1:
                    half_ref[at, pl.ds((3 + t // 2) * LANES, LANES)] = piece[EDGE:]

    left = lax.broadcasted_iota(jnp.int32, (HALF, LANES), 1) < EDGE
    for j in range(0, rows // 2, 4):
        at = pl.ds(j * EDGE, 4 * EDGE)
        nt = (((1,), (1,)), ((), ()))
        full = lax.dot_general(
            occ_ref[...], half_ref[at, pl.ds(0, 3 * LANES)], nt, preferred_element_type=jnp.float32
        )
        far = [
            lax.dot_general(
                far_ref[k],
                half_ref[at, pl.ds((3 + k) * LANES, LANES)],
                nt,
                preferred_element_type=jnp.float32,
            )
            for k in range(2)
        ]
        for half in range(2):
            for g in range(5):
                if g < 3:
                    block = full[(half * 3 + g) * EDGE : (half * 3 + g + 1) * EDGE]
                else:
                    block = far[g - 3][half * EDGE : (half + 1) * EDGE]
                for k in range(2):
                    even = block[:HALF, k * LANES : (k + 1) * LANES]
                    odd = block[HALF:, k * LANES : (k + 1) * LANES]
                    first = 2 * (j + 2 * k) + half
                    place = pl.ds(g * HALF, HALF)
                    full_ref[first, place, :] = jnp.where(
                        left, even, pltpu.roll(odd, EDGE, 1)
                    ).astype(jnp.bfloat16)
                    full_ref[first + 2, place, :] = jnp.where(
                        left, pltpu.roll(even, EDGE, 1), odd
                    ).astype(jnp.bfloat16)

    group = 16
    span = group * 16
    ri = lax.broadcasted_iota(jnp.int32, (span, span), 0)
    ci = lax.broadcasted_iota(jnp.int32, (span, span), 1)
    same = lax.rem(ri, 16) == lax.rem(ci, 16)
    pick = (
        lax.broadcasted_iota(jnp.int32, (span, group), 0) // 16
        == lax.broadcasted_iota(jnp.int32, (span, group), 1)
    ).astype(jnp.float32)
    for p in range(0, rows, group):
        for q in range(0, rows, group):
            acc = None
            for g, (s, a) in enumerate(((0, 2), (1, 1), (2, 0), (1, 2), (1, 0))):
                lhs = [slab(s, k, a) for k in range(p, p + group)]
                lhs = [jnp.concatenate([x[:16], x[16:]], 1) for x in lhs]
                rhs = [
                    full_ref[pl.ds(q, group), pl.ds(g * HALF + c * 16, 16), :].reshape(span, LANES)
                    for c in range(2)
                ]
                one = lax.dot_general(
                    jnp.concatenate(lhs, 0),
                    jnp.concatenate(rhs, 1),
                    (((1,), (1,)), ((), ())),
                    preferred_element_type=jnp.float32,
                )
                acc = one if acc is None else acc + one
            kept = jnp.where(same, acc, 0.0).reshape(group, 16, span)
            summed = jnp.sum(kept, axis=1)
            out_ref[pl.ds(p, group), pl.ds(q, group)] = scale * jnp.dot(
                summed, pick, preferred_element_type=jnp.float32, precision=lax.Precision.HIGHEST
            )


def body(integrals, occupied, virtual, imask, omask, vmask, count):
    total = integrals.shape[1]
    members = lax.axis_size("blk")
    order = block_order(members)
    works_on = [order.index(d) for d in range(members)]

    rows = pl.pallas_call(
        functools.partial(pack_kernel, works_on),
        out_shape=jax.ShapeDtypeStruct((members, 3 * HALF, LANES), jnp.bfloat16),
        in_specs=[pl.BlockSpec(memory_space=pl.ANY)] * 2,
        out_specs=pl.BlockSpec(memory_space=pl.ANY),
        scratch_shapes=[
            pltpu.VMEM((3, total, EDGE * EDGE), jnp.bfloat16),
            pltpu.VMEM((3, total), jnp.int32),
            pltpu.VMEM((3, total * HALF, LANES), jnp.float32),
            pltpu.VMEM((members, 3 * HALF, LANES), jnp.bfloat16),
            pltpu.SemaphoreType.DMA((7,)),
        ],
        compiler_params=pltpu.CompilerParams(vmem_limit_bytes=63 * 1024 * 1024),
        name="pack",
    )(jnp.transpose(integrals[0], (1, 0, 2)), imask.T)
    greens = pl.pallas_call(
        functools.partial(prep_kernel, total),
        out_shape=jax.ShapeDtypeStruct((6 * HALF, LANES), jnp.bfloat16),
        in_specs=[SMEM] * 3 + [VMEM] * 2,
        out_specs=VMEM,
        scratch_shapes=[pltpu.VMEM((2, 3 * HALF, LANES), jnp.float32)],
        name="prep",
    )(omask.T, vmask.T, count, occupied[0], virtual[0])
    greens = lax.ppermute(greens, "blk", list(enumerate(order)))
    own = lax.all_to_all(rows, "blk", split_axis=0, concat_axis=0, tiled=True)
    forth = [(order[j], order[(j + 1) % members]) for j in range(members)]
    back = [(order[(j + 1) % members], order[j]) for j in range(members)]
    later = jnp.concatenate([own[:, HALF:].reshape(-1, LANES), greens[EDGE:]], 0)
    early = jnp.concatenate([own[:, : 2 * HALF].reshape(-1, LANES), greens[: 2 * EDGE]], 0)
    sprev = lax.ppermute(later, "blk", forth)
    snext = lax.ppermute(early, "blk", back)
    part = pl.pallas_call(
        functools.partial(main_kernel, 1.0 / math.sqrt(5 * EDGE * EDGE * total), members),
        out_shape=jax.ShapeDtypeStruct((members, members), jnp.float32),
        in_specs=[VMEM] * 4,
        out_specs=VMEM,
        scratch_shapes=[
            pltpu.VMEM((6 * EDGE, 3 * LANES), jnp.bfloat16),
            pltpu.VMEM((2, 2 * EDGE, LANES), jnp.bfloat16),
            pltpu.VMEM((members // 2 * EDGE, 5 * LANES), jnp.bfloat16),
            pltpu.VMEM((members, 5 * HALF, LANES), jnp.bfloat16),
        ],
        compiler_params=pltpu.CompilerParams(vmem_limit_bytes=48 * 1024 * 1024),
        name="products",
    )(sprev, own, greens, snext)
    mine = lax.all_to_all(part, "blk", split_axis=0, concat_axis=0, tiled=True)
    return jnp.sum(mine, axis=0, keepdims=True)


def solution(mesh):
    return jax.shard_map(
        body,
        mesh=mesh,
        in_specs=(
            P(("grp", "blk"), None, None, None),
            P(("grp", "blk"), None, None),
            P(("grp", "blk"), None, None),
            P(),
            P(),
            P(),
            P(),
        ),
        out_specs=P(("grp", "blk"), None),
        check_vma=False,
    )
```

```python
import functools
import math

import jax
import jax.numpy as jnp
from jax import lax
from jax.experimental import pallas as pl
from jax.experimental.pallas import tpu as pltpu
from jax.sharding import PartitionSpec as P

EDGE = 64
HALF = 32
LANES = 128
PITCH = 40
VMEM = pl.BlockSpec(memory_space=pltpu.VMEM)
SMEM = pl.BlockSpec(memory_space=pltpu.SMEM)


def block_order(count):
    if count == 16:
        chips = [3, 1, 0, 2, 4, 6, 7, 5]
        return [2 * chip + core for chip in chips for core in (0, 1)]
    return list(range(count))


def pack_kernel(works_on, x_hbm, imask_hbm, out_hbm, x_ref, imask_ref, rows_ref, out_ref, sems):
    blocks = x_ref.shape[1]
    copies = [pltpu.make_async_copy(x_hbm.at[a], x_ref.at[a], sems.at[a]) for a in range(3)]
    masks = pltpu.make_async_copy(imask_hbm, imask_ref, sems.at[3])
    masks.start()
    for copy in copies:
        copy.start()
    diagonal = lax.broadcasted_iota(jnp.int32, (blocks, blocks), 0) == lax.broadcasted_iota(
        jnp.int32, (blocks, blocks), 1
    )
    masks.wait()
    sent = []
    for a in range(3):
        mask = jnp.where(diagonal, imask_ref[pl.ds(a, 1), :].astype(jnp.float32), 0.0)
        mask = jnp.broadcast_to(jnp.sum(mask, axis=1, keepdims=True), (blocks, LANES))
        copies[a].wait()
        for c in range(HALF):
            rows_ref[a, pl.ds(c, blocks, stride=PITCH), :] = (
                x_ref[a, :, c * LANES : (c + 1) * LANES].astype(jnp.float32) * mask
            )
        part = pl.ds(a * HALF, HALF)
        for d, b in enumerate(works_on):
            out_ref[d, part, :] = rows_ref[a, pl.ds(b * PITCH, HALF), :].astype(jnp.bfloat16)
        sent.append(
            pltpu.make_async_copy(out_ref.at[:, part, :], out_hbm.at[:, part, :], sems.at[4 + a])
        )
        sent[a].start()
    for copy in sent:
        copy.wait()


def prep_kernel(total, omask, vmask, count, occ_ref, vir_ref, out_ref, rows_ref):
    own = lax.axis_index("blk")
    for k, ref in enumerate((occ_ref, vir_ref)):
        for c in range(HALF):
            rows_ref[k, pl.ds(c, 3, stride=PITCH), :] = ref[
                :, c * LANES : (c + 1) * LANES
            ].astype(jnp.float32)
    lane = lax.broadcasted_iota(jnp.int32, (HALF, LANES), 1)
    row = lax.broadcasted_iota(jnp.int32, (HALF, LANES), 0)
    left = lane < EDGE
    col = jnp.where(left, lane, lane - EDGE)
    keep = [(2 * row + par < count[own]).astype(jnp.float32) for par in range(2)]
    vir, occ = [], []
    for a in range(3):
        used = (col < count[lax.rem(own + (total + a - 1), total)]).astype(jnp.float32)
        v = rows_ref[1, pl.ds(a * PITCH, HALF), :] * (used * vmask[a, own].astype(jnp.float32))
        vir += [v * keep[0], pltpu.roll(v, EDGE, 1) * keep[1]]
        o = rows_ref[0, pl.ds(a * PITCH, HALF), :] * (used * omask[a, own].astype(jnp.float32))
        occ.append((pltpu.roll(o, EDGE, 1) * keep[0], o * keep[1]))
    vir += [jnp.zeros((HALF, LANES), jnp.float32)] * 2
    first = jnp.concatenate(vir[:4], 0).T[:EDGE]
    second = jnp.concatenate(vir[4:], 0).T[:EDGE]
    for a, turned in enumerate((first, pltpu.roll(first, EDGE, 1), second)):
        for par in range(2):
            out_ref[pl.ds((2 * a + par) * HALF, HALF), :] = jnp.where(
                left, turned[par * HALF : (par + 1) * HALF], occ[a][par]
            ).astype(jnp.bfloat16)


def main_kernel(
    scale, rows, sprev, sown, gown, snext, out_ref, occ_ref, far_ref, half_ref, full_ref
):
    pair = 2 * HALF

    def slab(s, q, a):
        if s == 0:
            return sprev[pl.ds(q * pair + (a - 1) * HALF, HALF), :]
        if s == 2:
            return snext[pl.ds(q * pair + a * HALF, HALF), :]
        return sown[q, pl.ds(a * HALF, HALF), :]

    def green(s, a):
        if s == 0:
            return sprev[pl.ds(rows * pair + (a - 1) * EDGE, EDGE), :]
        if s == 2:
            return snext[pl.ds(rows * pair + a * EDGE, EDGE), :]
        return gown[pl.ds(a * EDGE, EDGE), :]

    none = jnp.zeros((EDGE, EDGE), jnp.bfloat16)
    near = [green(0, 2)[:, :EDGE], green(1, 1)[:, :EDGE], green(2, 0)[:, :EDGE]]
    vir = [
        jnp.concatenate(
            [
                jnp.concatenate(near[:2], 1),
                jnp.concatenate([none, green(1, 2)[:, :EDGE]], 1),
            ],
            0,
        ),
        jnp.concatenate(near, 1),
        jnp.concatenate(
            [
                jnp.concatenate(near[1:], 1),
                jnp.concatenate([green(1, 0)[:, :EDGE], none], 1),
            ],
            0,
        ),
    ]
    used = ({0: 1, 1: 2}, {0: 0, 1: 1, 2: 2}, {1: 0, 2: 1})
    for s in range(3):
        for t in range(3):
            for half in range(2):
                at = pl.ds((half * 3 + s) * EDGE, EDGE)
                to = pl.ds(t * LANES, LANES)
                if t in used[s]:
                    o = green(s, used[s][t])[:, EDGE:]
                    occ_ref[at, to] = jnp.concatenate([none, o] if half else [o, none], 1)
                else:
                    occ_ref[at, to] = jnp.zeros((EDGE, LANES), jnp.bfloat16)
    for k in range(2):
        o = green(1, 2 * k)[:, EDGE:]
        far_ref[k] = jnp.concatenate(
            [jnp.concatenate([o, none], 1), jnp.concatenate([none, o], 1)], 0
        )

    members = (((0, 1), (1, 0)), ((0, 2), (1, 1), (2, 0)), ((1, 2), (2, 1)))
    for j in range(0, rows // 2, 2):

        def side(s, a):
            even, odd = [], []
            for k in range(j, j + 2):
                one, two = slab(s, 2 * k, a), slab(s, 2 * k + 1, a)
                even.append(jnp.concatenate([one[:, :EDGE], two[:, :EDGE]], 1))
                odd.append(jnp.concatenate([one[:, EDGE:], two[:, EDGE:]], 1))
            return [jnp.concatenate(even, 1), jnp.concatenate(odd, 1)]

        for t in range(3):
            parts = []
            for s, a in members[t]:
                parts += side(s, a)
            both = jnp.dot(vir[t], jnp.concatenate(parts, 0), preferred_element_type=jnp.float32)
            both = both.astype(jnp.bfloat16)
            for k in range(2):
                at = pl.ds((j + k) * EDGE, EDGE)
                piece = both[:, k * LANES : (k + 1) * LANES]
                half_ref[at, pl.ds(t * LANES, LANES)] = piece[:EDGE]
                if t != 1:
                    half_ref[at, pl.ds((3 + t // 2) * LANES, LANES)] = piece[EDGE:]

    left = lax.broadcasted_iota(jnp.int32, (HALF, LANES), 1) < EDGE
    for j in range(0, rows // 2, 4):
        at = pl.ds(j * EDGE, 4 * EDGE)
        nt = (((1,), (1,)), ((), ()))
        full = lax.dot_general(
            occ_ref[...], half_ref[at, pl.ds(0, 3 * LANES)], nt, preferred_element_type=jnp.float32
        )
        far = [
            lax.dot_general(
                far_ref[k],
                half_ref[at, pl.ds((3 + k) * LANES, LANES)],
                nt,
                preferred_element_type=jnp.float32,
            )
            for k in range(2)
        ]
        for half in range(2):
            for g in range(5):
                if g < 3:
                    block = full[(half * 3 + g) * EDGE : (half * 3 + g + 1) * EDGE]
                else:
                    block = far[g - 3][half * EDGE : (half + 1) * EDGE]
                for k in range(2):
                    even = block[:HALF, k * LANES : (k + 1) * LANES]
                    odd = block[HALF:, k * LANES : (k + 1) * LANES]
                    first = 2 * (j + 2 * k) + half
                    place = pl.ds(g * HALF, HALF)
                    full_ref[first, place, :] = jnp.where(
                        left, even, pltpu.roll(odd, EDGE, 1)
                    ).astype(jnp.bfloat16)
                    full_ref[first + 2, place, :] = jnp.where(
                        left, pltpu.roll(even, EDGE, 1), odd
                    ).astype(jnp.bfloat16)

    group = 16
    span = group * 16
    ri = lax.broadcasted_iota(jnp.int32, (span, span), 0)
    ci = lax.broadcasted_iota(jnp.int32, (span, span), 1)
    same = lax.rem(ri, 16) == lax.rem(ci, 16)
    pick = (
        lax.broadcasted_iota(jnp.int32, (span, group), 0) // 16
        == lax.broadcasted_iota(jnp.int32, (span, group), 1)
    ).astype(jnp.float32)
    for p in range(0, rows, group):
        for q in range(0, rows, group):
            acc = None
            for g, (s, a) in enumerate(((0, 2), (1, 1), (2, 0), (1, 2), (1, 0))):
                lhs = [slab(s, k, a) for k in range(p, p + group)]
                lhs = [jnp.concatenate([x[:16], x[16:]], 1) for x in lhs]
                rhs = [
                    full_ref[pl.ds(q, group), pl.ds(g * HALF + c * 16, 16), :].reshape(span, LANES)
                    for c in range(2)
                ]
                one = lax.dot_general(
                    jnp.concatenate(lhs, 0),
                    jnp.concatenate(rhs, 1),
                    (((1,), (1,)), ((), ())),
                    preferred_element_type=jnp.float32,
                )
                acc = one if acc is None else acc + one
            kept = jnp.where(same, acc, 0.0).reshape(group, 16, span)
            summed = jnp.sum(kept, axis=1)
            out_ref[pl.ds(p, group), pl.ds(q, group)] = scale * jnp.dot(
                summed, pick, preferred_element_type=jnp.float32, precision=lax.Precision.HIGHEST
            )


def body(integrals, occupied, virtual, imask, omask, vmask, count):
    total = integrals.shape[1]
    members = lax.axis_size("blk")
    order = block_order(members)
    works_on = [order.index(d) for d in range(members)]

    rows = pl.pallas_call(
        functools.partial(pack_kernel, works_on),
        out_shape=jax.ShapeDtypeStruct((members, 3 * HALF, LANES), jnp.bfloat16),
        in_specs=[pl.BlockSpec(memory_space=pl.ANY)] * 2,
        out_specs=pl.BlockSpec(memory_space=pl.ANY),
        scratch_shapes=[
            pltpu.VMEM((3, total, EDGE * EDGE), jnp.bfloat16),
            pltpu.VMEM((3, total), jnp.int32),
            pltpu.VMEM((3, total * PITCH, LANES), jnp.float32),
            pltpu.VMEM((members, 3 * HALF, LANES), jnp.bfloat16),
            pltpu.SemaphoreType.DMA((7,)),
        ],
        compiler_params=pltpu.CompilerParams(vmem_limit_bytes=63 * 1024 * 1024),
        name="pack",
    )(jnp.transpose(integrals[0], (1, 0, 2)), imask.T)
    greens = pl.pallas_call(
        functools.partial(prep_kernel, total),
        out_shape=jax.ShapeDtypeStruct((6 * HALF, LANES), jnp.bfloat16),
        in_specs=[SMEM] * 3 + [VMEM] * 2,
        out_specs=VMEM,
        scratch_shapes=[pltpu.VMEM((2, 3 * PITCH, LANES), jnp.float32)],
        name="prep",
    )(omask.T, vmask.T, count, occupied[0], virtual[0])
    greens = lax.ppermute(greens, "blk", list(enumerate(order)))
    own = lax.all_to_all(rows, "blk", split_axis=0, concat_axis=0, tiled=True)
    forth = [(order[j], order[(j + 1) % members]) for j in range(members)]
    back = [(order[(j + 1) % members], order[j]) for j in range(members)]
    later = jnp.concatenate([own[:, HALF:].reshape(-1, LANES), greens[EDGE:]], 0)
    early = jnp.concatenate([own[:, : 2 * HALF].reshape(-1, LANES), greens[: 2 * EDGE]], 0)
    sprev = lax.ppermute(later, "blk", forth)
    snext = lax.ppermute(early, "blk", back)
    part = pl.pallas_call(
        functools.partial(main_kernel, 1.0 / math.sqrt(5 * EDGE * EDGE * total), members),
        out_shape=jax.ShapeDtypeStruct((members, members), jnp.float32),
        in_specs=[VMEM] * 4,
        out_specs=VMEM,
        scratch_shapes=[
            pltpu.VMEM((6 * EDGE, 3 * LANES), jnp.bfloat16),
            pltpu.VMEM((2, 2 * EDGE, LANES), jnp.bfloat16),
            pltpu.VMEM((members // 2 * EDGE, 5 * LANES), jnp.bfloat16),
            pltpu.VMEM((members, 5 * HALF, LANES), jnp.bfloat16),
        ],
        compiler_params=pltpu.CompilerParams(vmem_limit_bytes=48 * 1024 * 1024),
        name="products",
    )(sprev, own, greens, snext)
    mine = lax.all_to_all(part, "blk", split_axis=0, concat_axis=0, tiled=True)
    return jnp.sum(mine, axis=0, keepdims=True)


def solution(mesh):
    return jax.shard_map(
        body,
        mesh=mesh,
        in_specs=(
            P(("grp", "blk"), None, None, None),
            P(("grp", "blk"), None, None),
            P(("grp", "blk"), None, None),
            P(),
            P(),
            P(),
            P(),
        ),
        out_specs=P(("grp", "blk"), None),
        check_vma=False,
    )
```

```python
import functools
import math

import jax
import jax.numpy as jnp
from jax import lax
from jax.experimental import pallas as pl
from jax.experimental.pallas import tpu as pltpu
from jax.sharding import PartitionSpec as P

EDGE = 64
HALF = 32
LANES = 128
PITCH = 40
VMEM = pl.BlockSpec(memory_space=pltpu.VMEM)
SMEM = pl.BlockSpec(memory_space=pltpu.SMEM)


def block_order(count):
    if count == 16:
        chips = [3, 1, 0, 2, 4, 6, 7, 5]
        return [2 * chip + core for chip in chips for core in (0, 1)]
    return list(range(count))


def pack_kernel(works_on, x_hbm, imask_hbm, out_hbm, x_ref, imask_ref, rows_ref, out_ref, sems):
    blocks = x_ref.shape[1]
    copies = [pltpu.make_async_copy(x_hbm.at[a], x_ref.at[a], sems.at[a]) for a in range(3)]
    masks = pltpu.make_async_copy(imask_hbm, imask_ref, sems.at[3])
    masks.start()
    for copy in copies:
        copy.start()
    diagonal = lax.broadcasted_iota(jnp.int32, (blocks, blocks), 0) == lax.broadcasted_iota(
        jnp.int32, (blocks, blocks), 1
    )
    masks.wait()
    sent = []
    for a in (1, 0, 2):
        mask = jnp.where(diagonal, imask_ref[pl.ds(a, 1), :].astype(jnp.float32), 0.0)
        mask = jnp.broadcast_to(jnp.sum(mask, axis=1, keepdims=True), (blocks, LANES))
        copies[a].wait()
        for c in range(HALF):
            rows_ref[a, pl.ds(c, blocks, stride=PITCH), :] = (
                x_ref[a, :, c * LANES : (c + 1) * LANES].astype(jnp.float32) * mask
            )
        for d, b in enumerate(works_on):
            to = 2 - a if b % 2 else a
            out_ref[d, pl.ds(to * HALF, HALF), :] = rows_ref[a, pl.ds(b * PITCH, HALF), :].astype(
                jnp.bfloat16
            )
        for to in {0: (), 1: (1,), 2: (0, 2)}[a]:
            part = pl.ds(to * HALF, HALF)
            copy = pltpu.make_async_copy(
                out_ref.at[:, part, :], out_hbm.at[:, part, :], sems.at[4 + to]
            )
            copy.start()
            sent.append(copy)
    for copy in sent:
        copy.wait()


def prep_kernel(total, omask, vmask, count, occ_ref, vir_ref, out_ref, rows_ref):
    own = lax.axis_index("blk")
    for k, ref in enumerate((occ_ref, vir_ref)):
        for c in range(HALF):
            rows_ref[k, pl.ds(c, 3, stride=PITCH), :] = ref[
                :, c * LANES : (c + 1) * LANES
            ].astype(jnp.float32)
    lane = lax.broadcasted_iota(jnp.int32, (HALF, LANES), 1)
    row = lax.broadcasted_iota(jnp.int32, (HALF, LANES), 0)
    left = lane < EDGE
    col = jnp.where(left, lane, lane - EDGE)
    keep = [(2 * row + par < count[own]).astype(jnp.float32) for par in range(2)]
    vir, occ = [], []
    for a in range(3):
        used = (col < count[lax.rem(own + (total + a - 1), total)]).astype(jnp.float32)
        v = rows_ref[1, pl.ds(a * PITCH, HALF), :] * (used * vmask[a, own].astype(jnp.float32))
        vir += [v * keep[0], pltpu.roll(v, EDGE, 1) * keep[1]]
        o = rows_ref[0, pl.ds(a * PITCH, HALF), :] * (used * omask[a, own].astype(jnp.float32))
        occ.append((pltpu.roll(o, EDGE, 1) * keep[0], o * keep[1]))
    vir += [jnp.zeros((HALF, LANES), jnp.float32)] * 2
    first = jnp.concatenate(vir[:4], 0).T[:EDGE]
    second = jnp.concatenate(vir[4:], 0).T[:EDGE]
    odd = lax.rem(own, 2)
    for a, turned in enumerate((first, pltpu.roll(first, EDGE, 1), second)):
        at = pl.multiple_of((a + odd * (2 - 2 * a)) * EDGE, EDGE)
        for par in range(2):
            out_ref[pl.ds(at + par * HALF, HALF), :] = jnp.where(
                left, turned[par * HALF : (par + 1) * HALF], occ[a][par]
            ).astype(jnp.bfloat16)


def main_kernel(
    scale, rows, schip, sown, gown, score, out_ref, occ_ref, far_ref, half_ref, full_ref
):
    pair = 2 * HALF

    def slab(s, q, a):
        if s == 0:
            return schip[pl.ds(q * pair + (2 - a) * HALF, HALF), :]
        if s == 2:
            return score[pl.ds(q * pair + (1 - a) * HALF, HALF), :]
        return sown[q, pl.ds(a * HALF, HALF), :]

    def green(s, a):
        if s == 0:
            return schip[pl.ds(rows * pair + (2 - a) * EDGE, EDGE), :]
        if s == 2:
            return score[pl.ds(rows * pair + (1 - a) * EDGE, EDGE), :]
        return gown[pl.ds(a * EDGE, EDGE), :]

    none = jnp.zeros((EDGE, EDGE), jnp.bfloat16)
    near = [green(0, 2)[:, :EDGE], green(1, 1)[:, :EDGE], green(2, 0)[:, :EDGE]]
    vir = [
        jnp.concatenate(
            [
                jnp.concatenate(near[:2], 1),
                jnp.concatenate([none, green(1, 2)[:, :EDGE]], 1),
            ],
            0,
        ),
        jnp.concatenate(near, 1),
        jnp.concatenate(
            [
                jnp.concatenate(near[1:], 1),
                jnp.concatenate([green(1, 0)[:, :EDGE], none], 1),
            ],
            0,
        ),
    ]
    used = ({0: 1, 1: 2}, {0: 0, 1: 1, 2: 2}, {1: 0, 2: 1})
    for s in range(3):
        for t in range(3):
            for half in range(2):
                at = pl.ds((half * 3 + s) * EDGE, EDGE)
                to = pl.ds(t * LANES, LANES)
                if t in used[s]:
                    o = green(s, used[s][t])[:, EDGE:]
                    occ_ref[at, to] = jnp.concatenate([none, o] if half else [o, none], 1)
                else:
                    occ_ref[at, to] = jnp.zeros((EDGE, LANES), jnp.bfloat16)
    for k in range(2):
        o = green(1, 2 * k)[:, EDGE:]
        far_ref[k] = jnp.concatenate(
            [jnp.concatenate([o, none], 1), jnp.concatenate([none, o], 1)], 0
        )

    members = (((0, 1), (1, 0)), ((0, 2), (1, 1), (2, 0)), ((1, 2), (2, 1)))
    for j in range(0, rows // 2, 2):

        def side(s, a):
            even, odd = [], []
            for k in range(j, j + 2):
                one, two = slab(s, 2 * k, a), slab(s, 2 * k + 1, a)
                even.append(jnp.concatenate([one[:, :EDGE], two[:, :EDGE]], 1))
                odd.append(jnp.concatenate([one[:, EDGE:], two[:, EDGE:]], 1))
            return [jnp.concatenate(even, 1), jnp.concatenate(odd, 1)]

        for t in range(3):
            parts = []
            for s, a in members[t]:
                parts += side(s, a)
            both = jnp.dot(vir[t], jnp.concatenate(parts, 0), preferred_element_type=jnp.float32)
            both = both.astype(jnp.bfloat16)
            for k in range(2):
                at = pl.ds((j + k) * EDGE, EDGE)
                piece = both[:, k * LANES : (k + 1) * LANES]
                half_ref[at, pl.ds(t * LANES, LANES)] = piece[:EDGE]
                if t != 1:
                    half_ref[at, pl.ds((3 + t // 2) * LANES, LANES)] = piece[EDGE:]

    left = lax.broadcasted_iota(jnp.int32, (HALF, LANES), 1) < EDGE
    for j in range(0, rows // 2, 4):
        at = pl.ds(j * EDGE, 4 * EDGE)
        nt = (((1,), (1,)), ((), ()))
        full = lax.dot_general(
            occ_ref[...], half_ref[at, pl.ds(0, 3 * LANES)], nt, preferred_element_type=jnp.float32
        )
        far = [
            lax.dot_general(
                far_ref[k],
                half_ref[at, pl.ds((3 + k) * LANES, LANES)],
                nt,
                preferred_element_type=jnp.float32,
            )
            for k in range(2)
        ]
        for half in range(2):
            for g in range(5):
                if g < 3:
                    block = full[(half * 3 + g) * EDGE : (half * 3 + g + 1) * EDGE]
                else:
                    block = far[g - 3][half * EDGE : (half + 1) * EDGE]
                for k in range(2):
                    even = block[:HALF, k * LANES : (k + 1) * LANES]
                    odd = block[HALF:, k * LANES : (k + 1) * LANES]
                    first = 2 * (j + 2 * k) + half
                    place = pl.ds(g * HALF, HALF)
                    full_ref[first, place, :] = jnp.where(
                        left, even, pltpu.roll(odd, EDGE, 1)
                    ).astype(jnp.bfloat16)
                    full_ref[first + 2, place, :] = jnp.where(
                        left, pltpu.roll(even, EDGE, 1), odd
                    ).astype(jnp.bfloat16)

    group = 16
    span = group * 16
    ri = lax.broadcasted_iota(jnp.int32, (span, span), 0)
    ci = lax.broadcasted_iota(jnp.int32, (span, span), 1)
    same = lax.rem(ri, 16) == lax.rem(ci, 16)
    pick = (
        lax.broadcasted_iota(jnp.int32, (span, group), 0) // 16
        == lax.broadcasted_iota(jnp.int32, (span, group), 1)
    ).astype(jnp.float32)
    for p in range(0, rows, group):
        for q in range(0, rows, group):
            acc = None
            for g, (s, a) in enumerate(((0, 2), (1, 1), (2, 0), (1, 2), (1, 0))):
                lhs = [slab(s, k, a) for k in range(p, p + group)]
                lhs = [jnp.concatenate([x[:16], x[16:]], 1) for x in lhs]
                rhs = [
                    full_ref[pl.ds(q, group), pl.ds(g * HALF + c * 16, 16), :].reshape(span, LANES)
                    for c in range(2)
                ]
                one = lax.dot_general(
                    jnp.concatenate(lhs, 0),
                    jnp.concatenate(rhs, 1),
                    (((1,), (1,)), ((), ())),
                    preferred_element_type=jnp.float32,
                )
                acc = one if acc is None else acc + one
            kept = jnp.where(same, acc, 0.0).reshape(group, 16, span)
            summed = jnp.sum(kept, axis=1)
            out_ref[pl.ds(p, group), pl.ds(q, group)] = scale * jnp.dot(
                summed, pick, preferred_element_type=jnp.float32, precision=lax.Precision.HIGHEST
            )


def body(integrals, occupied, virtual, imask, omask, vmask, count):
    total = integrals.shape[1]
    members = lax.axis_size("blk")
    order = block_order(members)
    works_on = [order.index(d) for d in range(members)]

    rows = pl.pallas_call(
        functools.partial(pack_kernel, works_on),
        out_shape=jax.ShapeDtypeStruct((members, 3 * HALF, LANES), jnp.bfloat16),
        in_specs=[pl.BlockSpec(memory_space=pl.ANY)] * 2,
        out_specs=pl.BlockSpec(memory_space=pl.ANY),
        scratch_shapes=[
            pltpu.VMEM((3, total, EDGE * EDGE), jnp.bfloat16),
            pltpu.VMEM((3, total), jnp.int32),
            pltpu.VMEM((3, total * PITCH, LANES), jnp.float32),
            pltpu.VMEM((members, 3 * HALF, LANES), jnp.bfloat16),
            pltpu.SemaphoreType.DMA((7,)),
        ],
        compiler_params=pltpu.CompilerParams(vmem_limit_bytes=63 * 1024 * 1024),
        name="pack",
    )(jnp.transpose(integrals[0], (1, 0, 2)), imask.T)
    greens = pl.pallas_call(
        functools.partial(prep_kernel, total),
        out_shape=jax.ShapeDtypeStruct((6 * HALF, LANES), jnp.bfloat16),
        in_specs=[SMEM] * 3 + [VMEM] * 2,
        out_specs=VMEM,
        scratch_shapes=[pltpu.VMEM((2, 3 * PITCH, LANES), jnp.float32)],
        name="prep",
    )(omask.T, vmask.T, count, occupied[0], virtual[0])
    greens = lax.ppermute(greens, "blk", list(enumerate(order)))
    own = lax.all_to_all(rows, "blk", split_axis=0, concat_axis=0, tiled=True)
    core_pairs = [(order[j], order[j + 1 - 2 * (j % 2)]) for j in range(members)]
    chip_pairs = [(order[j], order[(j - 1 + 2 * (j % 2)) % members]) for j in range(members)]
    to_chip = jnp.concatenate([own[:, : 2 * HALF].reshape(-1, LANES), greens[: 2 * EDGE]], 0)
    to_core = jnp.concatenate([own[:, HALF:].reshape(-1, LANES), greens[EDGE:]], 0)
    schip = lax.ppermute(to_chip, "blk", chip_pairs)
    score = lax.ppermute(to_core, "blk", core_pairs)
    part = pl.pallas_call(
        functools.partial(main_kernel, 1.0 / math.sqrt(5 * EDGE * EDGE * total), members),
        out_shape=jax.ShapeDtypeStruct((members, members), jnp.float32),
        in_specs=[VMEM] * 4,
        out_specs=VMEM,
        scratch_shapes=[
            pltpu.VMEM((6 * EDGE, 3 * LANES), jnp.bfloat16),
            pltpu.VMEM((2, 2 * EDGE, LANES), jnp.bfloat16),
            pltpu.VMEM((members // 2 * EDGE, 5 * LANES), jnp.bfloat16),
            pltpu.VMEM((members, 5 * HALF, LANES), jnp.bfloat16),
        ],
        compiler_params=pltpu.CompilerParams(vmem_limit_bytes=48 * 1024 * 1024),
        name="products",
    )(schip, own, greens, score)
    mine = lax.all_to_all(part, "blk", split_axis=0, concat_axis=0, tiled=True)
    return jnp.sum(mine, axis=0, keepdims=True)


def solution(mesh):
    return jax.shard_map(
        body,
        mesh=mesh,
        in_specs=(
            P(("grp", "blk"), None, None, None),
            P(("grp", "blk"), None, None),
            P(("grp", "blk"), None, None),
            P(),
            P(),
            P(),
            P(),
        ),
        out_specs=P(("grp", "blk"), None),
        check_vma=False,
    )
```

```python
import functools
import math

import jax
import jax.numpy as jnp
from jax import lax
from jax.experimental import pallas as pl
from jax.experimental.pallas import tpu as pltpu
from jax.sharding import PartitionSpec as P

EDGE = 64
HALF = 32
LANES = 128
PITCH = 40
VMEM = pl.BlockSpec(memory_space=pltpu.VMEM)
SMEM = pl.BlockSpec(memory_space=pltpu.SMEM)
NT = (((1,), (1,)), ((), ()))


def block_order(count):
    if count == 16:
        chips = [3, 1, 0, 2, 4, 6, 7, 5]
        return [2 * chip + core for chip in chips for core in (0, 1)]
    return list(range(count))


def pack_kernel(works_on, x_hbm, imask_hbm, out_hbm, x_ref, imask_ref, rows_ref, out_ref, sems):
    blocks = x_ref.shape[1]
    copies = [pltpu.make_async_copy(x_hbm.at[a], x_ref.at[a], sems.at[a]) for a in range(3)]
    masks = pltpu.make_async_copy(imask_hbm, imask_ref, sems.at[3])
    masks.start()
    for copy in copies:
        copy.start()
    diagonal = lax.broadcasted_iota(jnp.int32, (blocks, blocks), 0) == lax.broadcasted_iota(
        jnp.int32, (blocks, blocks), 1
    )
    masks.wait()
    sent = []
    for a in (1, 0, 2):
        mask = jnp.where(diagonal, imask_ref[pl.ds(a, 1), :].astype(jnp.float32), 0.0)
        mask = jnp.broadcast_to(jnp.sum(mask, axis=1, keepdims=True), (blocks, LANES))
        copies[a].wait()
        for c in range(HALF):
            rows_ref[a, pl.ds(c, blocks, stride=PITCH), :] = (
                x_ref[a, :, c * LANES : (c + 1) * LANES].astype(jnp.float32) * mask
            )
        for d, b in enumerate(works_on):
            to = 2 - a if b % 2 else a
            out_ref[d, pl.ds(to * HALF, HALF), :] = rows_ref[a, pl.ds(b * PITCH, HALF), :].astype(
                jnp.bfloat16
            )
        for to in {0: (), 1: (1,), 2: (0, 2)}[a]:
            part = pl.ds(to * HALF, HALF)
            copy = pltpu.make_async_copy(
                out_ref.at[:, part, :], out_hbm.at[:, part, :], sems.at[4 + to]
            )
            copy.start()
            sent.append(copy)
    for copy in sent:
        copy.wait()


def prep_kernel(total, omask, vmask, count, occ_ref, vir_ref, out_ref, rows_ref):
    own = lax.axis_index("blk")
    for k, ref in enumerate((occ_ref, vir_ref)):
        for c in range(HALF):
            rows_ref[k, pl.ds(c, 3, stride=PITCH), :] = ref[
                :, c * LANES : (c + 1) * LANES
            ].astype(jnp.float32)
    lane = lax.broadcasted_iota(jnp.int32, (HALF, LANES), 1)
    row = lax.broadcasted_iota(jnp.int32, (HALF, LANES), 0)
    left = lane < EDGE
    col = jnp.where(left, lane, lane - EDGE)
    keep = [(2 * row + par < count[own]).astype(jnp.float32) for par in range(2)]
    vir, occ = [], []
    for a in range(3):
        used = (col < count[lax.rem(own + (total + a - 1), total)]).astype(jnp.float32)
        v = rows_ref[1, pl.ds(a * PITCH, HALF), :] * (used * vmask[a, own].astype(jnp.float32))
        vir += [v * keep[0], pltpu.roll(v, EDGE, 1) * keep[1]]
        o = rows_ref[0, pl.ds(a * PITCH, HALF), :] * (used * omask[a, own].astype(jnp.float32))
        occ.append((pltpu.roll(o, EDGE, 1) * keep[0], o * keep[1]))
    vir += [jnp.zeros((HALF, LANES), jnp.float32)] * 2
    first = jnp.concatenate(vir[:4], 0).T[:EDGE]
    second = jnp.concatenate(vir[4:], 0).T[:EDGE]
    odd = lax.rem(own, 2)
    for a, turned in enumerate((first, pltpu.roll(first, EDGE, 1), second)):
        at = pl.multiple_of((a + odd * (2 - 2 * a)) * EDGE, EDGE)
        for par in range(2):
            out_ref[pl.ds(at + par * HALF, HALF), :] = jnp.where(
                left, turned[par * HALF : (par + 1) * HALF], occ[a][par]
            ).astype(jnp.bfloat16)


def halves(slab, rows_at, j):
    even, odd = [], []
    for k in range(j, j + 2):
        one, two = slab(2 * k, *rows_at), slab(2 * k + 1, *rows_at)
        even.append(jnp.concatenate([one[:, :EDGE], two[:, :EDGE]], 1))
        odd.append(jnp.concatenate([one[:, EDGE:], two[:, EDGE:]], 1))
    return [jnp.concatenate(even, 1), jnp.concatenate(odd, 1)]


def unfold(block, j, g, half, full_ref):
    left = lax.broadcasted_iota(jnp.int32, (HALF, LANES), 1) < EDGE
    place = pl.ds(g * HALF, HALF)
    for k in range(2):
        even = block[:HALF, k * LANES : (k + 1) * LANES]
        odd = block[HALF:, k * LANES : (k + 1) * LANES]
        first = 2 * (j + 2 * k) + half
        full_ref[first, place, :] = jnp.where(left, even, pltpu.roll(odd, EDGE, 1)).astype(
            jnp.bfloat16
        )
        full_ref[first + 2, place, :] = jnp.where(left, pltpu.roll(even, EDGE, 1), odd).astype(
            jnp.bfloat16
        )


def inner(slabs, full_ref, rows, store):
    group = 16
    span = group * 16
    ri = lax.broadcasted_iota(jnp.int32, (span, span), 0)
    ci = lax.broadcasted_iota(jnp.int32, (span, span), 1)
    same = lax.rem(ri, 16) == lax.rem(ci, 16)
    pick = (
        lax.broadcasted_iota(jnp.int32, (span, group), 0) // 16
        == lax.broadcasted_iota(jnp.int32, (span, group), 1)
    ).astype(jnp.float32)
    for p in range(0, rows, group):
        for q in range(0, rows, group):
            acc = None
            for g, slab in enumerate(slabs):
                lhs = [slab(k) for k in range(p, p + group)]
                lhs = [jnp.concatenate([x[:16], x[16:]], 1) for x in lhs]
                rhs = [
                    full_ref[pl.ds(q, group), pl.ds(g * HALF + c * 16, 16), :].reshape(span, LANES)
                    for c in range(2)
                ]
                one = lax.dot_general(
                    jnp.concatenate(lhs, 0),
                    jnp.concatenate(rhs, 1),
                    NT,
                    preferred_element_type=jnp.float32,
                )
                acc = one if acc is None else acc + one
            kept = jnp.where(same, acc, 0.0).reshape(group, 16, span)
            store(
                pl.ds(p, group),
                pl.ds(q, group),
                jnp.dot(
                    jnp.sum(kept, axis=1),
                    pick,
                    preferred_element_type=jnp.float32,
                    precision=lax.Precision.HIGHEST,
                ),
            )


def readers(rows, schip, sown, gown, score):
    pair = 2 * HALF

    def slab(q, s, a):
        if s == 0:
            return schip[pl.ds(q * pair + (2 - a) * HALF, HALF), :]
        if s == 2:
            return score[pl.ds(q * pair + (1 - a) * HALF, HALF), :]
        return sown[q, pl.ds(a * HALF, HALF), :]

    def green(s, a):
        if s == 0:
            return schip[pl.ds(rows * pair + (2 - a) * EDGE, EDGE), :]
        if s == 2:
            return score[pl.ds(rows * pair + (1 - a) * EDGE, EDGE), :]
        return gown[pl.ds(a * EDGE, EDGE), :]

    return slab, green


def early_kernel(rows, sown, gown, score, part_ref, right_ref, far_ref, half_ref, full_ref):
    slab, green = readers(rows, None, sown, gown, score)
    none = jnp.zeros((EDGE, EDGE), jnp.bfloat16)
    for k in range(2):
        o = green(1, 2 * k)[:, EDGE:]
        far_ref[k] = jnp.concatenate(
            [jnp.concatenate([o, none], 1), jnp.concatenate([none, o], 1)], 0
        )
    vir = jnp.concatenate(
        [
            jnp.concatenate([green(1, 1)[:, :EDGE], green(2, 0)[:, :EDGE]], 1),
            jnp.concatenate([green(1, 0)[:, :EDGE], none], 1),
        ],
        0,
    )
    for j in range(0, rows // 2, 2):
        low = jnp.dot(
            green(1, 2)[:, :EDGE],
            jnp.concatenate(halves(slab, (1, 0), j), 0),
            preferred_element_type=jnp.float32,
        ).astype(jnp.bfloat16)
        high = jnp.dot(
            vir,
            jnp.concatenate(halves(slab, (1, 2), j) + halves(slab, (2, 1), j), 0),
            preferred_element_type=jnp.float32,
        ).astype(jnp.bfloat16)
        for k in range(2):
            at = pl.ds((j + k) * EDGE, EDGE)
            lanes = slice(k * LANES, (k + 1) * LANES)
            right_ref[at, :] = high[:EDGE, lanes]
            half_ref[0, at, :] = low[:, lanes]
            half_ref[1, at, :] = high[EDGE:, lanes]
    for j in range(0, rows // 2, 4):
        for k in range(2):
            full = lax.dot_general(
                far_ref[k],
                half_ref[k, pl.ds(j * EDGE, 4 * EDGE), :],
                NT,
                preferred_element_type=jnp.float32,
            )
            for half in range(2):
                unfold(full[half * EDGE : (half + 1) * EDGE], j, k, half, full_ref)

    def store(p, q, sums):
        part_ref[p, q] = sums

    inner([lambda q: slab(q, 1, 2), lambda q: slab(q, 1, 0)], full_ref, rows, store)


def main_kernel(
    scale, rows, part_ref, right_ref, schip, sown, gown, score, out_ref, occ_ref, half_ref, full_ref
):
    slab, green = readers(rows, schip, sown, gown, score)
    none = jnp.zeros((EDGE, EDGE), jnp.bfloat16)
    near = [green(s, 2 - s)[:, :EDGE] for s in range(3)]
    vir = [jnp.concatenate(near[:2], 1), jnp.concatenate(near, 1)]
    used = ({0: 1, 1: 2}, {0: 0, 1: 1, 2: 2}, {1: 0, 2: 1})
    for s in range(3):
        for t in range(3):
            for half in range(2):
                at = pl.ds((half * 3 + s) * EDGE, EDGE)
                to = pl.ds(t * LANES, LANES)
                if t in used[s]:
                    o = green(s, used[s][t])[:, EDGE:]
                    occ_ref[at, to] = jnp.concatenate([none, o] if half else [o, none], 1)
                else:
                    occ_ref[at, to] = jnp.zeros((EDGE, LANES), jnp.bfloat16)

    members = (((0, 1), (1, 0)), ((0, 2), (1, 1), (2, 0)))
    for j in range(0, rows // 2, 2):
        for t in range(2):
            parts = []
            for at in members[t]:
                parts += halves(slab, at, j)
            both = jnp.dot(vir[t], jnp.concatenate(parts, 0), preferred_element_type=jnp.float32)
            both = both.astype(jnp.bfloat16)
            for k in range(2):
                half_ref[pl.ds((j + k) * EDGE, EDGE), pl.ds(t * LANES, LANES)] = both[
                    :, k * LANES : (k + 1) * LANES
                ]

    for j in range(0, rows // 2, 4):
        at = pl.ds(j * EDGE, 4 * EDGE)
        full = lax.dot_general(
            occ_ref[...],
            jnp.concatenate([half_ref[at, :], right_ref[at, :]], 1),
            NT,
            preferred_element_type=jnp.float32,
        )
        for half in range(2):
            for s in range(3):
                block = full[(half * 3 + s) * EDGE : (half * 3 + s + 1) * EDGE]
                unfold(block, j, s, half, full_ref)

    def store(p, q, sums):
        out_ref[p, q] = scale * (sums + part_ref[p, q])

    inner([lambda q, s=s: slab(q, s, 2 - s) for s in range(3)], full_ref, rows, store)


def body(integrals, occupied, virtual, imask, omask, vmask, count):
    total = integrals.shape[1]
    members = lax.axis_size("blk")
    order = block_order(members)
    works_on = [order.index(d) for d in range(members)]

    rows = pl.pallas_call(
        functools.partial(pack_kernel, works_on),
        out_shape=jax.ShapeDtypeStruct((members, 3 * HALF, LANES), jnp.bfloat16),
        in_specs=[pl.BlockSpec(memory_space=pl.ANY)] * 2,
        out_specs=pl.BlockSpec(memory_space=pl.ANY),
        scratch_shapes=[
            pltpu.VMEM((3, total, EDGE * EDGE), jnp.bfloat16),
            pltpu.VMEM((3, total), jnp.int32),
            pltpu.VMEM((3, total * PITCH, LANES), jnp.float32),
            pltpu.VMEM((members, 3 * HALF, LANES), jnp.bfloat16),
            pltpu.SemaphoreType.DMA((7,)),
        ],
        compiler_params=pltpu.CompilerParams(vmem_limit_bytes=63 * 1024 * 1024),
        name="pack",
    )(jnp.transpose(integrals[0], (1, 0, 2)), imask.T)
    greens = pl.pallas_call(
        functools.partial(prep_kernel, total),
        out_shape=jax.ShapeDtypeStruct((6 * HALF, LANES), jnp.bfloat16),
        in_specs=[SMEM] * 3 + [VMEM] * 2,
        out_specs=VMEM,
        scratch_shapes=[pltpu.VMEM((2, 3 * PITCH, LANES), jnp.float32)],
        name="prep",
    )(omask.T, vmask.T, count, occupied[0], virtual[0])
    greens = lax.ppermute(greens, "blk", list(enumerate(order)))
    own = lax.all_to_all(rows, "blk", split_axis=0, concat_axis=0, tiled=True)
    core_pairs = [(order[j], order[j + 1 - 2 * (j % 2)]) for j in range(members)]
    chip_pairs = [(order[j], order[(j - 1 + 2 * (j % 2)) % members]) for j in range(members)]
    to_chip = jnp.concatenate([own[:, : 2 * HALF].reshape(-1, LANES), greens[: 2 * EDGE]], 0)
    to_core = jnp.concatenate([own[:, HALF:].reshape(-1, LANES), greens[EDGE:]], 0)
    schip = lax.ppermute(to_chip, "blk", chip_pairs)
    score = lax.ppermute(to_core, "blk", core_pairs)
    early, right = pl.pallas_call(
        functools.partial(early_kernel, members),
        out_shape=(
            jax.ShapeDtypeStruct((members, members), jnp.float32),
            jax.ShapeDtypeStruct((members // 2 * EDGE, LANES), jnp.bfloat16),
        ),
        in_specs=[VMEM] * 3,
        out_specs=(VMEM, VMEM),
        scratch_shapes=[
            pltpu.VMEM((2, 2 * EDGE, LANES), jnp.bfloat16),
            pltpu.VMEM((2, members // 2 * EDGE, LANES), jnp.bfloat16),
            pltpu.VMEM((members, 2 * HALF, LANES), jnp.bfloat16),
        ],
        compiler_params=pltpu.CompilerParams(vmem_limit_bytes=24 * 1024 * 1024),
        name="early",
    )(own, greens, score)
    part = pl.pallas_call(
        functools.partial(main_kernel, 1.0 / math.sqrt(5 * EDGE * EDGE * total), members),
        out_shape=jax.ShapeDtypeStruct((members, members), jnp.float32),
        in_specs=[VMEM] * 6,
        out_specs=VMEM,
        scratch_shapes=[
            pltpu.VMEM((6 * EDGE, 3 * LANES), jnp.bfloat16),
            pltpu.VMEM((members // 2 * EDGE, 2 * LANES), jnp.bfloat16),
            pltpu.VMEM((members, 3 * HALF, LANES), jnp.bfloat16),
        ],
        compiler_params=pltpu.CompilerParams(vmem_limit_bytes=24 * 1024 * 1024),
        name="products",
    )(early, right, schip, own, greens, score)
    mine = lax.all_to_all(part, "blk", split_axis=0, concat_axis=0, tiled=True)
    return jnp.sum(mine, axis=0, keepdims=True)


def solution(mesh):
    return jax.shard_map(
        body,
        mesh=mesh,
        in_specs=(
            P(("grp", "blk"), None, None, None),
            P(("grp", "blk"), None, None),
            P(("grp", "blk"), None, None),
            P(),
            P(),
            P(),
            P(),
        ),
        out_specs=P(("grp", "blk"), None),
        check_vma=False,
    )
```

```python
import functools
import math

import jax
import jax.numpy as jnp
from jax import lax
from jax.experimental import pallas as pl
from jax.experimental.pallas import tpu as pltpu
from jax.sharding import PartitionSpec as P

EDGE = 64
HALF = 32
LANES = 128
PITCH = 40
VMEM = pl.BlockSpec(memory_space=pltpu.VMEM)
SMEM = pl.BlockSpec(memory_space=pltpu.SMEM)
NT = (((1,), (1,)), ((), ()))


def block_order(count):
    if count == 16:
        chips = [3, 1, 0, 2, 4, 6, 7, 5]
        return [2 * chip + core for chip in chips for core in (0, 1)]
    return list(range(count))


def pack_kernel(works_on, x_hbm, imask_hbm, out_hbm, x_ref, imask_ref, rows_ref, out_ref, sems):
    blocks = x_ref.shape[1]
    copies = [pltpu.make_async_copy(x_hbm.at[a], x_ref.at[a], sems.at[a]) for a in range(3)]
    masks = pltpu.make_async_copy(imask_hbm, imask_ref, sems.at[3])
    masks.start()
    for copy in copies:
        copy.start()
    diagonal = lax.broadcasted_iota(jnp.int32, (blocks, blocks), 0) == lax.broadcasted_iota(
        jnp.int32, (blocks, blocks), 1
    )
    masks.wait()
    sent = []
    for a in (1, 0, 2):
        mask = jnp.where(diagonal, imask_ref[pl.ds(a, 1), :].astype(jnp.float32), 0.0)
        mask = jnp.broadcast_to(jnp.sum(mask, axis=1, keepdims=True), (blocks, LANES))
        copies[a].wait()
        for c in range(HALF):
            rows_ref[a, pl.ds(c, blocks, stride=PITCH), :] = (
                x_ref[a, :, c * LANES : (c + 1) * LANES].astype(jnp.float32) * mask
            )
        for d, b in enumerate(works_on):
            to = 2 - a if b % 2 else a
            out_ref[d, pl.ds(to * HALF, HALF), :] = rows_ref[a, pl.ds(b * PITCH, HALF), :].astype(
                jnp.bfloat16
            )
        for to in {0: (), 1: (1,), 2: (0, 2)}[a]:
            part = pl.ds(to * HALF, HALF)
            copy = pltpu.make_async_copy(
                out_ref.at[:, part, :], out_hbm.at[:, part, :], sems.at[4 + to]
            )
            copy.start()
            sent.append(copy)
    for copy in sent:
        copy.wait()


def prep_kernel(total, omask, vmask, count, occ_ref, vir_ref, out_ref, rows_ref):
    own = lax.axis_index("blk")
    for k, ref in enumerate((occ_ref, vir_ref)):
        for c in range(HALF):
            rows_ref[k, pl.ds(c, 3, stride=PITCH), :] = ref[
                :, c * LANES : (c + 1) * LANES
            ].astype(jnp.float32)
    lane = lax.broadcasted_iota(jnp.int32, (HALF, LANES), 1)
    row = lax.broadcasted_iota(jnp.int32, (HALF, LANES), 0)
    left = lane < EDGE
    col = jnp.where(left, lane, lane - EDGE)
    keep = [(2 * row + par < count[own]).astype(jnp.float32) for par in range(2)]
    vir, occ = [], []
    for a in range(3):
        used = (col < count[lax.rem(own + (total + a - 1), total)]).astype(jnp.float32)
        v = rows_ref[1, pl.ds(a * PITCH, HALF), :] * (used * vmask[a, own].astype(jnp.float32))
        vir += [v * keep[0], pltpu.roll(v, EDGE, 1) * keep[1]]
        o = rows_ref[0, pl.ds(a * PITCH, HALF), :] * (used * omask[a, own].astype(jnp.float32))
        occ.append((pltpu.roll(o, EDGE, 1) * keep[0], o * keep[1]))
    vir += [jnp.zeros((HALF, LANES), jnp.float32)] * 2
    first = jnp.concatenate(vir[:4], 0).T[:EDGE]
    second = jnp.concatenate(vir[4:], 0).T[:EDGE]
    odd = lax.rem(own, 2)
    for a, turned in enumerate((first, pltpu.roll(first, EDGE, 1), second)):
        at = pl.multiple_of((a + odd * (2 - 2 * a)) * EDGE, EDGE)
        for par in range(2):
            out_ref[pl.ds(at + par * HALF, HALF), :] = jnp.where(
                left, turned[par * HALF : (par + 1) * HALF], occ[a][par]
            ).astype(jnp.bfloat16)


def halves(slab, rows_at, j):
    even, odd = [], []
    for k in range(j, j + 2):
        one, two = slab(2 * k, *rows_at), slab(2 * k + 1, *rows_at)
        even.append(jnp.concatenate([one[:, :EDGE], two[:, :EDGE]], 1))
        odd.append(jnp.concatenate([one[:, EDGE:], two[:, EDGE:]], 1))
    return [jnp.concatenate(even, 1), jnp.concatenate(odd, 1)]


def unfold(block, j, g, half, full_ref):
    left = lax.broadcasted_iota(jnp.int32, (HALF, LANES), 1) < EDGE
    place = pl.ds(g * HALF, HALF)
    for k in range(2):
        even = block[:HALF, k * LANES : (k + 1) * LANES]
        odd = block[HALF:, k * LANES : (k + 1) * LANES]
        first = 2 * (j + 2 * k) + half
        full_ref[first, place, :] = jnp.where(left, even, pltpu.roll(odd, EDGE, 1)).astype(
            jnp.bfloat16
        )
        full_ref[first + 2, place, :] = jnp.where(left, pltpu.roll(even, EDGE, 1), odd).astype(
            jnp.bfloat16
        )


def inner(slabs, full_ref, rows, store):
    group = 16
    span = group * 16
    ri = lax.broadcasted_iota(jnp.int32, (span, span), 0)
    ci = lax.broadcasted_iota(jnp.int32, (span, span), 1)
    same = lax.rem(ri, 16) == lax.rem(ci, 16)
    pick = (
        lax.broadcasted_iota(jnp.int32, (span, group), 0) // 16
        == lax.broadcasted_iota(jnp.int32, (span, group), 1)
    ).astype(jnp.float32)
    for p in range(0, rows, group):
        for q in range(0, rows, group):
            acc = None
            for g, slab in enumerate(slabs):
                lhs = [slab(k) for k in range(p, p + group)]
                lhs = [jnp.concatenate([x[:16], x[16:]], 1) for x in lhs]
                rhs = [
                    full_ref[pl.ds(q, group), pl.ds(g * HALF + c * 16, 16), :].reshape(span, LANES)
                    for c in range(2)
                ]
                one = lax.dot_general(
                    jnp.concatenate(lhs, 0),
                    jnp.concatenate(rhs, 1),
                    NT,
                    preferred_element_type=jnp.float32,
                )
                acc = one if acc is None else acc + one
            kept = jnp.where(same, acc, 0.0).reshape(group, 16, span)
            store(
                pl.ds(p, group),
                pl.ds(q, group),
                jnp.dot(
                    jnp.sum(kept, axis=1),
                    pick,
                    preferred_element_type=jnp.float32,
                    precision=lax.Precision.HIGHEST,
                ),
            )


def readers(rows, schip, sown, gown, score):
    pair = 2 * HALF

    def slab(q, s, a):
        if s == 0:
            return schip[pl.ds(q * pair + (2 - a) * HALF, HALF), :]
        if s == 2:
            return score[pl.ds(q * pair + (1 - a) * HALF, HALF), :]
        return sown[q, pl.ds(a * HALF, HALF), :]

    def green(s, a):
        if s == 0:
            return schip[pl.ds(rows * pair + (2 - a) * EDGE, EDGE), :]
        if s == 2:
            return score[pl.ds(rows * pair + (1 - a) * EDGE, EDGE), :]
        return gown[pl.ds(a * EDGE, EDGE), :]

    return slab, green


def early_kernel(rows, sown, gown, part_ref, sides_ref, far_ref, half_ref, full_ref):
    slab, green = readers(rows, None, sown, gown, None)
    none = jnp.zeros((EDGE, EDGE), jnp.bfloat16)
    for k in range(2):
        o = green(1, 2 * k)[:, EDGE:]
        far_ref[k] = jnp.concatenate(
            [jnp.concatenate([o, none], 1), jnp.concatenate([none, o], 1)], 0
        )
    for j in range(0, rows // 2, 2):
        for a in range(3):
            side = jnp.concatenate(halves(slab, (1, a), j), 0)
            sides_ref[a, :, pl.ds(j * LANES, 2 * LANES)] = side
            if a == 1:
                continue
            both = jnp.dot(
                green(1, 2 - a)[:, :EDGE], side, preferred_element_type=jnp.float32
            ).astype(jnp.bfloat16)
            for k in range(2):
                half_ref[a // 2, pl.ds((j + k) * EDGE, EDGE), :] = both[
                    :, k * LANES : (k + 1) * LANES
                ]
    for j in range(0, rows // 2, 4):
        for k in range(2):
            full = lax.dot_general(
                far_ref[k],
                half_ref[k, pl.ds(j * EDGE, 4 * EDGE), :],
                NT,
                preferred_element_type=jnp.float32,
            )
            for half in range(2):
                unfold(full[half * EDGE : (half + 1) * EDGE], j, k, half, full_ref)

    def store(p, q, sums):
        part_ref[p, q] = sums

    inner([lambda q: slab(q, 1, 2), lambda q: slab(q, 1, 0)], full_ref, rows, store)


def main_kernel(
    scale, rows, part_ref, sides_ref, schip, sown, gown, score, out_ref, occ_ref, half_ref, full_ref
):
    slab, green = readers(rows, schip, sown, gown, score)
    none = jnp.zeros((EDGE, EDGE), jnp.bfloat16)
    near = [green(s, 2 - s)[:, :EDGE] for s in range(3)]
    vir = [jnp.concatenate(x, 1) for x in (near[:2], near, near[1:])]
    used = ({0: 1, 1: 2}, {0: 0, 1: 1, 2: 2}, {1: 0, 2: 1})
    for s in range(3):
        for t in range(3):
            for half in range(2):
                at = pl.ds((half * 3 + s) * EDGE, EDGE)
                to = pl.ds(t * LANES, LANES)
                if t in used[s]:
                    o = green(s, used[s][t])[:, EDGE:]
                    occ_ref[at, to] = jnp.concatenate([none, o] if half else [o, none], 1)
                else:
                    occ_ref[at, to] = jnp.zeros((EDGE, LANES), jnp.bfloat16)

    members = (((0, 1), (1, 0)), ((0, 2), (1, 1), (2, 0)), ((1, 2), (2, 1)))
    for j in range(0, rows // 2, 2):
        for t in range(3):
            parts = []
            for s, a in members[t]:
                if s == 1:
                    parts.append(sides_ref[a, :, pl.ds(j * LANES, 2 * LANES)])
                else:
                    parts += halves(slab, (s, a), j)
            both = jnp.dot(vir[t], jnp.concatenate(parts, 0), preferred_element_type=jnp.float32)
            both = both.astype(jnp.bfloat16)
            for k in range(2):
                half_ref[pl.ds((j + k) * EDGE, EDGE), pl.ds(t * LANES, LANES)] = both[
                    :, k * LANES : (k + 1) * LANES
                ]

    for j in range(0, rows // 2, 4):
        at = pl.ds(j * EDGE, 4 * EDGE)
        full = lax.dot_general(
            occ_ref[...],
            half_ref[at, :],
            NT,
            preferred_element_type=jnp.float32,
        )
        for half in range(2):
            for s in range(3):
                block = full[(half * 3 + s) * EDGE : (half * 3 + s + 1) * EDGE]
                unfold(block, j, s, half, full_ref)

    def store(p, q, sums):
        out_ref[p, q] = scale * (sums + part_ref[p, q])

    inner([lambda q, s=s: slab(q, s, 2 - s) for s in range(3)], full_ref, rows, store)


def body(integrals, occupied, virtual, imask, omask, vmask, count):
    total = integrals.shape[1]
    members = lax.axis_size("blk")
    order = block_order(members)
    works_on = [order.index(d) for d in range(members)]

    rows = pl.pallas_call(
        functools.partial(pack_kernel, works_on),
        out_shape=jax.ShapeDtypeStruct((members, 3 * HALF, LANES), jnp.bfloat16),
        in_specs=[pl.BlockSpec(memory_space=pl.ANY)] * 2,
        out_specs=pl.BlockSpec(memory_space=pl.ANY),
        scratch_shapes=[
            pltpu.VMEM((3, total, EDGE * EDGE), jnp.bfloat16),
            pltpu.VMEM((3, total), jnp.int32),
            pltpu.VMEM((3, total * PITCH, LANES), jnp.float32),
            pltpu.VMEM((members, 3 * HALF, LANES), jnp.bfloat16),
            pltpu.SemaphoreType.DMA((7,)),
        ],
        compiler_params=pltpu.CompilerParams(vmem_limit_bytes=63 * 1024 * 1024),
        name="pack",
    )(jnp.transpose(integrals[0], (1, 0, 2)), imask.T)
    greens = pl.pallas_call(
        functools.partial(prep_kernel, total),
        out_shape=jax.ShapeDtypeStruct((6 * HALF, LANES), jnp.bfloat16),
        in_specs=[SMEM] * 3 + [VMEM] * 2,
        out_specs=VMEM,
        scratch_shapes=[pltpu.VMEM((2, 3 * PITCH, LANES), jnp.float32)],
        name="prep",
    )(omask.T, vmask.T, count, occupied[0], virtual[0])
    greens = lax.ppermute(greens, "blk", list(enumerate(order)))
    own = lax.all_to_all(rows, "blk", split_axis=0, concat_axis=0, tiled=True)
    core_pairs = [(order[j], order[j + 1 - 2 * (j % 2)]) for j in range(members)]
    chip_pairs = [(order[j], order[(j - 1 + 2 * (j % 2)) % members]) for j in range(members)]
    to_chip = jnp.concatenate([own[:, : 2 * HALF].reshape(-1, LANES), greens[: 2 * EDGE]], 0)
    to_core = jnp.concatenate([own[:, HALF:].reshape(-1, LANES), greens[EDGE:]], 0)
    schip = lax.ppermute(to_chip, "blk", chip_pairs)
    score = lax.ppermute(to_core, "blk", core_pairs)
    early, sides = pl.pallas_call(
        functools.partial(early_kernel, members),
        out_shape=(
            jax.ShapeDtypeStruct((members, members), jnp.float32),
            jax.ShapeDtypeStruct((3, EDGE, members // 2 * LANES), jnp.bfloat16),
        ),
        in_specs=[VMEM] * 2,
        out_specs=(VMEM, VMEM),
        scratch_shapes=[
            pltpu.VMEM((2, 2 * EDGE, LANES), jnp.bfloat16),
            pltpu.VMEM((2, members // 2 * EDGE, LANES), jnp.bfloat16),
            pltpu.VMEM((members, 2 * HALF, LANES), jnp.bfloat16),
        ],
        compiler_params=pltpu.CompilerParams(vmem_limit_bytes=24 * 1024 * 1024),
        name="early",
    )(own, greens)
    part = pl.pallas_call(
        functools.partial(main_kernel, 1.0 / math.sqrt(5 * EDGE * EDGE * total), members),
        out_shape=jax.ShapeDtypeStruct((members, members), jnp.float32),
        in_specs=[VMEM] * 6,
        out_specs=VMEM,
        scratch_shapes=[
            pltpu.VMEM((6 * EDGE, 3 * LANES), jnp.bfloat16),
            pltpu.VMEM((members // 2 * EDGE, 3 * LANES), jnp.bfloat16),
            pltpu.VMEM((members, 3 * HALF, LANES), jnp.bfloat16),
        ],
        compiler_params=pltpu.CompilerParams(vmem_limit_bytes=24 * 1024 * 1024),
        name="products",
    )(early, sides, schip, own, greens, score)
    mine = lax.all_to_all(part, "blk", split_axis=0, concat_axis=0, tiled=True)
    return jnp.sum(mine, axis=0, keepdims=True)


def solution(mesh):
    return jax.shard_map(
        body,
        mesh=mesh,
        in_specs=(
            P(("grp", "blk"), None, None, None),
            P(("grp", "blk"), None, None),
            P(("grp", "blk"), None, None),
            P(),
            P(),
            P(),
            P(),
        ),
        out_specs=P(("grp", "blk"), None),
        check_vma=False,
    )
```

```python
import functools
import math

import jax
import jax.numpy as jnp
from jax import lax
from jax.experimental import pallas as pl
from jax.experimental.pallas import tpu as pltpu
from jax.sharding import PartitionSpec as P

EDGE = 64
HALF = 32
LANES = 128
PITCH = 40
VMEM = pl.BlockSpec(memory_space=pltpu.VMEM)
SMEM = pl.BlockSpec(memory_space=pltpu.SMEM)
NT = (((1,), (1,)), ((), ()))


def block_order(count):
    if count == 16:
        chips = [3, 1, 0, 2, 4, 6, 7, 5]
        return [2 * chip + core for chip in chips for core in (0, 1)]
    return list(range(count))


def pack_kernel(works_on, x_hbm, imask_hbm, out_hbm, x_ref, imask_ref, rows_ref, out_ref, sems):
    blocks = x_ref.shape[1]
    copies = [pltpu.make_async_copy(x_hbm.at[a], x_ref.at[a], sems.at[a]) for a in range(3)]
    masks = pltpu.make_async_copy(imask_hbm, imask_ref, sems.at[3])
    masks.start()
    for copy in copies:
        copy.start()
    diagonal = lax.broadcasted_iota(jnp.int32, (blocks, blocks), 0) == lax.broadcasted_iota(
        jnp.int32, (blocks, blocks), 1
    )
    masks.wait()
    sent = []
    for a in (1, 0, 2):
        mask = jnp.where(diagonal, imask_ref[pl.ds(a, 1), :].astype(jnp.float32), 0.0)
        mask = jnp.broadcast_to(jnp.sum(mask, axis=1, keepdims=True), (blocks, LANES))
        copies[a].wait()
        for c in range(HALF):
            rows_ref[a, pl.ds(c, blocks, stride=PITCH), :] = (
                x_ref[a, :, c * LANES : (c + 1) * LANES].astype(jnp.float32) * mask
            )
        for d, b in enumerate(works_on):
            to = 2 - a if b % 2 else a
            out_ref[d, pl.ds(to * HALF, HALF), :] = rows_ref[a, pl.ds(b * PITCH, HALF), :].astype(
                jnp.bfloat16
            )
        for to in {0: (), 1: (1,), 2: (0, 2)}[a]:
            part = pl.ds(to * HALF, HALF)
            copy = pltpu.make_async_copy(
                out_ref.at[:, part, :], out_hbm.at[:, part, :], sems.at[4 + to]
            )
            copy.start()
            sent.append(copy)
    for copy in sent:
        copy.wait()


def prep_kernel(total, omask, vmask, count, occ_ref, vir_ref, out_ref, rows_ref):
    own = lax.axis_index("blk")
    for k, ref in enumerate((occ_ref, vir_ref)):
        for c in range(HALF):
            rows_ref[k, pl.ds(c, 3, stride=PITCH), :] = ref[
                :, c * LANES : (c + 1) * LANES
            ].astype(jnp.float32)
    lane = lax.broadcasted_iota(jnp.int32, (HALF, LANES), 1)
    row = lax.broadcasted_iota(jnp.int32, (HALF, LANES), 0)
    left = lane < EDGE
    col = jnp.where(left, lane, lane - EDGE)
    keep = [(2 * row + par < count[own]).astype(jnp.float32) for par in range(2)]
    vir, occ = [], []
    for a in range(3):
        used = (col < count[lax.rem(own + (total + a - 1), total)]).astype(jnp.float32)
        v = rows_ref[1, pl.ds(a * PITCH, HALF), :] * (used * vmask[a, own].astype(jnp.float32))
        vir += [v * keep[0], pltpu.roll(v, EDGE, 1) * keep[1]]
        o = rows_ref[0, pl.ds(a * PITCH, HALF), :] * (used * omask[a, own].astype(jnp.float32))
        occ.append((pltpu.roll(o, EDGE, 1) * keep[0], o * keep[1]))
    vir += [jnp.zeros((HALF, LANES), jnp.float32)] * 2
    first = jnp.concatenate(vir[:4], 0).T[:EDGE]
    second = jnp.concatenate(vir[4:], 0).T[:EDGE]
    odd = lax.rem(own, 2)
    for a, turned in enumerate((first, pltpu.roll(first, EDGE, 1), second)):
        at = pl.multiple_of((a + odd * (2 - 2 * a)) * EDGE, EDGE)
        for par in range(2):
            out_ref[pl.ds(at + par * HALF, HALF), :] = jnp.where(
                left, turned[par * HALF : (par + 1) * HALF], occ[a][par]
            ).astype(jnp.bfloat16)


def halves(slab, rows_at, j):
    even, odd = [], []
    for k in range(j, j + 2):
        one, two = slab(2 * k, *rows_at), slab(2 * k + 1, *rows_at)
        even.append(jnp.concatenate([one[:, :EDGE], two[:, :EDGE]], 1))
        odd.append(jnp.concatenate([one[:, EDGE:], two[:, EDGE:]], 1))
    return [jnp.concatenate(even, 1), jnp.concatenate(odd, 1)]


def unfold(block, j, g, half, full_ref):
    block = block.astype(jnp.bfloat16)
    place = pl.ds(g * HALF, HALF)
    for k in range(2):
        even = block[:HALF, k * LANES : (k + 1) * LANES]
        odd = block[HALF:, k * LANES : (k + 1) * LANES]
        first = 2 * (j + 2 * k) + half
        full_ref[first, place, :] = jnp.concatenate([even[:, :EDGE], odd[:, :EDGE]], 1)
        full_ref[first + 2, place, :] = jnp.concatenate([even[:, EDGE:], odd[:, EDGE:]], 1)


def inner(slabs, full_ref, rows, store):
    group = 16
    span = group * 16
    ri = lax.broadcasted_iota(jnp.int32, (span, span), 0)
    ci = lax.broadcasted_iota(jnp.int32, (span, span), 1)
    same = lax.rem(ri, 16) == lax.rem(ci, 16)
    pick = (
        lax.broadcasted_iota(jnp.int32, (span, group), 0) // 16
        == lax.broadcasted_iota(jnp.int32, (span, group), 1)
    ).astype(jnp.float32)
    for p in range(0, rows, group):
        for q in range(0, rows, group):
            acc = None
            for g, slab in enumerate(slabs):
                lhs = [slab(k) for k in range(p, p + group)]
                lhs = [jnp.concatenate([x[:16], x[16:]], 1) for x in lhs]
                rhs = [
                    full_ref[pl.ds(q, group), pl.ds(g * HALF + c * 16, 16), :].reshape(span, LANES)
                    for c in range(2)
                ]
                one = lax.dot_general(
                    jnp.concatenate(lhs, 0),
                    jnp.concatenate(rhs, 1),
                    NT,
                    preferred_element_type=jnp.float32,
                )
                acc = one if acc is None else acc + one
            kept = jnp.where(same, acc, 0.0).reshape(group, 16, span)
            store(
                pl.ds(p, group),
                pl.ds(q, group),
                jnp.dot(
                    jnp.sum(kept, axis=1),
                    pick,
                    preferred_element_type=jnp.float32,
                    precision=lax.Precision.HIGHEST,
                ),
            )


def readers(rows, schip, sown, gown, score):
    pair = 2 * HALF

    def slab(q, s, a):
        if s == 0:
            return schip[pl.ds(q * pair + (2 - a) * HALF, HALF), :]
        if s == 2:
            return score[pl.ds(q * pair + (1 - a) * HALF, HALF), :]
        return sown[q, pl.ds(a * HALF, HALF), :]

    def green(s, a):
        if s == 0:
            return schip[pl.ds(rows * pair + (2 - a) * EDGE, EDGE), :]
        if s == 2:
            return score[pl.ds(rows * pair + (1 - a) * EDGE, EDGE), :]
        return gown[pl.ds(a * EDGE, EDGE), :]

    return slab, green


def early_kernel(rows, sown, gown, part_ref, sides_ref, far_ref, half_ref, full_ref):
    slab, green = readers(rows, None, sown, gown, None)
    none = jnp.zeros((EDGE, EDGE), jnp.bfloat16)
    for k in range(2):
        o = green(1, 2 * k)[:, EDGE:]
        far_ref[k] = jnp.concatenate(
            [jnp.concatenate([o, none], 1), jnp.concatenate([none, o], 1)], 0
        )
    for j in range(0, rows // 2, 2):
        for a in range(3):
            side = jnp.concatenate(halves(slab, (1, a), j), 0)
            sides_ref[a, :, pl.ds(j * LANES, 2 * LANES)] = side
            if a == 1:
                continue
            both = jnp.dot(
                green(1, 2 - a)[:, :EDGE], side, preferred_element_type=jnp.float32
            ).astype(jnp.bfloat16)
            for k in range(2):
                half_ref[a // 2, pl.ds((j + k) * EDGE, EDGE), :] = both[
                    :, k * LANES : (k + 1) * LANES
                ]
    for j in range(0, rows // 2, 4):
        for k in range(2):
            full = lax.dot_general(
                far_ref[k],
                half_ref[k, pl.ds(j * EDGE, 4 * EDGE), :],
                NT,
                preferred_element_type=jnp.float32,
            )
            for half in range(2):
                unfold(full[half * EDGE : (half + 1) * EDGE], j, k, half, full_ref)

    def store(p, q, sums):
        part_ref[p, q] = sums

    inner([lambda q: slab(q, 1, 2), lambda q: slab(q, 1, 0)], full_ref, rows, store)


def main_kernel(
    scale, rows, part_ref, sides_ref, schip, sown, gown, score, out_ref, occ_ref, half_ref, full_ref
):
    slab, green = readers(rows, schip, sown, gown, score)
    none = jnp.zeros((EDGE, EDGE), jnp.bfloat16)
    near = [green(s, 2 - s)[:, :EDGE] for s in range(3)]
    mid = jnp.concatenate(near, 1)
    ends = jnp.concatenate(
        [
            jnp.concatenate([near[0], near[1], none, none], 1),
            jnp.concatenate([none, none, near[1], near[2]], 1),
        ],
        0,
    )
    used = ({0: 1, 1: 2}, {0: 0, 1: 1, 2: 2}, {1: 0, 2: 1})
    for s in range(3):
        for t in range(3):
            for half in range(2):
                at = pl.ds((half * 3 + s) * EDGE, EDGE)
                to = pl.ds(t * LANES, LANES)
                if t in used[s]:
                    o = green(s, used[s][t])[:, EDGE:]
                    occ_ref[at, to] = jnp.concatenate([none, o] if half else [o, none], 1)
                else:
                    occ_ref[at, to] = jnp.zeros((EDGE, LANES), jnp.bfloat16)

    for j in range(0, rows // 2, 2):
        own = [sides_ref[a, :, pl.ds(j * LANES, 2 * LANES)] for a in range(3)]
        both = jnp.dot(
            ends,
            jnp.concatenate(halves(slab, (0, 1), j) + [own[0], own[2]] + halves(slab, (2, 1), j), 0),
            preferred_element_type=jnp.float32,
        ).astype(jnp.bfloat16)
        middle = jnp.dot(
            mid,
            jnp.concatenate(halves(slab, (0, 2), j) + [own[1]] + halves(slab, (2, 0), j), 0),
            preferred_element_type=jnp.float32,
        ).astype(jnp.bfloat16)
        for t, piece in enumerate((both[:EDGE], middle, both[EDGE:])):
            for k in range(2):
                half_ref[pl.ds((j + k) * EDGE, EDGE), pl.ds(t * LANES, LANES)] = piece[
                    :, k * LANES : (k + 1) * LANES
                ]

    for j in range(0, rows // 2, 4):
        at = pl.ds(j * EDGE, 4 * EDGE)
        full = lax.dot_general(
            occ_ref[...],
            half_ref[at, :],
            NT,
            preferred_element_type=jnp.float32,
        )
        for half in range(2):
            for s in range(3):
                block = full[(half * 3 + s) * EDGE : (half * 3 + s + 1) * EDGE]
                unfold(block, j, s, half, full_ref)

    def store(p, q, sums):
        out_ref[p, q] = scale * (sums + part_ref[p, q])

    inner([lambda q, s=s: slab(q, s, 2 - s) for s in range(3)], full_ref, rows, store)


def body(integrals, occupied, virtual, imask, omask, vmask, count):
    total = integrals.shape[1]
    members = lax.axis_size("blk")
    order = block_order(members)
    works_on = [order.index(d) for d in range(members)]

    rows = pl.pallas_call(
        functools.partial(pack_kernel, works_on),
        out_shape=jax.ShapeDtypeStruct((members, 3 * HALF, LANES), jnp.bfloat16),
        in_specs=[pl.BlockSpec(memory_space=pl.ANY)] * 2,
        out_specs=pl.BlockSpec(memory_space=pl.ANY),
        scratch_shapes=[
            pltpu.VMEM((3, total, EDGE * EDGE), jnp.bfloat16),
            pltpu.VMEM((3, total), jnp.int32),
            pltpu.VMEM((3, total * PITCH, LANES), jnp.float32),
            pltpu.VMEM((members, 3 * HALF, LANES), jnp.bfloat16),
            pltpu.SemaphoreType.DMA((7,)),
        ],
        compiler_params=pltpu.CompilerParams(vmem_limit_bytes=63 * 1024 * 1024),
        name="pack",
    )(jnp.transpose(integrals[0], (1, 0, 2)), imask.T)
    greens = pl.pallas_call(
        functools.partial(prep_kernel, total),
        out_shape=jax.ShapeDtypeStruct((6 * HALF, LANES), jnp.bfloat16),
        in_specs=[SMEM] * 3 + [VMEM] * 2,
        out_specs=VMEM,
        scratch_shapes=[pltpu.VMEM((2, 3 * PITCH, LANES), jnp.float32)],
        name="prep",
    )(omask.T, vmask.T, count, occupied[0], virtual[0])
    greens = lax.ppermute(greens, "blk", list(enumerate(order)))
    own = lax.all_to_all(rows, "blk", split_axis=0, concat_axis=0, tiled=True)
    core_pairs = [(order[j], order[j + 1 - 2 * (j % 2)]) for j in range(members)]
    chip_pairs = [(order[j], order[(j - 1 + 2 * (j % 2)) % members]) for j in range(members)]
    to_chip = jnp.concatenate([own[:, : 2 * HALF].reshape(-1, LANES), greens[: 2 * EDGE]], 0)
    to_core = jnp.concatenate([own[:, HALF:].reshape(-1, LANES), greens[EDGE:]], 0)
    schip = lax.ppermute(to_chip, "blk", chip_pairs)
    score = lax.ppermute(to_core, "blk", core_pairs)
    early, sides = pl.pallas_call(
        functools.partial(early_kernel, members),
        out_shape=(
            jax.ShapeDtypeStruct((members, members), jnp.float32),
            jax.ShapeDtypeStruct((3, EDGE, members // 2 * LANES), jnp.bfloat16),
        ),
        in_specs=[VMEM] * 2,
        out_specs=(VMEM, VMEM),
        scratch_shapes=[
            pltpu.VMEM((2, 2 * EDGE, LANES), jnp.bfloat16),
            pltpu.VMEM((2, members // 2 * EDGE, LANES), jnp.bfloat16),
            pltpu.VMEM((members, 2 * HALF, LANES), jnp.bfloat16),
        ],
        compiler_params=pltpu.CompilerParams(vmem_limit_bytes=24 * 1024 * 1024),
        name="early",
    )(own, greens)
    part = pl.pallas_call(
        functools.partial(main_kernel, 1.0 / math.sqrt(5 * EDGE * EDGE * total), members),
        out_shape=jax.ShapeDtypeStruct((members, members), jnp.float32),
        in_specs=[VMEM] * 6,
        out_specs=VMEM,
        scratch_shapes=[
            pltpu.VMEM((6 * EDGE, 3 * LANES), jnp.bfloat16),
            pltpu.VMEM((members // 2 * EDGE, 3 * LANES), jnp.bfloat16),
            pltpu.VMEM((members, 3 * HALF, LANES), jnp.bfloat16),
        ],
        compiler_params=pltpu.CompilerParams(vmem_limit_bytes=24 * 1024 * 1024),
        name="products",
    )(early, sides, schip, own, greens, score)
    mine = lax.all_to_all(part, "blk", split_axis=0, concat_axis=0, tiled=True)
    return jnp.sum(mine, axis=0, keepdims=True)


def solution(mesh):
    return jax.shard_map(
        body,
        mesh=mesh,
        in_specs=(
            P(("grp", "blk"), None, None, None),
            P(("grp", "blk"), None, None),
            P(("grp", "blk"), None, None),
            P(),
            P(),
            P(),
            P(),
        ),
        out_specs=P(("grp", "blk"), None),
        check_vma=False,
    )
```

```python
import functools
import math

import jax
import jax.numpy as jnp
from jax import lax
from jax.experimental import pallas as pl
from jax.experimental.pallas import tpu as pltpu
from jax.sharding import PartitionSpec as P

EDGE = 64
HALF = 32
LANES = 128
PITCH = 40
VMEM = pl.BlockSpec(memory_space=pltpu.VMEM)
SMEM = pl.BlockSpec(memory_space=pltpu.SMEM)
NT = (((1,), (1,)), ((), ()))


def block_order(count):
    if count == 16:
        chips = [3, 1, 0, 2, 4, 6, 7, 5]
        return [2 * chip + core for chip in chips for core in (0, 1)]
    return list(range(count))


def pack_kernel(works_on, x_hbm, imask_hbm, out_hbm, x_ref, imask_ref, rows_ref, out_ref, sems):
    blocks = x_ref.shape[1]
    copies = [pltpu.make_async_copy(x_hbm.at[a], x_ref.at[a], sems.at[a]) for a in range(3)]
    masks = pltpu.make_async_copy(imask_hbm, imask_ref, sems.at[3])
    masks.start()
    for copy in copies:
        copy.start()
    diagonal = lax.broadcasted_iota(jnp.int32, (blocks, blocks), 0) == lax.broadcasted_iota(
        jnp.int32, (blocks, blocks), 1
    )
    masks.wait()
    sent = []
    for a in (1, 0, 2):
        mask = jnp.where(diagonal, imask_ref[pl.ds(a, 1), :].astype(jnp.float32), 0.0)
        mask = jnp.broadcast_to(jnp.sum(mask, axis=1, keepdims=True), (blocks, LANES))
        copies[a].wait()
        for c in range(HALF):
            rows_ref[a, pl.ds(c, blocks, stride=PITCH), :] = (
                x_ref[a, :, c * LANES : (c + 1) * LANES].astype(jnp.float32) * mask
            )
        for d, b in enumerate(works_on):
            to = 2 - a if b % 2 else a
            out_ref[d, pl.ds(to * HALF, HALF), :] = rows_ref[a, pl.ds(b * PITCH, HALF), :].astype(
                jnp.bfloat16
            )
        for to in {0: (), 1: (1,), 2: (0, 2)}[a]:
            part = pl.ds(to * HALF, HALF)
            copy = pltpu.make_async_copy(
                out_ref.at[:, part, :], out_hbm.at[:, part, :], sems.at[4 + to]
            )
            copy.start()
            sent.append(copy)
    for copy in sent:
        copy.wait()


def prep_kernel(total, omask, vmask, count, occ_ref, vir_ref, out_ref, rows_ref):
    own = lax.axis_index("blk")
    for k, ref in enumerate((occ_ref, vir_ref)):
        for c in range(HALF):
            rows_ref[k, pl.ds(c, 3, stride=PITCH), :] = ref[
                :, c * LANES : (c + 1) * LANES
            ].astype(jnp.float32)
    lane = lax.broadcasted_iota(jnp.int32, (HALF, LANES), 1)
    row = lax.broadcasted_iota(jnp.int32, (HALF, LANES), 0)
    left = lane < EDGE
    col = jnp.where(left, lane, lane - EDGE)
    keep = [(2 * row + par < count[own]).astype(jnp.float32) for par in range(2)]
    vir, occ = [], []
    for a in range(3):
        used = (col < count[lax.rem(own + (total + a - 1), total)]).astype(jnp.float32)
        v = rows_ref[1, pl.ds(a * PITCH, HALF), :] * (used * vmask[a, own].astype(jnp.float32))
        vir += [v * keep[0], pltpu.roll(v, EDGE, 1) * keep[1]]
        o = rows_ref[0, pl.ds(a * PITCH, HALF), :] * (used * omask[a, own].astype(jnp.float32))
        occ.append((pltpu.roll(o, EDGE, 1) * keep[0], o * keep[1]))
    vir += [jnp.zeros((HALF, LANES), jnp.float32)] * 2
    first = jnp.concatenate(vir[:4], 0).T[:EDGE]
    second = jnp.concatenate(vir[4:], 0).T[:EDGE]
    odd = lax.rem(own, 2)
    for a, turned in enumerate((first, pltpu.roll(first, EDGE, 1), second)):
        at = pl.multiple_of((a + odd * (2 - 2 * a)) * EDGE, EDGE)
        for par in range(2):
            out_ref[pl.ds(at + par * HALF, HALF), :] = jnp.where(
                left, turned[par * HALF : (par + 1) * HALF], occ[a][par]
            ).astype(jnp.bfloat16)


def halves(slab, rows_at, j):
    even, odd = [], []
    for k in range(j, j + 2):
        one, two = slab(2 * k, *rows_at), slab(2 * k + 1, *rows_at)
        even.append(jnp.concatenate([one[:, :EDGE], two[:, :EDGE]], 1))
        odd.append(jnp.concatenate([one[:, EDGE:], two[:, EDGE:]], 1))
    return [jnp.concatenate(even, 1), jnp.concatenate(odd, 1)]


def unfold(block, j, g, half, full_ref):
    block = block.astype(jnp.bfloat16)
    place = pl.ds(g * HALF, HALF)
    for k in range(2):
        even = block[:HALF, k * LANES : (k + 1) * LANES]
        odd = block[HALF:, k * LANES : (k + 1) * LANES]
        first = 2 * (j + 2 * k) + half
        full_ref[first, place, :] = jnp.concatenate([even[:, :EDGE], odd[:, :EDGE]], 1)
        full_ref[first + 2, place, :] = jnp.concatenate([even[:, EDGE:], odd[:, EDGE:]], 1)


def inner(slabs, full_ref, rows, store):
    group = 16
    span = group * 16
    ri = lax.broadcasted_iota(jnp.int32, (span, span), 0)
    ci = lax.broadcasted_iota(jnp.int32, (span, span), 1)
    same = lax.rem(ri, 16) == lax.rem(ci, 16)
    pick = (
        lax.broadcasted_iota(jnp.int32, (span, group), 0) // 16
        == lax.broadcasted_iota(jnp.int32, (span, group), 1)
    ).astype(jnp.float32)
    for p in range(0, rows, group):
        for q in range(0, rows, group):
            acc = None
            for g, slab in enumerate(slabs):
                lhs = [slab(k) for k in range(p, p + group)]
                lhs = [jnp.concatenate([x[:16], x[16:]], 1) for x in lhs]
                rhs = [
                    full_ref[pl.ds(q, group), pl.ds(g * HALF + c * 16, 16), :].reshape(span, LANES)
                    for c in range(2)
                ]
                one = lax.dot_general(
                    jnp.concatenate(lhs, 0),
                    jnp.concatenate(rhs, 1),
                    NT,
                    preferred_element_type=jnp.float32,
                )
                acc = one if acc is None else acc + one
            kept = jnp.where(same, acc, 0.0).reshape(group, 16, span)
            store(
                pl.ds(p, group),
                pl.ds(q, group),
                jnp.dot(
                    jnp.sum(kept, axis=1),
                    pick,
                    preferred_element_type=jnp.float32,
                    precision=lax.Precision.HIGHEST,
                ),
            )


def readers(rows, schip, gchip, sown, gown, score):
    pair = 2 * HALF

    def slab(q, s, a):
        if s == 0:
            return schip[pl.ds(q * pair + (2 - a) * HALF, HALF), :]
        if s == 2:
            return score[pl.ds(q * pair + (1 - a) * HALF, HALF), :]
        return sown[q, pl.ds(a * HALF, HALF), :]

    def green(s, a):
        if s == 0:
            return gchip[pl.ds((2 - a) * EDGE, EDGE), :]
        if s == 2:
            return score[pl.ds(rows * pair + (1 - a) * EDGE, EDGE), :]
        return gown[pl.ds(a * EDGE, EDGE), :]

    return slab, green


def early_kernel(rows, sown, gown, part_ref, sides_ref, far_ref, half_ref, full_ref):
    slab, green = readers(rows, None, None, sown, gown, None)
    none = jnp.zeros((EDGE, EDGE), jnp.bfloat16)
    for k in range(2):
        o = green(1, 2 * k)[:, EDGE:]
        far_ref[k] = jnp.concatenate(
            [jnp.concatenate([o, none], 1), jnp.concatenate([none, o], 1)], 0
        )
    for j in range(0, rows // 2, 2):
        for a in range(3):
            side = jnp.concatenate(halves(slab, (1, a), j), 0)
            sides_ref[a, :, pl.ds(j * LANES, 2 * LANES)] = side
            if a == 1:
                continue
            both = jnp.dot(
                green(1, 2 - a)[:, :EDGE], side, preferred_element_type=jnp.float32
            ).astype(jnp.bfloat16)
            for k in range(2):
                half_ref[a // 2, pl.ds((j + k) * EDGE, EDGE), :] = both[
                    :, k * LANES : (k + 1) * LANES
                ]
    for j in range(0, rows // 2, 4):
        for k in range(2):
            full = lax.dot_general(
                far_ref[k],
                half_ref[k, pl.ds(j * EDGE, 4 * EDGE), :],
                NT,
                preferred_element_type=jnp.float32,
            )
            for half in range(2):
                unfold(full[half * EDGE : (half + 1) * EDGE], j, k, half, full_ref)

    def store(p, q, sums):
        part_ref[p, q] = sums

    inner([lambda q: slab(q, 1, 2), lambda q: slab(q, 1, 0)], full_ref, rows, store)


def main_kernel(
    scale, rows, part_ref, sides_ref, schip, gchip, sown, gown, score, out_ref, occ_ref, half_ref, full_ref
):
    slab, green = readers(rows, schip, gchip, sown, gown, score)
    none = jnp.zeros((EDGE, EDGE), jnp.bfloat16)
    near = [green(s, 2 - s)[:, :EDGE] for s in range(3)]
    mid = jnp.concatenate(near, 1)
    ends = jnp.concatenate(
        [
            jnp.concatenate([near[0], near[1], none, none], 1),
            jnp.concatenate([none, none, near[1], near[2]], 1),
        ],
        0,
    )
    used = ({0: 1, 1: 2}, {0: 0, 1: 1, 2: 2}, {1: 0, 2: 1})
    for s in range(3):
        for t in range(3):
            for half in range(2):
                at = pl.ds((half * 3 + s) * EDGE, EDGE)
                to = pl.ds(t * LANES, LANES)
                if t in used[s]:
                    o = green(s, used[s][t])[:, EDGE:]
                    occ_ref[at, to] = jnp.concatenate([none, o] if half else [o, none], 1)
                else:
                    occ_ref[at, to] = jnp.zeros((EDGE, LANES), jnp.bfloat16)

    for j in range(0, rows // 2, 2):
        own = [sides_ref[a, :, pl.ds(j * LANES, 2 * LANES)] for a in range(3)]
        both = jnp.dot(
            ends,
            jnp.concatenate(halves(slab, (0, 1), j) + [own[0], own[2]] + halves(slab, (2, 1), j), 0),
            preferred_element_type=jnp.float32,
        ).astype(jnp.bfloat16)
        middle = jnp.dot(
            mid,
            jnp.concatenate(halves(slab, (0, 2), j) + [own[1]] + halves(slab, (2, 0), j), 0),
            preferred_element_type=jnp.float32,
        ).astype(jnp.bfloat16)
        for t, piece in enumerate((both[:EDGE], middle, both[EDGE:])):
            for k in range(2):
                half_ref[pl.ds((j + k) * EDGE, EDGE), pl.ds(t * LANES, LANES)] = piece[
                    :, k * LANES : (k + 1) * LANES
                ]

    for j in range(0, rows // 2, 4):
        at = pl.ds(j * EDGE, 4 * EDGE)
        full = lax.dot_general(
            occ_ref[...],
            half_ref[at, :],
            NT,
            preferred_element_type=jnp.float32,
        )
        for half in range(2):
            for s in range(3):
                block = full[(half * 3 + s) * EDGE : (half * 3 + s + 1) * EDGE]
                unfold(block, j, s, half, full_ref)

    def store(p, q, sums):
        out_ref[p, q] = scale * (sums + part_ref[p, q])

    inner([lambda q, s=s: slab(q, s, 2 - s) for s in range(3)], full_ref, rows, store)


def body(integrals, occupied, virtual, imask, omask, vmask, count):
    total = integrals.shape[1]
    members = lax.axis_size("blk")
    order = block_order(members)
    works_on = [order.index(d) for d in range(members)]

    rows = pl.pallas_call(
        functools.partial(pack_kernel, works_on),
        out_shape=jax.ShapeDtypeStruct((members, 3 * HALF, LANES), jnp.bfloat16),
        in_specs=[pl.BlockSpec(memory_space=pl.ANY)] * 2,
        out_specs=pl.BlockSpec(memory_space=pl.ANY),
        scratch_shapes=[
            pltpu.VMEM((3, total, EDGE * EDGE), jnp.bfloat16),
            pltpu.VMEM((3, total), jnp.int32),
            pltpu.VMEM((3, total * PITCH, LANES), jnp.float32),
            pltpu.VMEM((members, 3 * HALF, LANES), jnp.bfloat16),
            pltpu.SemaphoreType.DMA((7,)),
        ],
        compiler_params=pltpu.CompilerParams(vmem_limit_bytes=63 * 1024 * 1024),
        name="pack",
    )(jnp.transpose(integrals[0], (1, 0, 2)), imask.T)
    greens = pl.pallas_call(
        functools.partial(prep_kernel, total),
        out_shape=jax.ShapeDtypeStruct((6 * HALF, LANES), jnp.bfloat16),
        in_specs=[SMEM] * 3 + [VMEM] * 2,
        out_specs=VMEM,
        scratch_shapes=[pltpu.VMEM((2, 3 * PITCH, LANES), jnp.float32)],
        name="prep",
    )(omask.T, vmask.T, count, occupied[0], virtual[0])
    chip_next = [order[(j - 1 + 2 * (j % 2)) % members] for j in range(members)]
    gchip = lax.ppermute(greens[: 2 * EDGE], "blk", list(enumerate(chip_next)))
    greens = lax.ppermute(greens, "blk", list(enumerate(order)))
    own = lax.all_to_all(rows, "blk", split_axis=0, concat_axis=0, tiled=True)
    core_pairs = [(order[j], order[j + 1 - 2 * (j % 2)]) for j in range(members)]
    chip_pairs = list(zip(order, chip_next))
    to_chip = own[:, : 2 * HALF].reshape(-1, LANES)
    to_core = jnp.concatenate([own[:, HALF:].reshape(-1, LANES), greens[EDGE:]], 0)
    schip = lax.ppermute(to_chip, "blk", chip_pairs)
    score = lax.ppermute(to_core, "blk", core_pairs)
    early, sides = pl.pallas_call(
        functools.partial(early_kernel, members),
        out_shape=(
            jax.ShapeDtypeStruct((members, members), jnp.float32),
            jax.ShapeDtypeStruct((3, EDGE, members // 2 * LANES), jnp.bfloat16),
        ),
        in_specs=[VMEM] * 2,
        out_specs=(VMEM, VMEM),
        scratch_shapes=[
            pltpu.VMEM((2, 2 * EDGE, LANES), jnp.bfloat16),
            pltpu.VMEM((2, members // 2 * EDGE, LANES), jnp.bfloat16),
            pltpu.VMEM((members, 2 * HALF, LANES), jnp.bfloat16),
        ],
        compiler_params=pltpu.CompilerParams(vmem_limit_bytes=24 * 1024 * 1024),
        name="early",
    )(own, greens)
    part = pl.pallas_call(
        functools.partial(main_kernel, 1.0 / math.sqrt(5 * EDGE * EDGE * total), members),
        out_shape=jax.ShapeDtypeStruct((members, members), jnp.float32),
        in_specs=[VMEM] * 7,
        out_specs=VMEM,
        scratch_shapes=[
            pltpu.VMEM((6 * EDGE, 3 * LANES), jnp.bfloat16),
            pltpu.VMEM((members // 2 * EDGE, 3 * LANES), jnp.bfloat16),
            pltpu.VMEM((members, 3 * HALF, LANES), jnp.bfloat16),
        ],
        compiler_params=pltpu.CompilerParams(vmem_limit_bytes=24 * 1024 * 1024),
        name="products",
    )(early, sides, schip, gchip, own, greens, score)
    mine = lax.all_to_all(part, "blk", split_axis=0, concat_axis=0, tiled=True)
    return jnp.sum(mine, axis=0, keepdims=True)


def solution(mesh):
    return jax.shard_map(
        body,
        mesh=mesh,
        in_specs=(
            P(("grp", "blk"), None, None, None),
            P(("grp", "blk"), None, None),
            P(("grp", "blk"), None, None),
            P(),
            P(),
            P(),
            P(),
        ),
        out_specs=P(("grp", "blk"), None),
        check_vma=False,
    )
```

```python
import functools
import math

import jax
import jax.numpy as jnp
from jax import lax
from jax.experimental import pallas as pl
from jax.experimental.pallas import tpu as pltpu
from jax.sharding import PartitionSpec as P

EDGE = 64
HALF = 32
LANES = 128
PITCH = 40
VMEM = pl.BlockSpec(memory_space=pltpu.VMEM)
SMEM = pl.BlockSpec(memory_space=pltpu.SMEM)
NT = (((1,), (1,)), ((), ()))


def block_order(count):
    if count == 16:
        chips = [3, 1, 0, 2, 4, 6, 7, 5]
        return [2 * chip + core for chip in chips for core in (0, 1)]
    return list(range(count))


def pack_kernel(works_on, x_hbm, imask_hbm, out_hbm, x_ref, imask_ref, rows_ref, out_ref, sems):
    blocks = x_ref.shape[1]
    copies = [pltpu.make_async_copy(x_hbm.at[a], x_ref.at[a], sems.at[a]) for a in range(3)]
    masks = pltpu.make_async_copy(imask_hbm, imask_ref, sems.at[3])
    masks.start()
    for copy in copies:
        copy.start()
    diagonal = lax.broadcasted_iota(jnp.int32, (blocks, blocks), 0) == lax.broadcasted_iota(
        jnp.int32, (blocks, blocks), 1
    )
    masks.wait()
    sent = []
    for a in (1, 0, 2):
        mask = jnp.where(diagonal, imask_ref[pl.ds(a, 1), :].astype(jnp.float32), 0.0)
        mask = jnp.broadcast_to(jnp.sum(mask, axis=1, keepdims=True), (blocks, LANES))
        copies[a].wait()
        for c in range(HALF):
            rows_ref[a, pl.ds(c, blocks, stride=PITCH), :] = (
                x_ref[a, :, c * LANES : (c + 1) * LANES].astype(jnp.float32) * mask
            )
        for d, b in enumerate(works_on):
            to = 2 - a if b % 2 else a
            out_ref[d, pl.ds(to * HALF, HALF), :] = rows_ref[a, pl.ds(b * PITCH, HALF), :].astype(
                jnp.bfloat16
            )
        for to in {0: (), 1: (1,), 2: (0, 2)}[a]:
            part = pl.ds(to * HALF, HALF)
            copy = pltpu.make_async_copy(
                out_ref.at[:, part, :], out_hbm.at[:, part, :], sems.at[4 + to]
            )
            copy.start()
            sent.append(copy)
    for copy in sent:
        copy.wait()


def prep_kernel(total, omask, vmask, count, occ_ref, vir_ref, out_ref, rows_ref):
    own = lax.axis_index("blk")
    for k, ref in enumerate((occ_ref, vir_ref)):
        for c in range(HALF):
            rows_ref[k, pl.ds(c, 3, stride=PITCH), :] = ref[
                :, c * LANES : (c + 1) * LANES
            ].astype(jnp.float32)
    lane = lax.broadcasted_iota(jnp.int32, (HALF, LANES), 1)
    row = lax.broadcasted_iota(jnp.int32, (HALF, LANES), 0)
    left = lane < EDGE
    col = jnp.where(left, lane, lane - EDGE)
    keep = [(2 * row + par < count[own]).astype(jnp.float32) for par in range(2)]
    vir, occ = [], []
    for a in range(3):
        used = (col < count[lax.rem(own + (total + a - 1), total)]).astype(jnp.float32)
        v = rows_ref[1, pl.ds(a * PITCH, HALF), :] * (used * vmask[a, own].astype(jnp.float32))
        vir += [v * keep[0], pltpu.roll(v, EDGE, 1) * keep[1]]
        o = rows_ref[0, pl.ds(a * PITCH, HALF), :] * (used * omask[a, own].astype(jnp.float32))
        occ.append((pltpu.roll(o, EDGE, 1) * keep[0], o * keep[1]))
    vir += [jnp.zeros((HALF, LANES), jnp.float32)] * 2
    first = jnp.concatenate(vir[:4], 0).T[:EDGE]
    second = jnp.concatenate(vir[4:], 0).T[:EDGE]
    odd = lax.rem(own, 2)
    for a, turned in enumerate((first, pltpu.roll(first, EDGE, 1), second)):
        at = pl.multiple_of((a + odd * (2 - 2 * a)) * EDGE, EDGE)
        for par in range(2):
            out_ref[pl.ds(at + par * HALF, HALF), :] = jnp.where(
                left, turned[par * HALF : (par + 1) * HALF], occ[a][par]
            ).astype(jnp.bfloat16)


def halves(slab, rows_at, j):
    even, odd = [], []
    for k in range(j, j + 2):
        one, two = slab(2 * k, *rows_at), slab(2 * k + 1, *rows_at)
        even.append(jnp.concatenate([one[:, :EDGE], two[:, :EDGE]], 1))
        odd.append(jnp.concatenate([one[:, EDGE:], two[:, EDGE:]], 1))
    return [jnp.concatenate(even, 1), jnp.concatenate(odd, 1)]


def unfold(block, j, g, half, full_ref):
    block = block.astype(jnp.bfloat16)
    place = pl.ds(g * HALF, HALF)
    for k in range(2):
        even = block[:HALF, k * LANES : (k + 1) * LANES]
        odd = block[HALF:, k * LANES : (k + 1) * LANES]
        first = 2 * (j + 2 * k) + half
        full_ref[first, place, :] = jnp.concatenate([even[:, :EDGE], odd[:, :EDGE]], 1)
        full_ref[first + 2, place, :] = jnp.concatenate([even[:, EDGE:], odd[:, EDGE:]], 1)


def inner(slabs, full_ref, rows, store):
    group = 16
    span = group * 16
    ri = lax.broadcasted_iota(jnp.int32, (span, span), 0)
    ci = lax.broadcasted_iota(jnp.int32, (span, span), 1)
    same = lax.rem(ri, 16) == lax.rem(ci, 16)
    pick = (
        lax.broadcasted_iota(jnp.int32, (span, group), 0) // 16
        == lax.broadcasted_iota(jnp.int32, (span, group), 1)
    ).astype(jnp.float32)
    for p in range(0, rows, group):
        for q in range(0, rows, group):
            acc = None
            for g, slab in enumerate(slabs):
                lhs = [slab(k) for k in range(p, p + group)]
                lhs = [jnp.concatenate([x[:16], x[16:]], 1) for x in lhs]
                rhs = [
                    full_ref[pl.ds(q, group), pl.ds(g * HALF + c * 16, 16), :].reshape(span, LANES)
                    for c in range(2)
                ]
                one = lax.dot_general(
                    jnp.concatenate(lhs, 0),
                    jnp.concatenate(rhs, 1),
                    NT,
                    preferred_element_type=jnp.float32,
                )
                acc = one if acc is None else acc + one
            kept = jnp.where(same, acc, 0.0).reshape(group, 16, span)
            store(
                pl.ds(p, group),
                pl.ds(q, group),
                jnp.dot(
                    jnp.sum(kept, axis=1),
                    pick,
                    preferred_element_type=jnp.float32,
                    precision=lax.Precision.HIGHEST,
                ),
            )


def readers(schip, gchip, sown, gown, score, gcore):
    pair = 2 * HALF

    def slab(q, s, a):
        if s == 0:
            return schip[pl.ds(q * pair + (2 - a) * HALF, HALF), :]
        if s == 2:
            return score[pl.ds(q * pair + (1 - a) * HALF, HALF), :]
        return sown[q, pl.ds(a * HALF, HALF), :]

    def green(s, a):
        if s == 0:
            return gchip[pl.ds((2 - a) * EDGE, EDGE), :]
        if s == 2:
            return gcore[pl.ds((1 - a) * EDGE, EDGE), :]
        return gown[pl.ds(a * EDGE, EDGE), :]

    return slab, green


def early_kernel(rows, sown, gown, part_ref, sides_ref, far_ref, half_ref, full_ref):
    slab, green = readers(None, None, sown, gown, None, None)
    none = jnp.zeros((EDGE, EDGE), jnp.bfloat16)
    for k in range(2):
        o = green(1, 2 * k)[:, EDGE:]
        far_ref[k] = jnp.concatenate(
            [jnp.concatenate([o, none], 1), jnp.concatenate([none, o], 1)], 0
        )
    for j in range(0, rows // 2, 2):
        for a in range(3):
            side = jnp.concatenate(halves(slab, (1, a), j), 0)
            sides_ref[a, :, pl.ds(j * LANES, 2 * LANES)] = side
            if a == 1:
                continue
            both = jnp.dot(
                green(1, 2 - a)[:, :EDGE], side, preferred_element_type=jnp.float32
            ).astype(jnp.bfloat16)
            for k in range(2):
                half_ref[a // 2, pl.ds((j + k) * EDGE, EDGE), :] = both[
                    :, k * LANES : (k + 1) * LANES
                ]
    for j in range(0, rows // 2, 4):
        for k in range(2):
            full = lax.dot_general(
                far_ref[k],
                half_ref[k, pl.ds(j * EDGE, 4 * EDGE), :],
                NT,
                preferred_element_type=jnp.float32,
            )
            for half in range(2):
                unfold(full[half * EDGE : (half + 1) * EDGE], j, k, half, full_ref)

    def store(p, q, sums):
        part_ref[p, q] = sums

    inner([lambda q: slab(q, 1, 2), lambda q: slab(q, 1, 0)], full_ref, rows, store)


def main_kernel(
    scale,
    rows,
    part_ref,
    sides_ref,
    schip,
    gchip,
    sown,
    gown,
    score,
    gcore,
    out_ref,
    occ_ref,
    half_ref,
    full_ref,
):
    slab, green = readers(schip, gchip, sown, gown, score, gcore)
    none = jnp.zeros((EDGE, EDGE), jnp.bfloat16)
    near = [green(s, 2 - s)[:, :EDGE] for s in range(3)]
    mid = jnp.concatenate(near, 1)
    ends = jnp.concatenate(
        [
            jnp.concatenate([near[0], near[1], none, none], 1),
            jnp.concatenate([none, none, near[1], near[2]], 1),
        ],
        0,
    )
    used = ({0: 1, 1: 2}, {0: 0, 1: 1, 2: 2}, {1: 0, 2: 1})
    for s in range(3):
        for t in range(3):
            for half in range(2):
                at = pl.ds((half * 3 + s) * EDGE, EDGE)
                to = pl.ds(t * LANES, LANES)
                if t in used[s]:
                    o = green(s, used[s][t])[:, EDGE:]
                    occ_ref[at, to] = jnp.concatenate([none, o] if half else [o, none], 1)
                else:
                    occ_ref[at, to] = jnp.zeros((EDGE, LANES), jnp.bfloat16)

    for j in range(0, rows // 2, 2):
        own = [sides_ref[a, :, pl.ds(j * LANES, 2 * LANES)] for a in range(3)]
        both = jnp.dot(
            ends,
            jnp.concatenate(halves(slab, (0, 1), j) + [own[0], own[2]] + halves(slab, (2, 1), j), 0),
            preferred_element_type=jnp.float32,
        ).astype(jnp.bfloat16)
        middle = jnp.dot(
            mid,
            jnp.concatenate(halves(slab, (0, 2), j) + [own[1]] + halves(slab, (2, 0), j), 0),
            preferred_element_type=jnp.float32,
        ).astype(jnp.bfloat16)
        for t, piece in enumerate((both[:EDGE], middle, both[EDGE:])):
            for k in range(2):
                half_ref[pl.ds((j + k) * EDGE, EDGE), pl.ds(t * LANES, LANES)] = piece[
                    :, k * LANES : (k + 1) * LANES
                ]

    for j in range(0, rows // 2, 4):
        at = pl.ds(j * EDGE, 4 * EDGE)
        full = lax.dot_general(
            occ_ref[...],
            half_ref[at, :],
            NT,
            preferred_element_type=jnp.float32,
        )
        for half in range(2):
            for s in range(3):
                block = full[(half * 3 + s) * EDGE : (half * 3 + s + 1) * EDGE]
                unfold(block, j, s, half, full_ref)

    def store(p, q, sums):
        out_ref[p, q] = scale * (sums + part_ref[p, q])

    inner([lambda q, s=s: slab(q, s, 2 - s) for s in range(3)], full_ref, rows, store)


def body(integrals, occupied, virtual, imask, omask, vmask, count):
    total = integrals.shape[1]
    members = lax.axis_size("blk")
    order = block_order(members)
    works_on = [order.index(d) for d in range(members)]

    rows = pl.pallas_call(
        functools.partial(pack_kernel, works_on),
        out_shape=jax.ShapeDtypeStruct((members, 3 * HALF, LANES), jnp.bfloat16),
        in_specs=[pl.BlockSpec(memory_space=pl.ANY)] * 2,
        out_specs=pl.BlockSpec(memory_space=pl.ANY),
        scratch_shapes=[
            pltpu.VMEM((3, total, EDGE * EDGE), jnp.bfloat16),
            pltpu.VMEM((3, total), jnp.int32),
            pltpu.VMEM((3, total * PITCH, LANES), jnp.float32),
            pltpu.VMEM((members, 3 * HALF, LANES), jnp.bfloat16),
            pltpu.SemaphoreType.DMA((7,)),
        ],
        compiler_params=pltpu.CompilerParams(vmem_limit_bytes=63 * 1024 * 1024),
        name="pack",
    )(jnp.transpose(integrals[0], (1, 0, 2)), imask.T)
    greens = pl.pallas_call(
        functools.partial(prep_kernel, total),
        out_shape=jax.ShapeDtypeStruct((6 * HALF, LANES), jnp.bfloat16),
        in_specs=[SMEM] * 3 + [VMEM] * 2,
        out_specs=VMEM,
        scratch_shapes=[pltpu.VMEM((2, 3 * PITCH, LANES), jnp.float32)],
        name="prep",
    )(omask.T, vmask.T, count, occupied[0], virtual[0])
    chip_next = [order[(j - 1 + 2 * (j % 2)) % members] for j in range(members)]
    gchip = lax.ppermute(greens[: 2 * EDGE], "blk", list(enumerate(chip_next)))
    greens = lax.ppermute(greens, "blk", list(enumerate(order)))
    own = lax.all_to_all(rows, "blk", split_axis=0, concat_axis=0, tiled=True)
    own, greens, gchip = lax.optimization_barrier((own, greens, gchip))
    core_pairs = [(order[j], order[j + 1 - 2 * (j % 2)]) for j in range(members)]
    chip_pairs = list(zip(order, chip_next))
    to_chip = own[:, : 2 * HALF].reshape(-1, LANES)
    to_core = own[:, HALF:].reshape(-1, LANES)
    schip = lax.ppermute(to_chip, "blk", chip_pairs)
    score = lax.ppermute(to_core, "blk", core_pairs)
    gcore = lax.ppermute(greens[EDGE:], "blk", core_pairs)
    early, sides = pl.pallas_call(
        functools.partial(early_kernel, members),
        out_shape=(
            jax.ShapeDtypeStruct((members, members), jnp.float32),
            jax.ShapeDtypeStruct((3, EDGE, members // 2 * LANES), jnp.bfloat16),
        ),
        in_specs=[VMEM] * 2,
        out_specs=(VMEM, VMEM),
        scratch_shapes=[
            pltpu.VMEM((2, 2 * EDGE, LANES), jnp.bfloat16),
            pltpu.VMEM((2, members // 2 * EDGE, LANES), jnp.bfloat16),
            pltpu.VMEM((members, 2 * HALF, LANES), jnp.bfloat16),
        ],
        compiler_params=pltpu.CompilerParams(vmem_limit_bytes=24 * 1024 * 1024),
        name="early",
    )(own, greens)
    part = pl.pallas_call(
        functools.partial(main_kernel, 1.0 / math.sqrt(5 * EDGE * EDGE * total), members),
        out_shape=jax.ShapeDtypeStruct((members, members), jnp.float32),
        in_specs=[VMEM] * 8,
        out_specs=VMEM,
        scratch_shapes=[
            pltpu.VMEM((6 * EDGE, 3 * LANES), jnp.bfloat16),
            pltpu.VMEM((members // 2 * EDGE, 3 * LANES), jnp.bfloat16),
            pltpu.VMEM((members, 3 * HALF, LANES), jnp.bfloat16),
        ],
        compiler_params=pltpu.CompilerParams(vmem_limit_bytes=24 * 1024 * 1024),
        name="products",
    )(early, sides, schip, gchip, own, greens, score, gcore)
    mine = lax.all_to_all(part, "blk", split_axis=0, concat_axis=0, tiled=True)
    return jnp.sum(mine, axis=0, keepdims=True)


def solution(mesh):
    return jax.shard_map(
        body,
        mesh=mesh,
        in_specs=(
            P(("grp", "blk"), None, None, None),
            P(("grp", "blk"), None, None),
            P(("grp", "blk"), None, None),
            P(),
            P(),
            P(),
            P(),
        ),
        out_specs=P(("grp", "blk"), None),
        check_vma=False,
    )
```

```python
import functools
import math

import jax
import jax.numpy as jnp
from jax import lax
from jax.experimental import pallas as pl
from jax.experimental.pallas import tpu as pltpu
from jax.sharding import PartitionSpec as P

EDGE = 64
HALF = 32
LANES = 128
PITCH = 40
VMEM = pl.BlockSpec(memory_space=pltpu.VMEM)
SMEM = pl.BlockSpec(memory_space=pltpu.SMEM)
NT = (((1,), (1,)), ((), ()))


def block_order(count):
    if count == 16:
        chips = [3, 1, 0, 2, 4, 6, 7, 5]
        return [2 * chip + core for chip in chips for core in (0, 1)]
    return list(range(count))


def pack_kernel(works_on, x_hbm, imask_hbm, out_hbm, x_ref, imask_ref, rows_ref, out_ref, sems):
    blocks = x_ref.shape[1]
    copies = [pltpu.make_async_copy(x_hbm.at[a], x_ref.at[a], sems.at[a]) for a in range(3)]
    masks = pltpu.make_async_copy(imask_hbm, imask_ref, sems.at[3])
    masks.start()
    for copy in copies:
        copy.start()
    diagonal = lax.broadcasted_iota(jnp.int32, (blocks, blocks), 0) == lax.broadcasted_iota(
        jnp.int32, (blocks, blocks), 1
    )
    masks.wait()
    sent = []
    for a in (1, 0, 2):
        mask = jnp.where(diagonal, imask_ref[pl.ds(a, 1), :].astype(jnp.float32), 0.0)
        mask = jnp.broadcast_to(jnp.sum(mask, axis=1, keepdims=True), (blocks, LANES))
        copies[a].wait()
        for c in range(HALF):
            rows_ref[a, pl.ds(c, blocks, stride=PITCH), :] = (
                x_ref[a, :, c * LANES : (c + 1) * LANES].astype(jnp.float32) * mask
            )
        for d, b in enumerate(works_on):
            to = 2 - a if b % 2 else a
            out_ref[d, pl.ds(to * HALF, HALF), :] = rows_ref[a, pl.ds(b * PITCH, HALF), :].astype(
                jnp.bfloat16
            )
        for to in {0: (), 1: (1,), 2: (0, 2)}[a]:
            part = pl.ds(to * HALF, HALF)
            copy = pltpu.make_async_copy(
                out_ref.at[:, part, :], out_hbm.at[:, part, :], sems.at[4 + to]
            )
            copy.start()
            sent.append(copy)
    for copy in sent:
        copy.wait()


def prep_kernel(total, omask, vmask, count, occ_ref, vir_ref, out_ref, chip_ref, rows_ref):
    own = lax.axis_index("blk")
    for k, ref in enumerate((occ_ref, vir_ref)):
        for c in range(HALF):
            rows_ref[k, pl.ds(c, 3, stride=PITCH), :] = ref[
                :, c * LANES : (c + 1) * LANES
            ].astype(jnp.float32)
    lane = lax.broadcasted_iota(jnp.int32, (HALF, LANES), 1)
    row = lax.broadcasted_iota(jnp.int32, (HALF, LANES), 0)
    left = lane < EDGE
    col = jnp.where(left, lane, lane - EDGE)
    keep = [(2 * row + par < count[own]).astype(jnp.float32) for par in range(2)]
    vir, occ = [], []
    for a in range(3):
        used = (col < count[lax.rem(own + (total + a - 1), total)]).astype(jnp.float32)
        v = rows_ref[1, pl.ds(a * PITCH, HALF), :] * (used * vmask[a, own].astype(jnp.float32))
        vir += [v * keep[0], pltpu.roll(v, EDGE, 1) * keep[1]]
        o = rows_ref[0, pl.ds(a * PITCH, HALF), :] * (used * omask[a, own].astype(jnp.float32))
        occ.append((pltpu.roll(o, EDGE, 1) * keep[0], o * keep[1]))
    vir += [jnp.zeros((HALF, LANES), jnp.float32)] * 2
    first = jnp.concatenate(vir[:4], 0).T[:EDGE]
    second = jnp.concatenate(vir[4:], 0).T[:EDGE]
    odd = lax.rem(own, 2)
    for a, turned in enumerate((first, pltpu.roll(first, EDGE, 1), second)):
        at = pl.multiple_of((a + odd * (2 - 2 * a)) * EDGE, EDGE)
        for par in range(2):
            out_ref[pl.ds(at + par * HALF, HALF), :] = jnp.where(
                left, turned[par * HALF : (par + 1) * HALF], occ[a][par]
            ).astype(jnp.bfloat16)
    chip_ref[...] = out_ref[pl.ds(0, 2 * EDGE), :]


def halves(slab, rows_at, j):
    even, odd = [], []
    for k in range(j, j + 2):
        one, two = slab(2 * k, *rows_at), slab(2 * k + 1, *rows_at)
        even.append(jnp.concatenate([one[:, :EDGE], two[:, :EDGE]], 1))
        odd.append(jnp.concatenate([one[:, EDGE:], two[:, EDGE:]], 1))
    return [jnp.concatenate(even, 1), jnp.concatenate(odd, 1)]


def unfold(block, j, g, half, full_ref):
    block = block.astype(jnp.bfloat16)
    place = pl.ds(g * HALF, HALF)
    for k in range(2):
        even = block[:HALF, k * LANES : (k + 1) * LANES]
        odd = block[HALF:, k * LANES : (k + 1) * LANES]
        first = 2 * (j + 2 * k) + half
        full_ref[first, place, :] = jnp.concatenate([even[:, :EDGE], odd[:, :EDGE]], 1)
        full_ref[first + 2, place, :] = jnp.concatenate([even[:, EDGE:], odd[:, EDGE:]], 1)


def inner(slabs, full_ref, rows, store):
    group = 16
    span = group * 16
    ri = lax.broadcasted_iota(jnp.int32, (span, span), 0)
    ci = lax.broadcasted_iota(jnp.int32, (span, span), 1)
    same = lax.rem(ri, 16) == lax.rem(ci, 16)
    pick = (
        lax.broadcasted_iota(jnp.int32, (span, group), 0) // 16
        == lax.broadcasted_iota(jnp.int32, (span, group), 1)
    ).astype(jnp.float32)
    for p in range(0, rows, group):
        for q in range(0, rows, group):
            acc = None
            for g, slab in enumerate(slabs):
                lhs = [slab(k) for k in range(p, p + group)]
                lhs = [jnp.concatenate([x[:16], x[16:]], 1) for x in lhs]
                rhs = [
                    full_ref[pl.ds(q, group), pl.ds(g * HALF + c * 16, 16), :].reshape(span, LANES)
                    for c in range(2)
                ]
                one = lax.dot_general(
                    jnp.concatenate(lhs, 0),
                    jnp.concatenate(rhs, 1),
                    NT,
                    preferred_element_type=jnp.float32,
                )
                acc = one if acc is None else acc + one
            kept = jnp.where(same, acc, 0.0).reshape(group, 16, span)
            store(
                pl.ds(p, group),
                pl.ds(q, group),
                jnp.dot(
                    jnp.sum(kept, axis=1),
                    pick,
                    preferred_element_type=jnp.float32,
                    precision=lax.Precision.HIGHEST,
                ),
            )


def readers(schip, gchip, sown, gown, score, gcore):
    pair = 2 * HALF

    def slab(q, s, a):
        if s == 0:
            return schip[pl.ds(q * pair + (2 - a) * HALF, HALF), :]
        if s == 2:
            return score[pl.ds(q * pair + (1 - a) * HALF, HALF), :]
        return sown[q, pl.ds(a * HALF, HALF), :]

    def green(s, a):
        if s == 0:
            return gchip[pl.ds((2 - a) * EDGE, EDGE), :]
        if s == 2:
            return gcore[pl.ds((1 - a) * EDGE, EDGE), :]
        return gown[pl.ds(a * EDGE, EDGE), :]

    return slab, green


def early_kernel(rows, sown, gown, part_ref, sides_ref, far_ref, half_ref, full_ref):
    slab, green = readers(None, None, sown, gown, None, None)
    none = jnp.zeros((EDGE, EDGE), jnp.bfloat16)
    for k in range(2):
        o = green(1, 2 * k)[:, EDGE:]
        far_ref[k] = jnp.concatenate(
            [jnp.concatenate([o, none], 1), jnp.concatenate([none, o], 1)], 0
        )
    for j in range(0, rows // 2, 2):
        for a in range(3):
            side = jnp.concatenate(halves(slab, (1, a), j), 0)
            sides_ref[a, :, pl.ds(j * LANES, 2 * LANES)] = side
            if a == 1:
                continue
            both = jnp.dot(
                green(1, 2 - a)[:, :EDGE], side, preferred_element_type=jnp.float32
            ).astype(jnp.bfloat16)
            for k in range(2):
                half_ref[a // 2, pl.ds((j + k) * EDGE, EDGE), :] = both[
                    :, k * LANES : (k + 1) * LANES
                ]
    for j in range(0, rows // 2, 4):
        for k in range(2):
            full = lax.dot_general(
                far_ref[k],
                half_ref[k, pl.ds(j * EDGE, 4 * EDGE), :],
                NT,
                preferred_element_type=jnp.float32,
            )
            for half in range(2):
                unfold(full[half * EDGE : (half + 1) * EDGE], j, k, half, full_ref)

    def store(p, q, sums):
        part_ref[p, q] = sums

    inner([lambda q: slab(q, 1, 2), lambda q: slab(q, 1, 0)], full_ref, rows, store)


def main_kernel(
    scale,
    rows,
    part_ref,
    sides_ref,
    schip,
    gchip,
    sown,
    gown,
    score,
    gcore,
    out_ref,
    occ_ref,
    half_ref,
    full_ref,
):
    slab, green = readers(schip, gchip, sown, gown, score, gcore)
    none = jnp.zeros((EDGE, EDGE), jnp.bfloat16)
    near = [green(s, 2 - s)[:, :EDGE] for s in range(3)]
    mid = jnp.concatenate(near, 1)
    ends = jnp.concatenate(
        [
            jnp.concatenate([near[0], near[1], none, none], 1),
            jnp.concatenate([none, none, near[1], near[2]], 1),
        ],
        0,
    )
    used = ({0: 1, 1: 2}, {0: 0, 1: 1, 2: 2}, {1: 0, 2: 1})
    for s in range(3):
        for t in range(3):
            for half in range(2):
                at = pl.ds((half * 3 + s) * EDGE, EDGE)
                to = pl.ds(t * LANES, LANES)
                if t in used[s]:
                    o = green(s, used[s][t])[:, EDGE:]
                    occ_ref[at, to] = jnp.concatenate([none, o] if half else [o, none], 1)
                else:
                    occ_ref[at, to] = jnp.zeros((EDGE, LANES), jnp.bfloat16)

    for j in range(0, rows // 2, 2):
        own = [sides_ref[a, :, pl.ds(j * LANES, 2 * LANES)] for a in range(3)]
        both = jnp.dot(
            ends,
            jnp.concatenate(halves(slab, (0, 1), j) + [own[0], own[2]] + halves(slab, (2, 1), j), 0),
            preferred_element_type=jnp.float32,
        ).astype(jnp.bfloat16)
        middle = jnp.dot(
            mid,
            jnp.concatenate(halves(slab, (0, 2), j) + [own[1]] + halves(slab, (2, 0), j), 0),
            preferred_element_type=jnp.float32,
        ).astype(jnp.bfloat16)
        for t, piece in enumerate((both[:EDGE], middle, both[EDGE:])):
            for k in range(2):
                half_ref[pl.ds((j + k) * EDGE, EDGE), pl.ds(t * LANES, LANES)] = piece[
                    :, k * LANES : (k + 1) * LANES
                ]

    for j in range(0, rows // 2, 4):
        at = pl.ds(j * EDGE, 4 * EDGE)
        full = lax.dot_general(
            occ_ref[...],
            half_ref[at, :],
            NT,
            preferred_element_type=jnp.float32,
        )
        for half in range(2):
            for s in range(3):
                block = full[(half * 3 + s) * EDGE : (half * 3 + s + 1) * EDGE]
                unfold(block, j, s, half, full_ref)

    def store(p, q, sums):
        out_ref[p, q] = scale * (sums + part_ref[p, q])

    inner([lambda q, s=s: slab(q, s, 2 - s) for s in range(3)], full_ref, rows, store)


def body(integrals, occupied, virtual, imask, omask, vmask, count):
    total = integrals.shape[1]
    members = lax.axis_size("blk")
    order = block_order(members)
    works_on = [order.index(d) for d in range(members)]

    rows = pl.pallas_call(
        functools.partial(pack_kernel, works_on),
        out_shape=jax.ShapeDtypeStruct((members, 3 * HALF, LANES), jnp.bfloat16),
        in_specs=[pl.BlockSpec(memory_space=pl.ANY)] * 2,
        out_specs=pl.BlockSpec(memory_space=pl.ANY),
        scratch_shapes=[
            pltpu.VMEM((3, total, EDGE * EDGE), jnp.bfloat16),
            pltpu.VMEM((3, total), jnp.int32),
            pltpu.VMEM((3, total * PITCH, LANES), jnp.float32),
            pltpu.VMEM((members, 3 * HALF, LANES), jnp.bfloat16),
            pltpu.SemaphoreType.DMA((7,)),
        ],
        compiler_params=pltpu.CompilerParams(vmem_limit_bytes=63 * 1024 * 1024),
        name="pack",
    )(jnp.transpose(integrals[0], (1, 0, 2)), imask.T)
    greens, gchip = pl.pallas_call(
        functools.partial(prep_kernel, total),
        out_shape=(
            jax.ShapeDtypeStruct((6 * HALF, LANES), jnp.bfloat16),
            jax.ShapeDtypeStruct((4 * HALF, LANES), jnp.bfloat16),
        ),
        in_specs=[SMEM] * 3 + [VMEM] * 2,
        out_specs=(VMEM, VMEM),
        scratch_shapes=[pltpu.VMEM((2, 3 * PITCH, LANES), jnp.float32)],
        name="prep",
    )(omask.T, vmask.T, count, occupied[0], virtual[0])
    chip_next = [order[(j - 1 + 2 * (j % 2)) % members] for j in range(members)]
    gchip = lax.ppermute(gchip, "blk", list(enumerate(chip_next)))
    greens = lax.ppermute(greens, "blk", list(enumerate(order)))
    own = lax.all_to_all(rows, "blk", split_axis=0, concat_axis=0, tiled=True)
    own, greens, gchip = lax.optimization_barrier((own, greens, gchip))
    core_pairs = [(order[j], order[j + 1 - 2 * (j % 2)]) for j in range(members)]
    chip_pairs = list(zip(order, chip_next))
    to_chip = own[:, : 2 * HALF].reshape(-1, LANES)
    to_core = own[:, HALF:].reshape(-1, LANES)
    schip = lax.ppermute(to_chip, "blk", chip_pairs)
    score = lax.ppermute(to_core, "blk", core_pairs)
    gcore = lax.ppermute(greens[EDGE:], "blk", core_pairs)
    early, sides = pl.pallas_call(
        functools.partial(early_kernel, members),
        out_shape=(
            jax.ShapeDtypeStruct((members, members), jnp.float32),
            jax.ShapeDtypeStruct((3, EDGE, members // 2 * LANES), jnp.bfloat16),
        ),
        in_specs=[VMEM] * 2,
        out_specs=(VMEM, VMEM),
        scratch_shapes=[
            pltpu.VMEM((2, 2 * EDGE, LANES), jnp.bfloat16),
            pltpu.VMEM((2, members // 2 * EDGE, LANES), jnp.bfloat16),
            pltpu.VMEM((members, 2 * HALF, LANES), jnp.bfloat16),
        ],
        compiler_params=pltpu.CompilerParams(vmem_limit_bytes=24 * 1024 * 1024),
        name="early",
    )(own, greens)
    part = pl.pallas_call(
        functools.partial(main_kernel, 1.0 / math.sqrt(5 * EDGE * EDGE * total), members),
        out_shape=jax.ShapeDtypeStruct((members, members), jnp.float32),
        in_specs=[VMEM] * 8,
        out_specs=VMEM,
        scratch_shapes=[
            pltpu.VMEM((6 * EDGE, 3 * LANES), jnp.bfloat16),
            pltpu.VMEM((members // 2 * EDGE, 3 * LANES), jnp.bfloat16),
            pltpu.VMEM((members, 3 * HALF, LANES), jnp.bfloat16),
        ],
        compiler_params=pltpu.CompilerParams(vmem_limit_bytes=24 * 1024 * 1024),
        name="products",
    )(early, sides, schip, gchip, own, greens, score, gcore)
    mine = lax.all_to_all(part, "blk", split_axis=0, concat_axis=0, tiled=True)
    return jnp.sum(mine, axis=0, keepdims=True)


def solution(mesh):
    return jax.shard_map(
        body,
        mesh=mesh,
        in_specs=(
            P(("grp", "blk"), None, None, None),
            P(("grp", "blk"), None, None),
            P(("grp", "blk"), None, None),
            P(),
            P(),
            P(),
            P(),
        ),
        out_specs=P(("grp", "blk"), None),
        check_vma=False,
    )
```

```python
import functools
import math

import jax
import jax.numpy as jnp
from jax import lax
from jax.experimental import pallas as pl
from jax.experimental.pallas import tpu as pltpu
from jax.sharding import PartitionSpec as P

EDGE = 64
HALF = 32
LANES = 128
PITCH = 40
VMEM = pl.BlockSpec(memory_space=pltpu.VMEM)
SMEM = pl.BlockSpec(memory_space=pltpu.SMEM)
NT = (((1,), (1,)), ((), ()))


def block_order(count):
    if count == 16:
        chips = [3, 1, 0, 2, 4, 6, 7, 5]
        return [2 * chip + core for chip in chips for core in (0, 1)]
    return list(range(count))


def pack_kernel(works_on, x_hbm, imask_hbm, out_hbm, x_ref, imask_ref, rows_ref, out_ref, sems):
    blocks = x_ref.shape[1]
    copies = [pltpu.make_async_copy(x_hbm.at[a], x_ref.at[a], sems.at[a]) for a in range(3)]
    masks = pltpu.make_async_copy(imask_hbm, imask_ref, sems.at[3])
    masks.start()
    for copy in copies:
        copy.start()
    diagonal = lax.broadcasted_iota(jnp.int32, (blocks, blocks), 0) == lax.broadcasted_iota(
        jnp.int32, (blocks, blocks), 1
    )
    masks.wait()
    sent = []
    for a in (1, 0, 2):
        mask = jnp.where(diagonal, imask_ref[pl.ds(a, 1), :].astype(jnp.float32), 0.0)
        mask = jnp.broadcast_to(jnp.sum(mask, axis=1, keepdims=True), (blocks, LANES))
        copies[a].wait()
        for c in range(HALF):
            rows_ref[a, pl.ds(c, blocks, stride=PITCH), :] = (
                x_ref[a, :, c * LANES : (c + 1) * LANES].astype(jnp.float32) * mask
            )
        for d, b in enumerate(works_on):
            to = 2 - a if b % 2 else a
            out_ref[d, pl.ds(to * HALF, HALF), :] = rows_ref[a, pl.ds(b * PITCH, HALF), :].astype(
                jnp.bfloat16
            )
        for to in {0: (), 1: (1,), 2: (0, 2)}[a]:
            part = pl.ds(to * HALF, HALF)
            copy = pltpu.make_async_copy(
                out_ref.at[:, part, :], out_hbm.at[:, part, :], sems.at[4 + to]
            )
            copy.start()
            sent.append(copy)
    for copy in sent:
        copy.wait()


def prep_kernel(total, omask, vmask, count, occ_ref, vir_ref, out_ref, chip_ref, rows_ref):
    own = lax.axis_index("blk")
    for k, ref in enumerate((occ_ref, vir_ref)):
        for c in range(HALF):
            rows_ref[k, pl.ds(c, 3, stride=PITCH), :] = ref[
                :, c * LANES : (c + 1) * LANES
            ].astype(jnp.float32)
    lane = lax.broadcasted_iota(jnp.int32, (HALF, LANES), 1)
    row = lax.broadcasted_iota(jnp.int32, (HALF, LANES), 0)
    left = lane < EDGE
    col = jnp.where(left, lane, lane - EDGE)
    keep = [(2 * row + par < count[own]).astype(jnp.float32) for par in range(2)]
    vir, occ = [], []
    for a in range(3):
        used = (col < count[lax.rem(own + (total + a - 1), total)]).astype(jnp.float32)
        v = rows_ref[1, pl.ds(a * PITCH, HALF), :] * (used * vmask[a, own].astype(jnp.float32))
        vir += [v * keep[0], pltpu.roll(v, EDGE, 1) * keep[1]]
        o = rows_ref[0, pl.ds(a * PITCH, HALF), :] * (used * omask[a, own].astype(jnp.float32))
        occ.append((pltpu.roll(o, EDGE, 1) * keep[0], o * keep[1]))
    vir += [jnp.zeros((HALF, LANES), jnp.float32)] * 2
    first = jnp.concatenate(vir[:4], 0).T[:EDGE]
    second = jnp.concatenate(vir[4:], 0).T[:EDGE]
    odd = lax.rem(own, 2)
    for a, turned in enumerate((first, pltpu.roll(first, EDGE, 1), second)):
        at = pl.multiple_of((a + odd * (2 - 2 * a)) * EDGE, EDGE)
        for par in range(2):
            out_ref[pl.ds(at + par * HALF, HALF), :] = jnp.where(
                left, turned[par * HALF : (par + 1) * HALF], occ[a][par]
            ).astype(jnp.bfloat16)
    chip_ref[...] = out_ref[pl.ds(0, 2 * EDGE), :]


def halves(slab, rows_at, j):
    even, odd = [], []
    for k in range(j, j + 2):
        one, two = slab(2 * k, *rows_at), slab(2 * k + 1, *rows_at)
        even.append(jnp.concatenate([one[:, :EDGE], two[:, :EDGE]], 1))
        odd.append(jnp.concatenate([one[:, EDGE:], two[:, EDGE:]], 1))
    return [jnp.concatenate(even, 1), jnp.concatenate(odd, 1)]


def unfold(block, members, g, full_ref):
    block = block.astype(jnp.bfloat16)
    for k, q in enumerate(members):
        lanes = slice(k * EDGE, (k + 1) * EDGE)
        full_ref[q, pl.ds(g * HALF, HALF), :] = jnp.concatenate(
            [block[:HALF, lanes], block[HALF:, lanes]], 1
        )


def inner(slabs, full_ref, rows, store):
    group = 16
    span = group * 16
    ri = lax.broadcasted_iota(jnp.int32, (span, span), 0)
    ci = lax.broadcasted_iota(jnp.int32, (span, span), 1)
    same = lax.rem(ri, 16) == lax.rem(ci, 16)
    pick = (
        lax.broadcasted_iota(jnp.int32, (span, group), 0) // 16
        == lax.broadcasted_iota(jnp.int32, (span, group), 1)
    ).astype(jnp.float32)
    for p in range(0, rows, group):
        for q in range(0, rows, group):
            acc = None
            for g, slab in enumerate(slabs):
                lhs = [slab(k) for k in range(p, p + group)]
                lhs = [jnp.concatenate([x[:16], x[16:]], 1) for x in lhs]
                rhs = [
                    full_ref[pl.ds(q, group), pl.ds(g * HALF + c * 16, 16), :].reshape(span, LANES)
                    for c in range(2)
                ]
                one = lax.dot_general(
                    jnp.concatenate(lhs, 0),
                    jnp.concatenate(rhs, 1),
                    NT,
                    preferred_element_type=jnp.float32,
                )
                acc = one if acc is None else acc + one
            kept = jnp.where(same, acc, 0.0).reshape(group, 16, span)
            store(
                pl.ds(p, group),
                pl.ds(q, group),
                jnp.dot(
                    jnp.sum(kept, axis=1),
                    pick,
                    preferred_element_type=jnp.float32,
                    precision=lax.Precision.HIGHEST,
                ),
            )


def readers(schip, gchip, sown, gown, score, gcore):
    pair = 2 * HALF

    def slab(q, s, a):
        if s == 0:
            return schip[pl.ds(q * pair + (2 - a) * HALF, HALF), :]
        if s == 2:
            return score[pl.ds(q * pair + (1 - a) * HALF, HALF), :]
        return sown[q, pl.ds(a * HALF, HALF), :]

    def green(s, a):
        if s == 0:
            return gchip[pl.ds((2 - a) * EDGE, EDGE), :]
        if s == 2:
            return gcore[pl.ds((1 - a) * EDGE, EDGE), :]
        return gown[pl.ds(a * EDGE, EDGE), :]

    return slab, green


def early_kernel(rows, sown, gown, part_ref, sides_ref, far_ref, half_ref, full_ref):
    slab, green = readers(None, None, sown, gown, None, None)
    none = jnp.zeros((EDGE, EDGE), jnp.bfloat16)
    for k in range(2):
        o = green(1, 2 * k)[:, EDGE:]
        far_ref[k] = jnp.concatenate(
            [jnp.concatenate([o, none], 1), jnp.concatenate([none, o], 1)], 0
        )
    for j in range(0, rows // 2, 2):
        for a in range(3):
            side = jnp.concatenate(halves(slab, (1, a), j), 0)
            sides_ref[a, :, pl.ds(j * LANES, 2 * LANES)] = side
            if a == 1:
                continue
            both = jnp.dot(
                green(1, 2 - a)[:, :EDGE], side, preferred_element_type=jnp.float32
            ).astype(jnp.bfloat16)
            for k in range(2):
                half_ref[a // 2, pl.ds((j + k) * EDGE, EDGE), :] = both[
                    :, k * LANES : (k + 1) * LANES
                ]
    for j in range(0, rows // 2, 4):
        for k in range(2):
            full = lax.dot_general(
                far_ref[k],
                half_ref[k, pl.ds(j * EDGE, 4 * EDGE), :],
                NT,
                preferred_element_type=jnp.float32,
            )
            for half in range(2):
                those = [2 * (j + n) + half for n in range(4)]
                unfold(full[half * EDGE : (half + 1) * EDGE], those, k, full_ref)

    def store(p, q, sums):
        part_ref[p, q] = sums

    inner([lambda q: slab(q, 1, 2), lambda q: slab(q, 1, 0)], full_ref, rows, store)


def main_kernel(
    scale,
    rows,
    part_ref,
    sides_ref,
    schip,
    gchip,
    sown,
    gown,
    score,
    gcore,
    out_ref,
    occ_ref,
    half_ref,
    full_ref,
):
    slab, green = readers(schip, gchip, sown, gown, score, gcore)
    none = jnp.zeros((EDGE, EDGE), jnp.bfloat16)
    near = [green(s, 2 - s)[:, :EDGE] for s in range(3)]
    mid = jnp.concatenate(near, 1)
    ends = jnp.concatenate(
        [
            jnp.concatenate([near[0], near[1], none, none], 1),
            jnp.concatenate([none, none, near[1], near[2]], 1),
        ],
        0,
    )
    used = ({0: 1, 1: 2}, {0: 0, 1: 1, 2: 2}, {1: 0, 2: 1})
    for s in range(3):
        o = [green(s, used[s][t])[:, EDGE:] if t in used[s] else none for t in range(3)]
        occ_ref[pl.ds(s * EDGE, EDGE), :] = jnp.concatenate(o + [none], 1)

    for j in range(0, rows // 2, 2):
        own = [sides_ref[a, :, pl.ds(j * LANES, 2 * LANES)] for a in range(3)]
        both = jnp.dot(
            ends,
            jnp.concatenate(halves(slab, (0, 1), j) + [own[0], own[2]] + halves(slab, (2, 1), j), 0),
            preferred_element_type=jnp.float32,
        ).astype(jnp.bfloat16)
        middle = jnp.dot(
            mid,
            jnp.concatenate(halves(slab, (0, 2), j) + [own[1]] + halves(slab, (2, 0), j), 0),
            preferred_element_type=jnp.float32,
        ).astype(jnp.bfloat16)
        pieces = (both[:EDGE], middle, both[EDGE:])
        for k in range(4):
            half_ref[pl.ds((2 * j + k) * EDGE, EDGE), :] = jnp.concatenate(
                [piece[:, k * EDGE : (k + 1) * EDGE] for piece in pieces] + [none], 1
            )

    for q in range(0, rows, 4):
        full = lax.dot_general(
            occ_ref[...],
            half_ref[pl.ds(q * EDGE, 4 * EDGE), :],
            NT,
            preferred_element_type=jnp.float32,
        )
        for s in range(3):
            unfold(full[s * EDGE : (s + 1) * EDGE], (q, q + 1, q + 2, q + 3), s, full_ref)

    def store(p, q, sums):
        out_ref[p, q] = scale * (sums + part_ref[p, q])

    inner([lambda q, s=s: slab(q, s, 2 - s) for s in range(3)], full_ref, rows, store)


def body(integrals, occupied, virtual, imask, omask, vmask, count):
    total = integrals.shape[1]
    members = lax.axis_size("blk")
    order = block_order(members)
    works_on = [order.index(d) for d in range(members)]

    rows = pl.pallas_call(
        functools.partial(pack_kernel, works_on),
        out_shape=jax.ShapeDtypeStruct((members, 3 * HALF, LANES), jnp.bfloat16),
        in_specs=[pl.BlockSpec(memory_space=pl.ANY)] * 2,
        out_specs=pl.BlockSpec(memory_space=pl.ANY),
        scratch_shapes=[
            pltpu.VMEM((3, total, EDGE * EDGE), jnp.bfloat16),
            pltpu.VMEM((3, total), jnp.int32),
            pltpu.VMEM((3, total * PITCH, LANES), jnp.float32),
            pltpu.VMEM((members, 3 * HALF, LANES), jnp.bfloat16),
            pltpu.SemaphoreType.DMA((7,)),
        ],
        compiler_params=pltpu.CompilerParams(vmem_limit_bytes=63 * 1024 * 1024),
        name="pack",
    )(jnp.transpose(integrals[0], (1, 0, 2)), imask.T)
    greens, gchip = pl.pallas_call(
        functools.partial(prep_kernel, total),
        out_shape=(
            jax.ShapeDtypeStruct((6 * HALF, LANES), jnp.bfloat16),
            jax.ShapeDtypeStruct((4 * HALF, LANES), jnp.bfloat16),
        ),
        in_specs=[SMEM] * 3 + [VMEM] * 2,
        out_specs=(VMEM, VMEM),
        scratch_shapes=[pltpu.VMEM((2, 3 * PITCH, LANES), jnp.float32)],
        name="prep",
    )(omask.T, vmask.T, count, occupied[0], virtual[0])
    chip_next = [order[(j - 1 + 2 * (j % 2)) % members] for j in range(members)]
    gchip = lax.ppermute(gchip, "blk", list(enumerate(chip_next)))
    greens = lax.ppermute(greens, "blk", list(enumerate(order)))
    own = lax.all_to_all(rows, "blk", split_axis=0, concat_axis=0, tiled=True)
    own, greens, gchip = lax.optimization_barrier((own, greens, gchip))
    core_pairs = [(order[j], order[j + 1 - 2 * (j % 2)]) for j in range(members)]
    chip_pairs = list(zip(order, chip_next))
    to_chip = own[:, : 2 * HALF].reshape(-1, LANES)
    to_core = own[:, HALF:].reshape(-1, LANES)
    schip = lax.ppermute(to_chip, "blk", chip_pairs)
    score = lax.ppermute(to_core, "blk", core_pairs)
    gcore = lax.ppermute(greens[EDGE:], "blk", core_pairs)
    early, sides = pl.pallas_call(
        functools.partial(early_kernel, members),
        out_shape=(
            jax.ShapeDtypeStruct((members, members), jnp.float32),
            jax.ShapeDtypeStruct((3, EDGE, members // 2 * LANES), jnp.bfloat16),
        ),
        in_specs=[VMEM] * 2,
        out_specs=(VMEM, VMEM),
        scratch_shapes=[
            pltpu.VMEM((2, 2 * EDGE, LANES), jnp.bfloat16),
            pltpu.VMEM((2, members // 2 * EDGE, LANES), jnp.bfloat16),
            pltpu.VMEM((members, 2 * HALF, LANES), jnp.bfloat16),
        ],
        compiler_params=pltpu.CompilerParams(vmem_limit_bytes=24 * 1024 * 1024),
        name="early",
    )(own, greens)
    part = pl.pallas_call(
        functools.partial(main_kernel, 1.0 / math.sqrt(5 * EDGE * EDGE * total), members),
        out_shape=jax.ShapeDtypeStruct((members, members), jnp.float32),
        in_specs=[VMEM] * 8,
        out_specs=VMEM,
        scratch_shapes=[
            pltpu.VMEM((3 * EDGE, 2 * LANES), jnp.bfloat16),
            pltpu.VMEM((members * EDGE, 2 * LANES), jnp.bfloat16),
            pltpu.VMEM((members, 3 * HALF, LANES), jnp.bfloat16),
        ],
        compiler_params=pltpu.CompilerParams(vmem_limit_bytes=24 * 1024 * 1024),
        name="products",
    )(early, sides, schip, gchip, own, greens, score, gcore)
    mine = lax.all_to_all(part, "blk", split_axis=0, concat_axis=0, tiled=True)
    return jnp.sum(mine, axis=0, keepdims=True)


def solution(mesh):
    return jax.shard_map(
        body,
        mesh=mesh,
        in_specs=(
            P(("grp", "blk"), None, None, None),
            P(("grp", "blk"), None, None),
            P(("grp", "blk"), None, None),
            P(),
            P(),
            P(),
            P(),
        ),
        out_specs=P(("grp", "blk"), None),
        check_vma=False,
    )
```

```python
import functools
import math

import jax
import jax.numpy as jnp
from jax import lax
from jax.experimental import pallas as pl
from jax.experimental.pallas import tpu as pltpu
from jax.sharding import PartitionSpec as P

EDGE = 64
HALF = 32
LANES = 128
PITCH = 40
VMEM = pl.BlockSpec(memory_space=pltpu.VMEM)
SMEM = pl.BlockSpec(memory_space=pltpu.SMEM)
NT = (((1,), (1,)), ((), ()))


def block_order(count):
    if count == 16:
        chips = [3, 1, 0, 2, 4, 6, 7, 5]
        return [2 * chip + core for chip in chips for core in (0, 1)]
    return list(range(count))


def pack_kernel(works_on, x_hbm, imask_hbm, out_hbm, x_ref, imask_ref, rows_ref, out_ref, sems):
    blocks = x_ref.shape[1]
    copies = [pltpu.make_async_copy(x_hbm.at[a], x_ref.at[a], sems.at[a]) for a in range(3)]
    masks = pltpu.make_async_copy(imask_hbm, imask_ref, sems.at[3])
    for a in (1, 0, 2):
        copies[a].start()
        if a == 1:
            masks.start()
    diagonal = lax.broadcasted_iota(jnp.int32, (blocks, blocks), 0) == lax.broadcasted_iota(
        jnp.int32, (blocks, blocks), 1
    )
    masks.wait()
    sent = []
    for a in (1, 0, 2):
        mask = jnp.where(diagonal, imask_ref[pl.ds(a, 1), :].astype(jnp.float32), 0.0)
        mask = jnp.broadcast_to(jnp.sum(mask, axis=1, keepdims=True), (blocks, LANES))
        copies[a].wait()
        for c in range(HALF):
            rows_ref[a, pl.ds(c, blocks, stride=PITCH), :] = (
                x_ref[a, :, c * LANES : (c + 1) * LANES].astype(jnp.float32) * mask
            )
        for d, b in enumerate(works_on):
            to = 2 - a if b % 2 else a
            out_ref[d, pl.ds(to * HALF, HALF), :] = rows_ref[a, pl.ds(b * PITCH, HALF), :].astype(
                jnp.bfloat16
            )
        for to in {0: (), 1: (1,), 2: (0, 2)}[a]:
            part = pl.ds(to * HALF, HALF)
            copy = pltpu.make_async_copy(
                out_ref.at[:, part, :], out_hbm.at[:, part, :], sems.at[4 + to]
            )
            copy.start()
            sent.append(copy)
    for copy in sent:
        copy.wait()


def prep_kernel(total, omask, vmask, count, occ_ref, vir_ref, out_ref, chip_ref, rows_ref):
    own = lax.axis_index("blk")
    for k, ref in enumerate((occ_ref, vir_ref)):
        for c in range(HALF):
            rows_ref[k, pl.ds(c, 3, stride=PITCH), :] = ref[
                :, c * LANES : (c + 1) * LANES
            ].astype(jnp.float32)
    lane = lax.broadcasted_iota(jnp.int32, (HALF, LANES), 1)
    row = lax.broadcasted_iota(jnp.int32, (HALF, LANES), 0)
    left = lane < EDGE
    col = jnp.where(left, lane, lane - EDGE)
    keep = [(2 * row + par < count[own]).astype(jnp.float32) for par in range(2)]
    vir, occ = [], []
    for a in range(3):
        used = (col < count[lax.rem(own + (total + a - 1), total)]).astype(jnp.float32)
        v = rows_ref[1, pl.ds(a * PITCH, HALF), :] * (used * vmask[a, own].astype(jnp.float32))
        vir += [v * keep[0], pltpu.roll(v, EDGE, 1) * keep[1]]
        o = rows_ref[0, pl.ds(a * PITCH, HALF), :] * (used * omask[a, own].astype(jnp.float32))
        occ.append((pltpu.roll(o, EDGE, 1) * keep[0], o * keep[1]))
    vir += [jnp.zeros((HALF, LANES), jnp.float32)] * 2
    first = jnp.concatenate(vir[:4], 0).T[:EDGE]
    second = jnp.concatenate(vir[4:], 0).T[:EDGE]
    odd = lax.rem(own, 2)
    for a, turned in enumerate((first, pltpu.roll(first, EDGE, 1), second)):
        at = pl.multiple_of((a + odd * (2 - 2 * a)) * EDGE, EDGE)
        for par in range(2):
            out_ref[pl.ds(at + par * HALF, HALF), :] = jnp.where(
                left, turned[par * HALF : (par + 1) * HALF], occ[a][par]
            ).astype(jnp.bfloat16)
    chip_ref[...] = out_ref[pl.ds(0, 2 * EDGE), :]


def halves(slab, rows_at, j):
    even, odd = [], []
    for k in range(j, j + 2):
        one, two = slab(2 * k, *rows_at), slab(2 * k + 1, *rows_at)
        even.append(jnp.concatenate([one[:, :EDGE], two[:, :EDGE]], 1))
        odd.append(jnp.concatenate([one[:, EDGE:], two[:, EDGE:]], 1))
    return [jnp.concatenate(even, 1), jnp.concatenate(odd, 1)]


def unfold(block, members, g, full_ref):
    block = block.astype(jnp.bfloat16)
    for k, q in enumerate(members):
        lanes = slice(k * EDGE, (k + 1) * EDGE)
        full_ref[q, pl.ds(g * HALF, HALF), :] = jnp.concatenate(
            [block[:HALF, lanes], block[HALF:, lanes]], 1
        )


def inner(slabs, full_ref, rows, store):
    group = 16
    span = group * 16
    ri = lax.broadcasted_iota(jnp.int32, (span, span), 0)
    ci = lax.broadcasted_iota(jnp.int32, (span, span), 1)
    same = lax.rem(ri, 16) == lax.rem(ci, 16)
    pick = (
        lax.broadcasted_iota(jnp.int32, (span, group), 0) // 16
        == lax.broadcasted_iota(jnp.int32, (span, group), 1)
    ).astype(jnp.float32)
    for p in range(0, rows, group):
        for q in range(0, rows, group):
            acc = None
            for g, slab in enumerate(slabs):
                lhs = [slab(k) for k in range(p, p + group)]
                lhs = [jnp.concatenate([x[:16], x[16:]], 1) for x in lhs]
                rhs = [
                    full_ref[pl.ds(q, group), pl.ds(g * HALF + c * 16, 16), :].reshape(span, LANES)
                    for c in range(2)
                ]
                one = lax.dot_general(
                    jnp.concatenate(lhs, 0),
                    jnp.concatenate(rhs, 1),
                    NT,
                    preferred_element_type=jnp.float32,
                )
                acc = one if acc is None else acc + one
            kept = jnp.where(same, acc, 0.0).reshape(group, 16, span)
            store(
                pl.ds(p, group),
                pl.ds(q, group),
                jnp.dot(
                    jnp.sum(kept, axis=1),
                    pick,
                    preferred_element_type=jnp.float32,
                    precision=lax.Precision.HIGHEST,
                ),
            )


def readers(schip, gchip, sown, gown, score, gcore):
    pair = 2 * HALF

    def slab(q, s, a):
        if s == 0:
            return schip[pl.ds(q * pair + (2 - a) * HALF, HALF), :]
        if s == 2:
            return score[pl.ds(q * pair + (1 - a) * HALF, HALF), :]
        return sown[q, pl.ds(a * HALF, HALF), :]

    def green(s, a):
        if s == 0:
            return gchip[pl.ds((2 - a) * EDGE, EDGE), :]
        if s == 2:
            return gcore[pl.ds((1 - a) * EDGE, EDGE), :]
        return gown[pl.ds(a * EDGE, EDGE), :]

    return slab, green


def early_kernel(rows, sown, gown, part_ref, sides_ref, far_ref, half_ref, full_ref):
    slab, green = readers(None, None, sown, gown, None, None)
    none = jnp.zeros((EDGE, EDGE), jnp.bfloat16)
    for k in range(2):
        o = green(1, 2 * k)[:, EDGE:]
        far_ref[k] = jnp.concatenate(
            [jnp.concatenate([o, none], 1), jnp.concatenate([none, o], 1)], 0
        )
    for j in range(0, rows // 2, 2):
        for a in range(3):
            side = jnp.concatenate(halves(slab, (1, a), j), 0)
            sides_ref[a, :, pl.ds(j * LANES, 2 * LANES)] = side
            if a == 1:
                continue
            both = jnp.dot(
                green(1, 2 - a)[:, :EDGE], side, preferred_element_type=jnp.float32
            ).astype(jnp.bfloat16)
            for k in range(2):
                half_ref[a // 2, pl.ds((j + k) * EDGE, EDGE), :] = both[
                    :, k * LANES : (k + 1) * LANES
                ]
    for j in range(0, rows // 2, 4):
        for k in range(2):
            full = lax.dot_general(
                far_ref[k],
                half_ref[k, pl.ds(j * EDGE, 4 * EDGE), :],
                NT,
                preferred_element_type=jnp.float32,
            )
            for half in range(2):
                those = [2 * (j + n) + half for n in range(4)]
                unfold(full[half * EDGE : (half + 1) * EDGE], those, k, full_ref)

    def store(p, q, sums):
        part_ref[p, q] = sums

    inner([lambda q: slab(q, 1, 2), lambda q: slab(q, 1, 0)], full_ref, rows, store)


def main_kernel(
    scale,
    rows,
    part_ref,
    sides_ref,
    schip,
    gchip,
    sown,
    gown,
    score,
    gcore,
    out_ref,
    occ_ref,
    half_ref,
    full_ref,
):
    slab, green = readers(schip, gchip, sown, gown, score, gcore)
    none = jnp.zeros((EDGE, EDGE), jnp.bfloat16)
    near = [green(s, 2 - s)[:, :EDGE] for s in range(3)]
    mid = jnp.concatenate(near, 1)
    ends = jnp.concatenate(
        [
            jnp.concatenate([near[0], near[1], none, none], 1),
            jnp.concatenate([none, none, near[1], near[2]], 1),
        ],
        0,
    )
    used = ({0: 1, 1: 2}, {0: 0, 1: 1, 2: 2}, {1: 0, 2: 1})
    for s in range(3):
        o = [green(s, used[s][t])[:, EDGE:] if t in used[s] else none for t in range(3)]
        occ_ref[pl.ds(s * EDGE, EDGE), :] = jnp.concatenate(o + [none], 1)

    for j in range(0, rows // 2, 2):
        own = [sides_ref[a, :, pl.ds(j * LANES, 2 * LANES)] for a in range(3)]
        both = jnp.dot(
            ends,
            jnp.concatenate(halves(slab, (0, 1), j) + [own[0], own[2]] + halves(slab, (2, 1), j), 0),
            preferred_element_type=jnp.float32,
        ).astype(jnp.bfloat16)
        middle = jnp.dot(
            mid,
            jnp.concatenate(halves(slab, (0, 2), j) + [own[1]] + halves(slab, (2, 0), j), 0),
            preferred_element_type=jnp.float32,
        ).astype(jnp.bfloat16)
        pieces = (both[:EDGE], middle, both[EDGE:])
        for k in range(4):
            half_ref[pl.ds((2 * j + k) * EDGE, EDGE), :] = jnp.concatenate(
                [piece[:, k * EDGE : (k + 1) * EDGE] for piece in pieces] + [none], 1
            )

    for q in range(0, rows, 4):
        full = lax.dot_general(
            occ_ref[...],
            half_ref[pl.ds(q * EDGE, 4 * EDGE), :],
            NT,
            preferred_element_type=jnp.float32,
        )
        for s in range(3):
            unfold(full[s * EDGE : (s + 1) * EDGE], (q, q + 1, q + 2, q + 3), s, full_ref)

    def store(p, q, sums):
        out_ref[p, q] = scale * (sums + part_ref[p, q])

    inner([lambda q, s=s: slab(q, s, 2 - s) for s in range(3)], full_ref, rows, store)


def body(integrals, occupied, virtual, imask, omask, vmask, count):
    total = integrals.shape[1]
    members = lax.axis_size("blk")
    order = block_order(members)
    works_on = [order.index(d) for d in range(members)]

    rows = pl.pallas_call(
        functools.partial(pack_kernel, works_on),
        out_shape=jax.ShapeDtypeStruct((members, 3 * HALF, LANES), jnp.bfloat16),
        in_specs=[pl.BlockSpec(memory_space=pl.ANY)] * 2,
        out_specs=pl.BlockSpec(memory_space=pl.ANY),
        scratch_shapes=[
            pltpu.VMEM((3, total, EDGE * EDGE), jnp.bfloat16),
            pltpu.VMEM((3, total), jnp.int32),
            pltpu.VMEM((3, total * PITCH, LANES), jnp.float32),
            pltpu.VMEM((members, 3 * HALF, LANES), jnp.bfloat16),
            pltpu.SemaphoreType.DMA((7,)),
        ],
        compiler_params=pltpu.CompilerParams(vmem_limit_bytes=63 * 1024 * 1024),
        name="pack",
    )(jnp.transpose(integrals[0], (1, 0, 2)), imask.T)
    greens, gchip = pl.pallas_call(
        functools.partial(prep_kernel, total),
        out_shape=(
            jax.ShapeDtypeStruct((6 * HALF, LANES), jnp.bfloat16),
            jax.ShapeDtypeStruct((4 * HALF, LANES), jnp.bfloat16),
        ),
        in_specs=[SMEM] * 3 + [VMEM] * 2,
        out_specs=(VMEM, VMEM),
        scratch_shapes=[pltpu.VMEM((2, 3 * PITCH, LANES), jnp.float32)],
        name="prep",
    )(omask.T, vmask.T, count, occupied[0], virtual[0])
    chip_next = [order[(j - 1 + 2 * (j % 2)) % members] for j in range(members)]
    gchip = lax.ppermute(gchip, "blk", list(enumerate(chip_next)))
    greens = lax.ppermute(greens, "blk", list(enumerate(order)))
    own = lax.all_to_all(rows, "blk", split_axis=0, concat_axis=0, tiled=True)
    own, greens, gchip = lax.optimization_barrier((own, greens, gchip))
    core_pairs = [(order[j], order[j + 1 - 2 * (j % 2)]) for j in range(members)]
    chip_pairs = list(zip(order, chip_next))
    to_chip = own[:, : 2 * HALF].reshape(-1, LANES)
    to_core = own[:, HALF:].reshape(-1, LANES)
    schip = lax.ppermute(to_chip, "blk", chip_pairs)
    score = lax.ppermute(to_core, "blk", core_pairs)
    gcore = lax.ppermute(greens[EDGE:], "blk", core_pairs)
    early, sides = pl.pallas_call(
        functools.partial(early_kernel, members),
        out_shape=(
            jax.ShapeDtypeStruct((members, members), jnp.float32),
            jax.ShapeDtypeStruct((3, EDGE, members // 2 * LANES), jnp.bfloat16),
        ),
        in_specs=[VMEM] * 2,
        out_specs=(VMEM, VMEM),
        scratch_shapes=[
            pltpu.VMEM((2, 2 * EDGE, LANES), jnp.bfloat16),
            pltpu.VMEM((2, members // 2 * EDGE, LANES), jnp.bfloat16),
            pltpu.VMEM((members, 2 * HALF, LANES), jnp.bfloat16),
        ],
        compiler_params=pltpu.CompilerParams(vmem_limit_bytes=24 * 1024 * 1024),
        name="early",
    )(own, greens)
    part = pl.pallas_call(
        functools.partial(main_kernel, 1.0 / math.sqrt(5 * EDGE * EDGE * total), members),
        out_shape=jax.ShapeDtypeStruct((members, members), jnp.float32),
        in_specs=[VMEM] * 8,
        out_specs=VMEM,
        scratch_shapes=[
            pltpu.VMEM((3 * EDGE, 2 * LANES), jnp.bfloat16),
            pltpu.VMEM((members * EDGE, 2 * LANES), jnp.bfloat16),
            pltpu.VMEM((members, 3 * HALF, LANES), jnp.bfloat16),
        ],
        compiler_params=pltpu.CompilerParams(vmem_limit_bytes=24 * 1024 * 1024),
        name="products",
    )(early, sides, schip, gchip, own, greens, score, gcore)
    mine = lax.all_to_all(part, "blk", split_axis=0, concat_axis=0, tiled=True)
    return jnp.sum(mine, axis=0, keepdims=True)


def solution(mesh):
    return jax.shard_map(
        body,
        mesh=mesh,
        in_specs=(
            P(("grp", "blk"), None, None, None),
            P(("grp", "blk"), None, None),
            P(("grp", "blk"), None, None),
            P(),
            P(),
            P(),
            P(),
        ),
        out_specs=P(("grp", "blk"), None),
        check_vma=False,
    )
```

```python
import functools
import math

import jax
import jax.numpy as jnp
from jax import lax
from jax.experimental import pallas as pl
from jax.experimental.pallas import tpu as pltpu
from jax.sharding import PartitionSpec as P

EDGE = 64
HALF = 32
LANES = 128
PITCH = 40
VMEM = pl.BlockSpec(memory_space=pltpu.VMEM)
SMEM = pl.BlockSpec(memory_space=pltpu.SMEM)
NT = (((1,), (1,)), ((), ()))


def block_order(count):
    if count == 16:
        chips = [3, 1, 0, 2, 4, 6, 7, 5]
        return [2 * chip + core for chip in chips for core in (0, 1)]
    return list(range(count))


def pack_kernel(works_on, x_hbm, imask_hbm, out_hbm, x_ref, imask_ref, rows_ref, out_ref, sems):
    blocks = x_ref.shape[1]
    cut = HALF // 2 * LANES
    copies = [
        [
            pltpu.make_async_copy(
                x_hbm.at[a, :, pl.ds(k * cut, cut)], x_ref.at[a, :, pl.ds(k * cut, cut)], sems.at[7 + 2 * a + k]
            )
            for k in range(2)
        ]
        for a in range(3)
    ]
    masks = pltpu.make_async_copy(imask_hbm, imask_ref, sems.at[3])
    masks.start()
    for a in (1, 0, 2):
        for copy in copies[a]:
            copy.start()
    diagonal = lax.broadcasted_iota(jnp.int32, (blocks, blocks), 0) == lax.broadcasted_iota(
        jnp.int32, (blocks, blocks), 1
    )
    masks.wait()
    sent = []
    for a in (1, 0, 2):
        mask = jnp.where(diagonal, imask_ref[pl.ds(a, 1), :].astype(jnp.float32), 0.0)
        mask = jnp.broadcast_to(jnp.sum(mask, axis=1, keepdims=True), (blocks, LANES))
        for c in range(HALF):
            if c % (HALF // 2) == 0:
                copies[a][c // (HALF // 2)].wait()
            rows_ref[a, pl.ds(c, blocks, stride=PITCH), :] = (
                x_ref[a, :, c * LANES : (c + 1) * LANES].astype(jnp.float32) * mask
            )
        for d, b in enumerate(works_on):
            to = 2 - a if b % 2 else a
            out_ref[d, pl.ds(to * HALF, HALF), :] = rows_ref[a, pl.ds(b * PITCH, HALF), :].astype(
                jnp.bfloat16
            )
        for to in {0: (), 1: (1,), 2: (0, 2)}[a]:
            part = pl.ds(to * HALF, HALF)
            copy = pltpu.make_async_copy(
                out_ref.at[:, part, :], out_hbm.at[:, part, :], sems.at[4 + to]
            )
            copy.start()
            sent.append(copy)
    for copy in sent:
        copy.wait()


def prep_kernel(total, omask, vmask, count, occ_ref, vir_ref, out_ref, chip_ref, rows_ref):
    own = lax.axis_index("blk")
    for k, ref in enumerate((occ_ref, vir_ref)):
        for c in range(HALF):
            rows_ref[k, pl.ds(c, 3, stride=PITCH), :] = ref[
                :, c * LANES : (c + 1) * LANES
            ].astype(jnp.float32)
    lane = lax.broadcasted_iota(jnp.int32, (HALF, LANES), 1)
    row = lax.broadcasted_iota(jnp.int32, (HALF, LANES), 0)
    left = lane < EDGE
    col = jnp.where(left, lane, lane - EDGE)
    keep = [(2 * row + par < count[own]).astype(jnp.float32) for par in range(2)]
    vir, occ = [], []
    for a in range(3):
        used = (col < count[lax.rem(own + (total + a - 1), total)]).astype(jnp.float32)
        v = rows_ref[1, pl.ds(a * PITCH, HALF), :] * (used * vmask[a, own].astype(jnp.float32))
        vir += [v * keep[0], pltpu.roll(v, EDGE, 1) * keep[1]]
        o = rows_ref[0, pl.ds(a * PITCH, HALF), :] * (used * omask[a, own].astype(jnp.float32))
        occ.append((pltpu.roll(o, EDGE, 1) * keep[0], o * keep[1]))
    vir += [jnp.zeros((HALF, LANES), jnp.float32)] * 2
    first = jnp.concatenate(vir[:4], 0).T[:EDGE]
    second = jnp.concatenate(vir[4:], 0).T[:EDGE]
    odd = lax.rem(own, 2)
    for a, turned in enumerate((first, pltpu.roll(first, EDGE, 1), second)):
        at = pl.multiple_of((a + odd * (2 - 2 * a)) * EDGE, EDGE)
        for par in range(2):
            out_ref[pl.ds(at + par * HALF, HALF), :] = jnp.where(
                left, turned[par * HALF : (par + 1) * HALF], occ[a][par]
            ).astype(jnp.bfloat16)
    chip_ref[...] = out_ref[pl.ds(0, 2 * EDGE), :]


def halves(slab, rows_at, j):
    even, odd = [], []
    for k in range(j, j + 2):
        one, two = slab(2 * k, *rows_at), slab(2 * k + 1, *rows_at)
        even.append(jnp.concatenate([one[:, :EDGE], two[:, :EDGE]], 1))
        odd.append(jnp.concatenate([one[:, EDGE:], two[:, EDGE:]], 1))
    return [jnp.concatenate(even, 1), jnp.concatenate(odd, 1)]


def unfold(block, members, g, full_ref):
    block = block.astype(jnp.bfloat16)
    for k, q in enumerate(members):
        lanes = slice(k * EDGE, (k + 1) * EDGE)
        full_ref[q, pl.ds(g * HALF, HALF), :] = jnp.concatenate(
            [block[:HALF, lanes], block[HALF:, lanes]], 1
        )


def inner(slabs, full_ref, rows, store):
    group = 16
    span = group * 16
    ri = lax.broadcasted_iota(jnp.int32, (span, span), 0)
    ci = lax.broadcasted_iota(jnp.int32, (span, span), 1)
    same = lax.rem(ri, 16) == lax.rem(ci, 16)
    pick = (
        lax.broadcasted_iota(jnp.int32, (span, group), 0) // 16
        == lax.broadcasted_iota(jnp.int32, (span, group), 1)
    ).astype(jnp.float32)
    for p in range(0, rows, group):
        for q in range(0, rows, group):
            acc = None
            for g, slab in enumerate(slabs):
                lhs = [slab(k) for k in range(p, p + group)]
                lhs = [jnp.concatenate([x[:16], x[16:]], 1) for x in lhs]
                rhs = [
                    full_ref[pl.ds(q, group), pl.ds(g * HALF + c * 16, 16), :].reshape(span, LANES)
                    for c in range(2)
                ]
                one = lax.dot_general(
                    jnp.concatenate(lhs, 0),
                    jnp.concatenate(rhs, 1),
                    NT,
                    preferred_element_type=jnp.float32,
                )
                acc = one if acc is None else acc + one
            kept = jnp.where(same, acc, 0.0).reshape(group, 16, span)
            store(
                pl.ds(p, group),
                pl.ds(q, group),
                jnp.dot(
                    jnp.sum(kept, axis=1),
                    pick,
                    preferred_element_type=jnp.float32,
                    precision=lax.Precision.HIGHEST,
                ),
            )


def readers(schip, gchip, sown, gown, score, gcore):
    pair = 2 * HALF

    def slab(q, s, a):
        if s == 0:
            return schip[pl.ds(q * pair + (2 - a) * HALF, HALF), :]
        if s == 2:
            return score[pl.ds(q * pair + (1 - a) * HALF, HALF), :]
        return sown[q, pl.ds(a * HALF, HALF), :]

    def green(s, a):
        if s == 0:
            return gchip[pl.ds((2 - a) * EDGE, EDGE), :]
        if s == 2:
            return gcore[pl.ds((1 - a) * EDGE, EDGE), :]
        return gown[pl.ds(a * EDGE, EDGE), :]

    return slab, green


def early_kernel(rows, sown, gown, part_ref, sides_ref, far_ref, half_ref, full_ref):
    slab, green = readers(None, None, sown, gown, None, None)
    none = jnp.zeros((EDGE, EDGE), jnp.bfloat16)
    for k in range(2):
        o = green(1, 2 * k)[:, EDGE:]
        far_ref[k] = jnp.concatenate(
            [jnp.concatenate([o, none], 1), jnp.concatenate([none, o], 1)], 0
        )
    for j in range(0, rows // 2, 2):
        for a in range(3):
            side = jnp.concatenate(halves(slab, (1, a), j), 0)
            sides_ref[a, :, pl.ds(j * LANES, 2 * LANES)] = side
            if a == 1:
                continue
            both = jnp.dot(
                green(1, 2 - a)[:, :EDGE], side, preferred_element_type=jnp.float32
            ).astype(jnp.bfloat16)
            for k in range(2):
                half_ref[a // 2, pl.ds((j + k) * EDGE, EDGE), :] = both[
                    :, k * LANES : (k + 1) * LANES
                ]
    for j in range(0, rows // 2, 4):
        for k in range(2):
            full = lax.dot_general(
                far_ref[k],
                half_ref[k, pl.ds(j * EDGE, 4 * EDGE), :],
                NT,
                preferred_element_type=jnp.float32,
            )
            for half in range(2):
                those = [2 * (j + n) + half for n in range(4)]
                unfold(full[half * EDGE : (half + 1) * EDGE], those, k, full_ref)

    def store(p, q, sums):
        part_ref[p, q] = sums

    inner([lambda q: slab(q, 1, 2), lambda q: slab(q, 1, 0)], full_ref, rows, store)


def main_kernel(
    scale,
    rows,
    part_ref,
    sides_ref,
    schip,
    gchip,
    sown,
    gown,
    score,
    gcore,
    out_ref,
    occ_ref,
    half_ref,
    full_ref,
):
    slab, green = readers(schip, gchip, sown, gown, score, gcore)
    none = jnp.zeros((EDGE, EDGE), jnp.bfloat16)
    near = [green(s, 2 - s)[:, :EDGE] for s in range(3)]
    mid = jnp.concatenate(near, 1)
    ends = jnp.concatenate(
        [
            jnp.concatenate([near[0], near[1], none, none], 1),
            jnp.concatenate([none, none, near[1], near[2]], 1),
        ],
        0,
    )
    used = ({0: 1, 1: 2}, {0: 0, 1: 1, 2: 2}, {1: 0, 2: 1})
    for s in range(3):
        o = [green(s, used[s][t])[:, EDGE:] if t in used[s] else none for t in range(3)]
        occ_ref[pl.ds(s * EDGE, EDGE), :] = jnp.concatenate(o + [none], 1)

    for j in range(0, rows // 2, 2):
        own = [sides_ref[a, :, pl.ds(j * LANES, 2 * LANES)] for a in range(3)]
        both = jnp.dot(
            ends,
            jnp.concatenate(halves(slab, (0, 1), j) + [own[0], own[2]] + halves(slab, (2, 1), j), 0),
            preferred_element_type=jnp.float32,
        ).astype(jnp.bfloat16)
        middle = jnp.dot(
            mid,
            jnp.concatenate(halves(slab, (0, 2), j) + [own[1]] + halves(slab, (2, 0), j), 0),
            preferred_element_type=jnp.float32,
        ).astype(jnp.bfloat16)
        pieces = (both[:EDGE], middle, both[EDGE:])
        for k in range(4):
            half_ref[pl.ds((2 * j + k) * EDGE, EDGE), :] = jnp.concatenate(
                [piece[:, k * EDGE : (k + 1) * EDGE] for piece in pieces] + [none], 1
            )

    for q in range(0, rows, 4):
        full = lax.dot_general(
            occ_ref[...],
            half_ref[pl.ds(q * EDGE, 4 * EDGE), :],
            NT,
            preferred_element_type=jnp.float32,
        )
        for s in range(3):
            unfold(full[s * EDGE : (s + 1) * EDGE], (q, q + 1, q + 2, q + 3), s, full_ref)

    def store(p, q, sums):
        out_ref[p, q] = scale * (sums + part_ref[p, q])

    inner([lambda q, s=s: slab(q, s, 2 - s) for s in range(3)], full_ref, rows, store)


def body(integrals, occupied, virtual, imask, omask, vmask, count):
    total = integrals.shape[1]
    members = lax.axis_size("blk")
    order = block_order(members)
    works_on = [order.index(d) for d in range(members)]

    rows = pl.pallas_call(
        functools.partial(pack_kernel, works_on),
        out_shape=jax.ShapeDtypeStruct((members, 3 * HALF, LANES), jnp.bfloat16),
        in_specs=[pl.BlockSpec(memory_space=pl.ANY)] * 2,
        out_specs=pl.BlockSpec(memory_space=pl.ANY),
        scratch_shapes=[
            pltpu.VMEM((3, total, EDGE * EDGE), jnp.bfloat16),
            pltpu.VMEM((3, total), jnp.int32),
            pltpu.VMEM((3, total * PITCH, LANES), jnp.float32),
            pltpu.VMEM((members, 3 * HALF, LANES), jnp.bfloat16),
            pltpu.SemaphoreType.DMA((13,)),
        ],
        compiler_params=pltpu.CompilerParams(vmem_limit_bytes=63 * 1024 * 1024),
        name="pack",
    )(jnp.transpose(integrals[0], (1, 0, 2)), imask.T)
    greens, gchip = pl.pallas_call(
        functools.partial(prep_kernel, total),
        out_shape=(
            jax.ShapeDtypeStruct((6 * HALF, LANES), jnp.bfloat16),
            jax.ShapeDtypeStruct((4 * HALF, LANES), jnp.bfloat16),
        ),
        in_specs=[SMEM] * 3 + [VMEM] * 2,
        out_specs=(VMEM, VMEM),
        scratch_shapes=[pltpu.VMEM((2, 3 * PITCH, LANES), jnp.float32)],
        name="prep",
    )(omask.T, vmask.T, count, occupied[0], virtual[0])
    chip_next = [order[(j - 1 + 2 * (j % 2)) % members] for j in range(members)]
    gchip = lax.ppermute(gchip, "blk", list(enumerate(chip_next)))
    greens = lax.ppermute(greens, "blk", list(enumerate(order)))
    own = lax.all_to_all(rows, "blk", split_axis=0, concat_axis=0, tiled=True)
    own, greens, gchip = lax.optimization_barrier((own, greens, gchip))
    core_pairs = [(order[j], order[j + 1 - 2 * (j % 2)]) for j in range(members)]
    chip_pairs = list(zip(order, chip_next))
    to_chip = own[:, : 2 * HALF].reshape(-1, LANES)
    to_core = own[:, HALF:].reshape(-1, LANES)
    schip = lax.ppermute(to_chip, "blk", chip_pairs)
    score = lax.ppermute(to_core, "blk", core_pairs)
    gcore = lax.ppermute(greens[EDGE:], "blk", core_pairs)
    early, sides = pl.pallas_call(
        functools.partial(early_kernel, members),
        out_shape=(
            jax.ShapeDtypeStruct((members, members), jnp.float32),
            jax.ShapeDtypeStruct((3, EDGE, members // 2 * LANES), jnp.bfloat16),
        ),
        in_specs=[VMEM] * 2,
        out_specs=(VMEM, VMEM),
        scratch_shapes=[
            pltpu.VMEM((2, 2 * EDGE, LANES), jnp.bfloat16),
            pltpu.VMEM((2, members // 2 * EDGE, LANES), jnp.bfloat16),
            pltpu.VMEM((members, 2 * HALF, LANES), jnp.bfloat16),
        ],
        compiler_params=pltpu.CompilerParams(vmem_limit_bytes=24 * 1024 * 1024),
        name="early",
    )(own, greens)
    part = pl.pallas_call(
        functools.partial(main_kernel, 1.0 / math.sqrt(5 * EDGE * EDGE * total), members),
        out_shape=jax.ShapeDtypeStruct((members, members), jnp.float32),
        in_specs=[VMEM] * 8,
        out_specs=VMEM,
        scratch_shapes=[
            pltpu.VMEM((3 * EDGE, 2 * LANES), jnp.bfloat16),
            pltpu.VMEM((members * EDGE, 2 * LANES), jnp.bfloat16),
            pltpu.VMEM((members, 3 * HALF, LANES), jnp.bfloat16),
        ],
        compiler_params=pltpu.CompilerParams(vmem_limit_bytes=24 * 1024 * 1024),
        name="products",
    )(early, sides, schip, gchip, own, greens, score, gcore)
    mine = lax.all_to_all(part, "blk", split_axis=0, concat_axis=0, tiled=True)
    return jnp.sum(mine, axis=0, keepdims=True)


def solution(mesh):
    return jax.shard_map(
        body,
        mesh=mesh,
        in_specs=(
            P(("grp", "blk"), None, None, None),
            P(("grp", "blk"), None, None),
            P(("grp", "blk"), None, None),
            P(),
            P(),
            P(),
            P(),
        ),
        out_specs=P(("grp", "blk"), None),
        check_vma=False,
    )
```
